32 devices in a mesh: section: 2 (over x), row: 4 (over z), col: 4 (over y, core).
Axes of the slice: x: 2, y: 2, z: 4, core: 2. Of those that a mesh axis runs over, the one named last changes fastest.
Arguments:
- tokens_in: bfloat16 [2, 1024, 4096], P(None, 'row', 'col'), may hold values from -6 to 6
- doc_ids: int32 [2, 4, 1024], P(None, 'col'), may hold values from 0 to 7, never falling along the last dimension, each value on 1 to 512 neighbouring positions
- cotangent: bfloat16 [2, 1024, 4096], P(None, 'row', 'col'), may hold values from -6 to 6
- qkv_master: float32 [2, 3, 1024, 1024], P('section', None, 'row', 'col'), may hold values from -0.25 to 0.25
- out_master: float32 [2, 1024, 1024], P('section', 'row', 'col'), may hold values from -0.5 to 0.5
- unit_master: float32 [2, 1024, 4096], P('section', 'row', 'col'), may hold values from -0.1875 to 0.1875
- down_master: float32 [2, 1024, 4096], P('section', 'row', 'col'), may hold values from -0.09375 to 0.09375
- unit_bias: float32 [2, 4096], P('section', 'col'), may hold values from -3 to 3
- width_bias: float32 [2, 6, 1024], P('section', None, 'row'), may hold values from -2 to 2
- norm_gain: float32 [2, 2, 1024], P('section', None, 'row'), may hold values from 0.25 to 1.75
Outputs:
- layer_out: float32 [2, 2, 1024, 4096], P('section', None, 'row', 'col')
- input_grad: float32 [2, 2, 1024, 4096], P('section', None, 'row', 'col')
- grad_qkv: float32 [2, 3, 1024, 1024], P('section', None, 'row', 'col')
- grad_out: float32 [2, 1024, 1024], P('section', 'row', 'col')
- grad_unit: float32 [2, 1024, 4096], P('section', 'row', 'col')
- grad_down: float32 [2, 1024, 4096], P('section', 'row', 'col')
- grad_unit_bias: float32 [2, 4096], P('section', 'col')
- grad_width_bias: float32 [2, 6, 1024], P('section', None, 'row')
- grad_gain: float32 [2, 2, 1024], P('section', None, 'row')
The draws below stay inside these ranges and needn't reach their ends.
Inputs may be any that keep to these rules, and one draw needn't show every extreme that they name: `doc_ids`: within each sequence the document numbers never fall, each of the 8 documents has 1 to 512 tokens, and one has exactly 512.
All inputs are finite; a program needn't handle non-finite values.
Results may differ from the reference program's by a relative error of at most 0.04.
Values may be sent and summed in bfloat16 or wider, within the bound.
A program may use at most 192 MiB of HBM per device.

```python
import math
import jax
import jax.numpy as jnp
import numpy as np
from jax import lax

H = 16
HD = 64
D = 1024
FF = 4096
LEN = 1024
MICRO = 2
DOCS = 8
DOC_MOST = 512
SEQS = 4
TMB = 4096
N_SECTION = 2


def level_of(rng, shape, cuts, least, largest):
    factor_of, own = 1.0, jax.random.fold_in(rng, 6)
    for position, shards_of in cuts:
        draws = jnp.exp(jax.random.uniform(jax.random.fold_in(own, position), (shards_of,), jnp.float32, least / len(cuts), largest / len(cuts)))
        factor_of = factor_of * jnp.repeat(draws, shape[position] // shards_of).reshape([-1 if axis == position else 1 for axis in range(len(shape))])
    return factor_of


def split_up(amount, total, reach, skew):
    portions = [(1 << 20) // math.isqrt(grade ** skew) + 1 for grade in range(2, amount + 1)]
    rest, given = total - reach - (amount - 1), [1] * (amount - 1)
    while rest > 0:
        free = [i for i in range(amount - 1) if given[i] < reach]
        whole, budget = sum([portions[i] for i in free]), rest
        for i in free:
            more = min(reach - given[i], max(1, budget * portions[i] // whole), rest)
            given[i] = given[i] + more
            rest = rest - more
    return np.array([reach] + given)


def ragged(own_key, count, total, most, slope):
    if count == 2:
        one = jax.random.randint(own_key, (), max(1, total - most), min(most, total - 1) + 1)
        return jnp.stack([one, total - one])
    sizes = jnp.asarray(split_up(count, total, most, slope), jnp.int32)
    pairs = (count - 1) // 2
    donor, receiver = sizes[1:1 + 2 * pairs:2], sizes[2:2 + 2 * pairs:2]
    room = jnp.minimum(donor - 1, most - receiver)
    moved = jax.random.randint(jax.random.fold_in(own_key, 1), (pairs,), 0, 1 << 20) % (room + 1)
    sizes = sizes.at[1:1 + 2 * pairs:2].set(donor - moved).at[2:2 + 2 * pairs:2].set(receiver + moved)
    return sizes[jax.random.permutation(jax.random.fold_in(own_key, 2), count)]


def noise(own_key, extent, scale, reach, shards=(), held_as=jnp.bfloat16):
    drawn = jax.random.normal(own_key, extent, jnp.float32) * scale
    if len(shards) > 0:
        drawn = level_of(own_key, extent, shards, -0.22, 0.18) * drawn
    return jnp.clip(drawn, min=-reach, max=reach).astype(held_as)


def setup_inputs(seed: int = 0) -> dict:
    key_list = jax.random.split(jax.random.key(seed), 11)
    tokens_in = noise(key_list[0], (MICRO, D, TMB), 1.0, 6.0, ((1, 4), (2, 4)))
    doc_ids = jax.vmap(lambda own: jnp.searchsorted(jnp.cumsum(ragged(own, DOCS, LEN, DOC_MOST, 2)), jnp.arange(LEN), side="right"))(jax.random.split(key_list[1], MICRO * SEQS)).reshape((MICRO, SEQS, LEN)).astype(jnp.int32)
    cotangent = noise(key_list[2], (MICRO, D, TMB), 1.0, 6.0, ((1, 4), (2, 4)))
    qkv_master = noise(key_list[3], (N_SECTION, 3, D, D), (D // 2) ** -0.5, 0.25, ((0, 2), (2, 4), (3, 4)), jnp.float32)
    out_master = noise(key_list[4], (N_SECTION, D, D), (D // 8) ** -0.5, 0.5, ((0, 2), (1, 4), (2, 4)), jnp.float32)
    unit_master = noise(key_list[5], (N_SECTION, D, FF), D ** -0.5, 0.1875, ((0, 2), (1, 4), (2, 4)), jnp.float32)
    down_master = noise(key_list[6], (N_SECTION, D, FF), FF ** -0.5, 0.09375, ((0, 2), (1, 4), (2, 4)), jnp.float32)
    unit_bias = noise(key_list[7], (N_SECTION, FF), 0.5, 3.0, ((0, 2), (1, 4)), jnp.float32)
    width_bias = noise(key_list[8], (N_SECTION, 6, D), 0.3, 2.0, ((0, 2), (2, 4)), jnp.float32)
    norm_gain = jnp.clip(1.0 + 0.15 * jax.random.normal(key_list[9], (N_SECTION, 2, D), jnp.float32), 0.25, 1.75)
    return dict(tokens_in=tokens_in, doc_ids=doc_ids, cotangent=cotangent, qkv_master=qkv_master, out_master=out_master, unit_master=unit_master, down_master=down_master, unit_bias=unit_bias, width_bias=width_bias, norm_gain=norm_gain)


EPSILON = 1e-05
NEG_BIG = -1e+30
PRECISION_HIGH = lax.Precision.HIGHEST

@jax.custom_vjp
def lowered_input(v):
    return lax.optimization_barrier(v.astype(jnp.bfloat16)).astype(jnp.float32)

@jax.custom_vjp
def lowered_gradient(v):
    return v

def low_keep(v):
    return (lowered_input(v), None)

def low_pass(kept, grad):
    return (grad,)

def back_keep(v):
    return (v, None)

def back_low(kept, grad):
    return (lowered_input(grad),)
lowered_input.defvjp(low_keep, low_pass)
lowered_gradient.defvjp(back_keep, back_low)

def both_round(values):
    return lowered_input(lowered_gradient(values))

def norm_rows(hidden, gain_row, bias_row):
    center = hidden - lax.optimization_barrier(jnp.mean(hidden, axis=-1, keepdims=True))
    spread = lax.optimization_barrier(jnp.mean(jnp.square(center), axis=-1, keepdims=True))
    return center * lax.rsqrt(spread + EPSILON) * gain_row + bias_row

def attend_sequence(seq_items):
    query_matrix, key_matrix, value_matrix, doc_row = seq_items
    logit_scores = lowered_gradient(jnp.einsum('xgj,igj->gxi', query_matrix, key_matrix, precision=PRECISION_HIGH))
    same_doc = doc_row[:, None] == doc_row[None, :]
    logit_scores = jnp.where(same_doc[None], logit_scores, NEG_BIG)
    shifted = logit_scores - lax.optimization_barrier(jnp.max(logit_scores, axis=2, keepdims=True))
    weight_set = jnp.exp(shifted)
    weight_set = weight_set / lax.optimization_barrier(jnp.sum(weight_set, axis=2, keepdims=True))
    return jnp.einsum('bgy,ybt->gbt', lowered_input(weight_set), value_matrix, precision=PRECISION_HIGH)

def micro_layer(inputs, doc_rows, params):
    qkv_low, out_low, unit_low, down_low, unit_shift, width_shift, gain_rows = params
    seq_count = doc_rows.shape[0]
    head_scale = HD ** (-0.5)
    head_shape = (seq_count, LEN, H, HD)
    projected = jnp.einsum('td,ked->kte', inputs, qkv_low, precision=PRECISION_HIGH)
    query_matrix = both_round((projected[0] + width_shift[0]) * head_scale).reshape(head_shape)
    key_matrix = both_round(projected[1]).reshape(head_shape)
    value_matrix = both_round(projected[2] + width_shift[1]).reshape(head_shape)
    attended_rows = lax.map(jax.checkpoint(attend_sequence), (query_matrix, key_matrix, value_matrix, doc_rows))
    attended_rows = both_round(attended_rows.reshape(inputs.shape))
    attn_out = lowered_gradient(jnp.dot(attended_rows, out_low, precision=PRECISION_HIGH) + width_shift[2])
    normed_one = norm_rows(inputs + attn_out, gain_rows[0], width_shift[3])
    unit_pre = lowered_gradient(jnp.dot(lowered_input(normed_one), unit_low, precision=PRECISION_HIGH) + unit_shift)
    unit_act = lowered_input(jax.nn.gelu(unit_pre, approximate=False))
    down_out = lowered_gradient(jnp.einsum('tf,df->td', unit_act, down_low, precision=PRECISION_HIGH) + width_shift[4])
    return norm_rows(normed_one + down_out, gain_rows[1], width_shift[5])

def run_layer(inputs, doc_ids, params):
    qkv_w, out_w, unit_w, down_w, unit_shift, width_shift, gain_rows = params
    lowered = (lowered_input(qkv_w), lowered_input(out_w), lowered_input(unit_w), lowered_input(down_w), unit_shift, width_shift, gain_rows)
    one_micro = jax.checkpoint(micro_layer)

    def micro_step(carry, micro_items):
        return (carry, one_micro(micro_items[0], micro_items[1], lowered))
    unused, outputs = lax.scan(micro_step, jnp.zeros((), jnp.float32), (inputs, doc_ids))
    return outputs

def reference(tokens_in, doc_ids, cotangent, qkv_master, out_master, unit_master, down_master, unit_bias, width_bias, norm_gain):
    masters = tuple((master_item.astype(jnp.float32) for master_item in (qkv_master, out_master, unit_master, down_master, unit_bias, width_bias, norm_gain)))

    def forward(first_in, probe_in, params):
        layer_one = tuple((master_item[0] for master_item in params))
        layer_two = tuple((master_item[1] for master_item in params))
        out_one = run_layer(first_in, doc_ids, layer_one)
        out_two = run_layer(both_round(out_one) + probe_in, doc_ids, layer_two)
        return (out_one, out_two)
    start_in = jnp.swapaxes(tokens_in.astype(jnp.float32), 1, 2)
    probe_in = jnp.zeros_like(start_in)
    outs_pair, pullback = jax.vjp(forward, start_in, probe_in, masters)
    grad_first, grad_probe, grad_masters = pullback((jnp.zeros_like(outs_pair[0]), jnp.swapaxes(cotangent.astype(jnp.float32), 1, 2)))
    layer_out = jnp.swapaxes(jnp.stack([outs_pair[0], outs_pair[1]]), 2, 3)
    input_grad = jnp.swapaxes(jnp.stack([grad_first, grad_probe]), 2, 3)
    return (layer_out, input_grad, grad_masters[0], grad_masters[1], grad_masters[2], grad_masters[3], grad_masters[4], grad_masters[5], grad_masters[6])
```

```python
import jax
import jax.numpy as jnp
from jax import lax
from jax.sharding import Mesh
from jax.sharding import PartitionSpec as P

HD = 64
EPSILON = 1e-05
NEG_BIG = -1e30
CORES = 2
PLANE = ("row", "high", "core")
F32 = jnp.float32
BF16 = jnp.bfloat16


def gelu_exact(values):
    return jax.nn.gelu(values, approximate=False)


def dot(pattern, left, right):
    return jnp.einsum(pattern, left, right, preferred_element_type=F32)


class Layout:
    def __init__(self, tokens_in, doc_ids):
        self.micro, self.narrow, _ = tokens_in.shape
        self.seq_here, self.seq_len = doc_ids.shape[1:]
        self.rows = lax.axis_size("row")
        self.highs = lax.axis_size("high")
        self.cols = self.highs * CORES
        self.width = self.narrow * self.rows
        self.places = self.rows * CORES
        self.sequences = self.micro * self.seq_here * CORES
        self.group = self.places // self.sequences
        self.part = self.seq_len // self.group
        place = lax.axis_index("row") * CORES + lax.axis_index("core")
        self.row = lax.axis_index("row")
        self.sequence = place // self.group
        self.position = place % self.group
        self.block = (self.sequence // CORES) * self.group + self.position

    def routes(self, shift):
        pairs = []
        for source in range(self.places):
            row, core = divmod(source, CORES)
            block = (row + shift) % self.rows
            sequence = (block // self.group) * CORES + core
            pairs.append((source, sequence * self.group + block % self.group))
        return pairs

    def to_tokens(self, array):
        blocks = array.reshape(self.micro, self.narrow, self.seq_here * self.group, self.part)
        blocks = blocks.transpose(0, 2, 1, 3).reshape(self.rows, self.narrow, self.part)
        got = []
        for shift in range(self.rows):
            block = lax.dynamic_index_in_dim(blocks, (self.row + shift) % self.rows, 0, False)
            got.append(lax.ppermute(block, ("row", "core"), self.routes(shift)))
        order = (self.block - jnp.arange(self.rows)) % self.rows
        whole = jnp.take(jnp.stack(got), order, axis=0)
        return whole.reshape(self.width, self.part).T

    def to_features(self, array):
        blocks = array.T.reshape(self.rows, self.narrow, self.part)
        got = []
        for shift in range(self.rows):
            block = lax.dynamic_index_in_dim(blocks, (self.block - shift) % self.rows, 0, False)
            pairs = [(there, here) for here, there in self.routes(shift)]
            got.append(lax.ppermute(block, ("row", "core"), pairs))
        order = (jnp.arange(self.rows) - self.row) % self.rows
        whole = jnp.take(jnp.stack(got), order, axis=0)
        whole = whole.reshape(self.micro, self.seq_here * self.group, self.narrow, self.part)
        return whole.transpose(0, 2, 1, 3).reshape(self.micro, self.narrow, self.seq_here * self.seq_len)

    def within(self, step):
        return [
            (place, place // self.group * self.group + (place + step) % self.group)
            for place in range(self.places)
        ]

    def share(self, array):
        return [array] + [
            lax.ppermute(array, ("row", "core"), self.within(step)) for step in range(1, self.group)
        ]

    def give_back(self, blocks):
        total = blocks[0].astype(F32)
        for step in range(1, self.group):
            total += lax.ppermute(
                blocks[step].astype(BF16), ("row", "core"), self.within(self.group - step)
            ).astype(F32)
        return total

    def documents(self, doc_ids):
        other = lax.ppermute(doc_ids, "core", [(i, (i + 1) % CORES) for i in range(CORES)])
        here = lax.axis_index("core")
        pair = jnp.stack([jnp.where(here == c, doc_ids, other) for c in range(CORES)], axis=2)
        rows = pair.reshape(self.sequences, self.group, self.part)
        mine = lax.dynamic_index_in_dim(rows, self.sequence, 0, False)
        order = (self.position - jnp.arange(self.group)) % self.group
        ordered = jnp.take(mine, order, axis=0)
        return ordered[0], ordered.reshape(-1)


def attend(query, key, value, doc_query, doc_key):
    same = (doc_query[:, None] == doc_key[None, :])[None]
    scores = jnp.where(same, dot("qhj,khj->hqk", query, key), NEG_BIG)
    row_max = jnp.max(scores, axis=2, keepdims=True)
    expo = jnp.exp(scores - row_max)
    row_total = jnp.sum(expo, axis=2, keepdims=True)
    prob = (expo / row_total).astype(BF16)
    return dot("hqk,khj->qhj", prob, value), row_max + jnp.log(row_total)


def attend_back(query, key, value, grad_mixed, log_total, doc_query, doc_key):
    same = (doc_query[:, None] == doc_key[None, :])[None]
    scores = jnp.where(same, dot("qhj,khj->hqk", query, key), NEG_BIG)
    prob = jnp.where(same, jnp.exp(scores - log_total), 0.0)
    grad_value = dot("hqk,qhj->khj", prob.astype(BF16), grad_mixed)
    grad_prob = dot("qhj,khj->hqk", grad_mixed, value)
    inner = jnp.sum(prob * grad_prob, axis=2, keepdims=True)
    grad_scores = (prob * (grad_prob - inner)).astype(BF16)
    grad_query = dot("hqk,khj->qhj", grad_scores, key)
    grad_key = dot("hqk,qhj->khj", grad_scores, query)
    return grad_query, grad_key, grad_value


def norm_forward(hidden, gain, bias):
    center = hidden - jnp.mean(hidden, axis=1, keepdims=True)
    scale = lax.rsqrt(jnp.mean(center * center, axis=1, keepdims=True) + EPSILON)
    normed = center * scale
    return normed * gain + bias, normed, scale


def norm_backward(grad_out, normed, scale, gain):
    scaled = grad_out * gain
    first = jnp.mean(scaled, axis=1, keepdims=True)
    second = jnp.mean(scaled * normed, axis=1, keepdims=True)
    return scale * (scaled - first - normed * second)


def local(tokens_in, doc_ids, cotangent, qkv_master, out_master, unit_master, down_master, unit_bias, width_bias, norm_gain):
    at = Layout(tokens_in, doc_ids)
    section = lax.axis_index("section")
    rows, cols, width = at.rows, at.cols, at.width
    units = unit_master.shape[2] * cols
    heads = width // HD
    head_scale = HD**-0.5

    def gathered(weight):
        whole = lax.all_gather(weight.astype(BF16), PLANE, axis=0)
        return whole.reshape((rows, cols) + weight.shape)

    def square(weight):
        whole = gathered(weight)
        return whole.transpose(0, 2, 1, 3).reshape(width, -1)

    qkv_bf = gathered(qkv_master[0]).transpose(2, 0, 3, 1, 4).reshape(3, width, width)
    out_bf = square(out_master[0])
    unit_bf = square(unit_master[0])
    down_bf = square(down_master[0])
    unit_shift = lax.all_gather(unit_bias[0], ("high", "core"), axis=0, tiled=True)
    small = lax.all_gather(jnp.concatenate([width_bias[0], norm_gain[0]]), "row", axis=1, tiled=True)
    bias, gain = small[:6], small[6:]

    first_in = at.to_tokens(tokens_in)
    last_grad = at.to_tokens(cotangent)
    doc_query, doc_key = at.documents(doc_ids)

    def by_head(array):
        return array.reshape(array.shape[0], heads, HD)

    def forward(layer_in):
        projected = dot("td,ked->kte", layer_in, qkv_bf)
        query = ((projected[0] + bias[0]) * head_scale).astype(BF16)
        key = jnp.concatenate(at.share(projected[1].astype(BF16)))
        value = jnp.concatenate(at.share((projected[2] + bias[1]).astype(BF16)))
        mixed, log_total = attend(by_head(query), by_head(key), by_head(value), doc_query, doc_key)
        mixed = mixed.reshape(-1, width).astype(BF16)
        attn = dot("th,hd->td", mixed, out_bf) + bias[2]
        x1, hat_one, scale_one = norm_forward(layer_in.astype(F32) + attn, gain[0], bias[3])
        x1_bf = x1.astype(BF16)
        pre = dot("td,df->tf", x1_bf, unit_bf) + unit_shift
        act = gelu_exact(pre).astype(BF16)
        down = dot("tf,df->td", act, down_bf) + bias[4]
        y, hat_two, scale_two = norm_forward(x1 + down, gain[1], bias[5])
        saved = (layer_in, query, key, value, mixed, log_total, x1_bf, hat_one, scale_one, pre, hat_two, scale_two)
        return y, saved

    def backward(dy, saved, weights_too):
        layer_in, query, key, value, mixed, log_total, x1_bf, hat_one, scale_one, pre, hat_two, scale_two = saved
        dh2 = norm_backward(dy, hat_two, scale_two, gain[1])
        ddown = dh2.astype(BF16)
        act, pull = jax.vjp(gelu_exact, pre)
        dact = dot("td,df->tf", ddown, down_bf)
        dpre = pull(dact)[0].astype(BF16)
        dx1 = dh2 + dot("tf,df->td", dpre, unit_bf)
        dh1 = norm_backward(dx1, hat_one, scale_one, gain[0])
        dattn = dh1.astype(BF16)
        dmixed = dot("td,hd->th", dattn, out_bf).astype(BF16)
        dquery, dkey, dvalue = attend_back(
            by_head(query), by_head(key), by_head(value), by_head(dmixed), log_total, doc_query, doc_key
        )
        dquery = dquery.reshape(-1, width).astype(BF16) * head_scale
        dkey = at.give_back(jnp.split(dkey.reshape(-1, width), at.group)).astype(BF16)
        dvalue = at.give_back(jnp.split(dvalue.reshape(-1, width), at.group)).astype(BF16)
        dproj = jnp.stack([dquery, dkey, dvalue])
        dx = dh1 + dot("kte,ked->td", dproj, qkv_bf)
        if not weights_too:
            return dx, None
        sums = jnp.stack(
            [
                jnp.sum(dquery.astype(F32), axis=0),
                jnp.sum(dvalue.astype(F32), axis=0),
                jnp.sum(dattn.astype(F32), axis=0),
                jnp.sum(dx1, axis=0),
                jnp.sum(ddown.astype(F32), axis=0),
                jnp.sum(dy, axis=0),
                jnp.sum(dx1 * hat_one, axis=0),
                jnp.sum(dy * hat_two, axis=0),
            ]
        )
        grads = (
            dot("kte,td->ked", dproj, layer_in),
            dot("th,td->hd", mixed, dattn),
            dot("td,tf->df", x1_bf, dpre),
            dot("td,tf->df", ddown, act.astype(BF16)),
            jnp.sum(dpre.astype(F32), axis=0),
            sums,
        )
        return dx, grads

    def scattered(grad):
        blocks = grad.astype(BF16).reshape(rows, grad.shape[0] // rows, cols, grad.shape[1] // cols)
        blocks = blocks.transpose(0, 2, 1, 3).reshape(rows * cols, grad.shape[0] // rows, grad.shape[1] // cols)
        return lax.psum_scatter(blocks, PLANE, scatter_dimension=0, tiled=True)[0].astype(F32)

    early, _ = forward(first_in)
    passed = lax.ppermute(early.astype(BF16), "section", [(0, 1)])
    layer_out, saved = forward(jnp.where(section == 0, first_in, passed))
    early_grad, _ = backward(last_grad.astype(F32), saved, False)
    passed = lax.ppermute(early_grad.astype(BF16), "section", [(1, 0)])
    dy = jnp.where(section == 0, passed, last_grad).astype(F32)
    input_grad, (qkv_grad, out_grad, unit_grad, down_grad, pre_sum, sums) = backward(dy, saved, True)

    qkv_blocks = qkv_grad.astype(BF16).reshape(3, rows, width // rows, cols, width // cols)
    qkv_blocks = qkv_blocks.transpose(1, 3, 0, 2, 4).reshape((rows * cols, 3, width // rows, width // cols))
    qkv_sum = lax.psum_scatter(qkv_blocks, PLANE, scatter_dimension=0, tiled=True)[0].astype(F32)
    out_sum, unit_sum, down_sum = scattered(out_grad), scattered(unit_grad), scattered(down_grad)
    pre_sum, sums = lax.psum((pre_sum, sums), PLANE)
    here = lax.axis_index("high") * CORES + lax.axis_index("core")
    pre_sum = lax.dynamic_slice_in_dim(pre_sum, here * (units // cols), units // cols)
    sums = lax.dynamic_slice_in_dim(sums, at.row * at.narrow, at.narrow, axis=1)
    layer_out = at.to_features(layer_out.astype(BF16)).astype(F32)
    input_grad = at.to_features(input_grad.astype(BF16)).astype(F32)
    return (
        layer_out[None],
        input_grad[None],
        qkv_sum[None],
        out_sum[None],
        unit_sum[None],
        down_sum[None],
        pre_sum[None],
        sums[:6][None],
        sums[6:][None],
    )


def solution(mesh):
    sections, rows, cols = (mesh.shape[name] for name in ("section", "row", "col"))
    fine = Mesh(
        mesh.devices.reshape(sections, rows, cols // CORES, CORES), ("section", "row", "high", "core")
    )
    col = ("high", "core")
    block = P("section", "row", col)
    stream = P("section", None, "row", col)
    return jax.shard_map(
        local,
        mesh=fine,
        in_specs=(
            P(None, "row", col),
            P(None, col, None),
            P(None, "row", col),
            P("section", None, "row", col),
            block,
            block,
            block,
            P("section", col),
            P("section", None, "row"),
            P("section", None, "row"),
        ),
        out_specs=(
            stream,
            stream,
            stream,
            block,
            block,
            block,
            P("section", col),
            P("section", None, "row"),
            P("section", None, "row"),
        ),
        check_vma=False,
    )
```

```python
import functools

import jax
import jax.numpy as jnp
from jax import lax
from jax.experimental import pallas as pl
from jax.experimental.pallas import tpu as pltpu
from jax.sharding import Mesh
from jax.sharding import PartitionSpec as P

HD = 64
EPSILON = 1e-05
NEG_BIG = -1e30
CORES = 2
PAIR = 128
PLANE = ("row", "high", "core")
MESH = pl.DeviceIdType.MESH
F32 = jnp.float32
BF16 = jnp.bfloat16
VMEM_BYTES = 56 * 1024 * 1024
LOW_VMEM = 63 * 1024 * 1024


def nn(left, right):
    return lax.dot_general(left, right, (((1,), (0,)), ((), ())), preferred_element_type=F32)


def nt(left, right):
    return lax.dot_general(left, right, (((1,), (1,)), ((), ())), preferred_element_type=F32)


def held(shape):
    return pl.BlockSpec(shape, lambda *_: (0,) * len(shape), pipeline_mode=pl.Buffered(1))


def call(kernel, grid, in_specs, out_specs, out_shape, scratch, name, flops, moved, args):
    return pl.pallas_call(
        kernel,
        grid=grid,
        in_specs=in_specs,
        out_specs=out_specs,
        out_shape=out_shape,
        scratch_shapes=scratch,
        name=name,
        compiler_params=pltpu.CompilerParams(
            vmem_limit_bytes=VMEM_BYTES, dimension_semantics=("arbitrary",) * len(grid)
        ),
        cost_estimate=pl.CostEstimate(flops=flops, bytes_accessed=moved, transcendentals=0),
    )(*args)


def shaped(shape, dtype):
    return jax.ShapeDtypeStruct(shape, dtype)


def row_blocks(rows, narrow):
    take = min(rows, max(1, 256 // narrow))
    while rows % take:
        take += 1
    return take


def side_by_side(blocks):
    take, cols, narrow, deep = blocks.shape
    return jnp.concatenate([blocks[:, k].reshape(take * narrow, deep) for k in range(cols)], axis=1)


def project_kernel(x_ref, w_ref, b_ref, o_ref, *, scale):
    out = nt(x_ref[...], side_by_side(w_ref[...])) + b_ref[0]
    o_ref[0] = (out * scale).astype(BF16)


QKV, OUT, UNIT = 0, 3, 4
FEED_BLOCKS = 2


def project(x, weight, bias, first, count, scale):
    tokens, width = x.shape
    rows, cols, _, deep = weight.shape
    narrow = width // rows
    take = row_blocks(rows, narrow)
    return call(
        functools.partial(project_kernel, scale=scale),
        (count, rows // take),
        [
            held((tokens, width)),
            pl.BlockSpec((take, cols, narrow, deep), lambda k, r: (r, 0, QKV + k + first, 0)),
            pl.BlockSpec((1, 1, take * narrow), lambda k, r: (k, 0, r)),
        ],
        pl.BlockSpec((1, tokens, take * narrow), lambda k, r: (k, 0, r)),
        shaped((count, tokens, width), BF16),
        [],
        "project",
        2 * count * tokens * width * width,
        2 * count * width * width,
        (x, weight, bias),
    )


def head_lanes(shape, axis):
    return lax.broadcasted_iota(jnp.int32, shape, axis) < HD


def pair_front(query, keys, values, bias_ref):
    values_t = values.T
    lanes = head_lanes(query.shape, 1)
    outs, log_rows = [], []
    for h in range(2):
        mine = jnp.where(lanes if h == 0 else ~lanes, query, 0)
        scores = nt(keys, mine) + bias_ref[...]
        top = jnp.max(scores, axis=0, keepdims=True)
        expo = jnp.exp(scores - top)
        total = jnp.sum(expo, axis=0, keepdims=True)
        outs.append(nn(values_t, expo.astype(BF16)) / total)
        log_rows.append(top + jnp.log(total))
    mixed_t = jnp.where(head_lanes(outs[0].shape, 0), outs[0], outs[1])
    return mixed_t.T.astype(BF16), log_rows


def attend_kernel(*refs, group):
    q_ref, kv_refs = refs[0], refs[1 : 1 + group]
    dq_ref, dk_ref, o_ref, l_ref, bias_ref = refs[1 + group :]

    @pl.when(pl.program_id(0) == 0)
    def _():
        bias_ref[...] = jnp.where(dk_ref[...] == dq_ref[...], 0.0, NEG_BIG)

    keys = jnp.concatenate([ref[0] for ref in kv_refs], axis=0)
    values = jnp.concatenate([ref[1] for ref in kv_refs], axis=0)
    o_ref[...], log_rows = pair_front(q_ref[0], keys, values, bias_ref)
    for h in range(2):
        l_ref[0, h : h + 1, :] = log_rows[h]


def attend(query, shared, doc_query, doc_key):
    _, tokens, width = query.shape
    group = len(shared)
    keys = group * tokens
    pairs = width // PAIR
    kv_spec = pl.BlockSpec((2, tokens, PAIR), lambda p: (0, 0, p))
    return call(
        functools.partial(attend_kernel, group=group),
        (pairs,),
        [pl.BlockSpec((1, tokens, PAIR), lambda p: (0, 0, p))]
        + [kv_spec] * group
        + [held((1, tokens)), held((keys, 1))],
        [
            pl.BlockSpec((tokens, PAIR), lambda p: (0, p)),
            pl.BlockSpec((1, 2, tokens), lambda p: (p, 0, 0)),
        ],
        [shaped((tokens, width), BF16), shaped((pairs, 2, tokens), F32)],
        [pltpu.VMEM((keys, tokens), F32)],
        "attend",
        16 * tokens * keys * width,
        10 * tokens * width,
        (query, *shared, doc_query, doc_key),
    )


def pair_back(query, grad, mixed, log_rows, keys, values, bias_ref, tile):
    tokens = query.shape[0]
    keys_t = keys.T
    lanes = head_lanes((tile, PAIR), 1)
    low_t = head_lanes(keys_t.shape, 0)
    products = (grad.astype(F32) * mixed.astype(F32)).T
    grad_query = []
    grad_key = jnp.zeros(keys.shape, F32)
    grad_value = jnp.zeros(keys.shape, F32)
    for at in range(0, tokens, tile):
        some = slice(at, at + tile)
        grad_some = jnp.zeros((PAIR, tile), F32)
        for h in range(2):
            here = lanes if h == 0 else ~lanes
            mine = jnp.where(here, query[some], 0)
            grad_mine = jnp.where(here, grad[some], 0)
            inner = jnp.sum(products[h * HD : (h + 1) * HD, some], axis=0, keepdims=True)
            prob = jnp.exp(nt(keys, mine) + bias_ref[:, some] - log_rows[h][:, some])
            grad_value += nn(prob.astype(BF16), grad_mine)
            grad_scores = (prob * (nt(values, grad_mine) - inner)).astype(BF16)
            grad_key += nn(grad_scores, mine)
            keys_mine = jnp.where(low_t if h == 0 else ~low_t, keys_t, 0)
            grad_some += nn(keys_mine, grad_scores)
        grad_query.append(grad_some)
    grad_query = jnp.concatenate(grad_query, axis=1).T.astype(BF16) * HD**-0.5
    return grad_query, grad_key.astype(BF16), grad_value.astype(BF16)


def attend_back_kernel(*refs, group):
    q_ref, g_ref, o_ref, l_ref, kv_refs = refs[0], refs[1], refs[2], refs[3], refs[4 : 4 + group]
    dq_doc, dk_doc, dq_ref, dkv_ref, bias_ref = refs[4 + group :]

    @pl.when(pl.program_id(0) == 0)
    def _():
        bias_ref[...] = jnp.where(dk_doc[...] == dq_doc[...], 0.0, NEG_BIG)

    tokens = q_ref.shape[1]
    keys = jnp.concatenate([ref[0] for ref in kv_refs], axis=0)
    values = jnp.concatenate([ref[1] for ref in kv_refs], axis=0)
    log_rows = [l_ref[0, h : h + 1, :] for h in range(2)]
    grad_query, grad_key, grad_value = pair_back(
        q_ref[0], g_ref[...], o_ref[...], log_rows, keys, values, bias_ref, tokens
    )
    dq_ref[...] = grad_query
    for part in range(group):
        dkv_ref[part, 0] = grad_key[part * tokens : (part + 1) * tokens]
        dkv_ref[part, 1] = grad_value[part * tokens : (part + 1) * tokens]


def attend_back(query, grad_mixed, mixed, log_total, shared, doc_query, doc_key):
    _, tokens, width = query.shape
    group = len(shared)
    keys = group * tokens
    pairs = width // PAIR
    flat = pl.BlockSpec((tokens, PAIR), lambda p: (0, p))
    kv_spec = pl.BlockSpec((2, tokens, PAIR), lambda p: (0, 0, p))
    return call(
        functools.partial(attend_back_kernel, group=group),
        (pairs,),
        [
            pl.BlockSpec((1, tokens, PAIR), lambda p: (0, 0, p)),
            flat,
            flat,
            pl.BlockSpec((1, 2, tokens), lambda p: (p, 0, 0)),
        ]
        + [kv_spec] * group
        + [held((1, tokens)), held((keys, 1))],
        [flat, pl.BlockSpec((group, 2, tokens, PAIR), lambda p: (0, 0, 0, p))],
        [shaped((tokens, width), BF16), shaped((group, 2, tokens, width), BF16)],
        [pltpu.VMEM((keys, tokens), F32)],
        "attend_back",
        40 * tokens * keys * width,
        20 * tokens * width,
        (query, grad_mixed, mixed, log_total, *shared, doc_query, doc_key),
    )


def normed_of(hidden):
    center = hidden - jnp.mean(hidden, axis=1, keepdims=True)
    scale = lax.rsqrt(jnp.mean(center * center, axis=1, keepdims=True) + EPSILON)
    return center * scale, scale


def norm_back(grad_out, normed, scale, gain):
    scaled = grad_out * gain
    first = jnp.mean(scaled, axis=1, keepdims=True)
    second = jnp.mean(scaled * normed, axis=1, keepdims=True)
    return scale * (scaled - first - normed * second)


SLICE = 128


def by_tokens(tokens, body):
    step = min(SLICE, tokens)
    for at in range(0, tokens, step):
        body(pl.ds(at, step))


def out_kernel(m_ref, w_ref, x_ref, b_ref, n_ref, x1_ref, xb_ref, hat_ref, scale_ref, acc_ref, *, cols, deep):
    k = pl.program_id(0)
    rows, _, narrow, _ = w_ref.shape
    acc_ref[k] = nn(m_ref[...], w_ref[...].reshape(rows * narrow, deep))

    @pl.when(k == cols - 1)
    def _():
        def some(at):
            attn = jnp.concatenate([acc_ref[j, at] for j in range(cols)], axis=1)
            normed, scale = normed_of(x_ref[at].astype(F32) + (attn + b_ref[2:3]))
            x1 = normed * n_ref[0:1] + b_ref[3:4]
            x1_ref[at] = x1
            xb_ref[at] = x1.astype(BF16)
            hat_ref[at] = normed
            scale_ref[at] = jnp.broadcast_to(scale, scale_ref[at].shape)

        by_tokens(x_ref.shape[0], some)


def out_norm(mixed, weight, x, bias, gain):
    tokens, width = x.shape
    rows, cols, _, deep = weight.shape
    narrow = width // rows
    flat = held((tokens, width))
    return call(
        functools.partial(out_kernel, cols=cols, deep=deep),
        (cols,),
        [
            flat,
            pl.BlockSpec((rows, 1, narrow, deep), lambda k: (0, k, OUT, 0)),
            flat,
            held(bias.shape),
            held(gain.shape),
        ],
        [flat, flat, flat, held((tokens, 128))],
        [
            shaped((tokens, width), F32),
            shaped((tokens, width), BF16),
            shaped((tokens, width), F32),
            shaped((tokens, 128), F32),
        ],
        [pltpu.VMEM((cols, tokens, deep), F32)],
        "out_norm",
        2 * tokens * width * width,
        2 * width * width + 12 * tokens * width,
        (mixed, weight, x, bias, gain),
    )


def gelu_parts(pre):
    below = 0.5 * (1.0 + lax.erf(pre * 0.5**0.5))
    return pre * below, below + pre * jnp.exp(-0.5 * pre * pre) * (2.0 * jnp.pi) ** -0.5


def hidden_columns(block, width):
    rows, _, tall, deep = block.shape
    narrow = width // rows
    parts = [block[:, 0, i * narrow : (i + 1) * narrow].reshape(width, deep) for i in range(FEED_BLOCKS)]
    return jnp.concatenate(parts, axis=1)


def feed_kernel(xb_ref, wu_ref, wd_ref, ub_ref, x1_ref, b_ref, n_ref, y_ref, *rest, steps, saving):
    acc_ref = rest[-1]
    s = pl.program_id(0)
    width = xb_ref.shape[1]
    pre = nn(xb_ref[...], hidden_columns(wu_ref[...], width)) + ub_ref[...]
    act, slope = gelu_parts(pre)
    act = act.astype(BF16)
    if saving:
        rest[0][...] = act
        rest[1][...] = slope.astype(BF16)
    down = nt(act, hidden_columns(wd_ref[...], width))

    @pl.when(s == 0)
    def _():
        acc_ref[...] = down

    @pl.when(s > 0)
    def _():
        acc_ref[...] += down

    @pl.when(s == steps - 1)
    def _():
        def some(at):
            normed, scale = normed_of(x1_ref[at] + (acc_ref[at] + b_ref[4:5]))
            y_ref[at] = (normed * n_ref[1:2] + b_ref[5:6]).astype(BF16)
            if saving:
                rest[2][at] = normed
                rest[3][at] = jnp.broadcast_to(scale, rest[3][at].shape)

        by_tokens(xb_ref.shape[0], some)


def feed_specs(weight, tokens, width, units):
    rows, cols, _, deep = weight.shape
    tall = FEED_BLOCKS * (width // rows)
    block = FEED_BLOCKS * deep
    per = units // cols // block

    def at(first):
        return pl.BlockSpec((rows, 1, tall, deep), lambda s: (0, s // per, first // FEED_BLOCKS + s % per, 0))

    wide = pl.BlockSpec((tokens, block), lambda s: (0, s))
    line = pl.BlockSpec((1, block), lambda s: (0, s))
    return cols * per, at(UNIT), at(UNIT + per * FEED_BLOCKS), wide, line


def feed(x1_bf, weight, unit_shift, x1, bias, gain, saving):
    tokens, width = x1.shape
    units = unit_shift.shape[1]
    steps, first, second, wide, line = feed_specs(weight, tokens, width, units)
    flat = held((tokens, width))
    out_specs, out_shape = [flat], [shaped((tokens, width), BF16)]
    if saving:
        out_specs += [wide, wide, flat, held((tokens, 128))]
        out_shape += [
            shaped((tokens, units), BF16),
            shaped((tokens, units), BF16),
            shaped((tokens, width), F32),
            shaped((tokens, 128), F32),
        ]
    return call(
        functools.partial(feed_kernel, steps=steps, saving=saving),
        (steps,),
        [flat, first, second, line, flat, held(bias.shape), held(gain.shape)],
        out_specs,
        out_shape,
        [pltpu.VMEM((tokens, width), F32)],
        "feed",
        4 * tokens * width * units,
        4 * width * units,
        (x1_bf, weight, weight, unit_shift, x1, bias, gain),
    )


def column_sum(value):
    return jnp.sum(value, axis=0, keepdims=True)


def top_back_kernel(dy_ref, hat_ref, scale_ref, n_ref, dh2_ref, ddown_ref, *sums_ref):
    for ref in sums_ref:
        ref[...] = jnp.zeros_like(ref)

    def some(at):
        dy, hat = dy_ref[at].astype(F32), hat_ref[at]
        dh2 = norm_back(dy, hat, scale_ref[at][:, :1], n_ref[1:2])
        dh2_ref[at] = dh2
        ddown = dh2.astype(BF16)
        ddown_ref[at] = ddown
        for ref in sums_ref:
            ref[0:1] += column_sum(ddown.astype(F32))
            ref[1:2] += column_sum(dy)
            ref[2:3] += column_sum(dy * hat)

    by_tokens(dy_ref.shape[0], some)


def top_back(dy, hat2, scale2, gain, sums_too):
    tokens, width = hat2.shape
    flat = held((tokens, width))
    return call(
        top_back_kernel,
        (1,),
        [flat, flat, held((tokens, 128)), held(gain.shape)],
        [flat, flat] + [held((8, width))] * sums_too,
        [shaped((tokens, width), F32), shaped((tokens, width), BF16)] + [shaped((8, width), F32)] * sums_too,
        [],
        "top_back",
        20 * tokens * width,
        12 * tokens * width,
        (dy, hat2, scale2, gain),
    )


def feed_back_kernel(*refs, steps, sums_too):
    dh2_ref, ddown_ref, hat1_ref, scale1_ref, slope_ref, wu_ref, wd_ref, n_ref, dattn_ref = refs[:9]
    acc_ref = refs[-1]
    s = pl.program_id(0)
    tokens, width = dh2_ref.shape
    dact = nn(ddown_ref[...], hidden_columns(wd_ref[...], width))
    dpre = (dact * slope_ref[...].astype(F32)).astype(BF16)
    back = nt(dpre, hidden_columns(wu_ref[...], width))
    if sums_too:
        dpre_ref, pre_ref, sums_ref = refs[9:12]
        dpre_ref[...] = dpre
        pre_ref[...] = column_sum(dpre.astype(F32))

    @pl.when(s == 0)
    def _():
        acc_ref[...] = back

    @pl.when(s > 0)
    def _():
        acc_ref[...] += back

    @pl.when(s == steps - 1)
    def _():
        if sums_too:
            sums_ref[...] = jnp.zeros_like(sums_ref)

        def some(at):
            dx1, hat = dh2_ref[at] + acc_ref[at], hat1_ref[at]
            dattn = norm_back(dx1, hat, scale1_ref[at][:, :1], n_ref[0:1]).astype(BF16)
            dattn_ref[at] = dattn
            if sums_too:
                sums_ref[0:1] += column_sum(dattn.astype(F32))
                sums_ref[1:2] += column_sum(dx1)
                sums_ref[2:3] += column_sum(dx1 * hat)

        by_tokens(tokens, some)


def feed_back(dh2, ddown, hat1, scale1, slope, weight, gain, sums_too):
    tokens, width = dh2.shape
    units = slope.shape[1]
    steps, first, second, wide, line = feed_specs(weight, tokens, width, units)
    flat = held((tokens, width))
    out_specs, out_shape = [flat], [shaped((tokens, width), BF16)]
    if sums_too:
        out_specs += [wide, line, held((8, width))]
        out_shape += [shaped((tokens, units), BF16), shaped((1, units), F32), shaped((8, width), F32)]
    return call(
        functools.partial(feed_back_kernel, steps=steps, sums_too=sums_too),
        (steps,),
        [flat, flat, flat, held((tokens, 128)), wide, first, second, held(gain.shape)],
        out_specs,
        out_shape,
        [pltpu.VMEM((tokens, width), F32)],
        "feed_back",
        4 * tokens * width * units,
        4 * width * units,
        (dh2, ddown, hat1, scale1, slope, weight, weight, gain),
    )


def mixed_back_kernel(g_ref, w_ref, o_ref):
    o_ref[...] = nt(g_ref[...], side_by_side(w_ref[...])).astype(BF16)


def mixed_back(grad, weight):
    tokens, width = grad.shape
    rows, cols, _, deep = weight.shape
    narrow = width // rows
    take = row_blocks(rows, narrow)
    return call(
        mixed_back_kernel,
        (rows // take,),
        [held((tokens, width)), pl.BlockSpec((take, cols, narrow, deep), lambda r: (r, 0, OUT, 0))],
        pl.BlockSpec((tokens, take * narrow), lambda r: (0, r)),
        shaped((tokens, width), BF16),
        [],
        "mixed_back",
        2 * tokens * width * width,
        2 * width * width,
        (grad, weight),
    )


def input_back_kernel(*refs, group):
    dq_ref, own_ref, others, (w_ref, dattn_ref, dx_ref, dp_ref) = refs[0], refs[1], refs[2 : 1 + group], refs[1 + group :]
    tokens, width = dq_ref.shape
    rows, _, tall, deep = w_ref.shape
    narrow = tall // 3

    @pl.when(pl.program_id(0) == 0)
    def _():
        def some(at):
            dp_ref[0, at] = dq_ref[at]
            for j in range(2):
                total = own_ref[0, j, at].astype(F32)
                for other in others:
                    total += other[j, at].astype(F32)
                dp_ref[1 + j, at] = total.astype(BF16)

        by_tokens(tokens, some)

    total = dattn_ref[...].astype(F32)
    for j in range(3):
        total += nn(dp_ref[j], w_ref[:, 0, j * narrow : (j + 1) * narrow].reshape(width, deep))
    dx_ref[...] = total.astype(BF16)


def input_back(dq, dkv, others, weight, dattn):
    tokens, width = dq.shape
    group = dkv.shape[0]
    rows, cols, _, deep = weight.shape
    part = pl.BlockSpec((tokens, deep), lambda k: (0, k))
    return call(
        functools.partial(input_back_kernel, group=group),
        (cols,),
        [held((tokens, width)), held((1, 2, tokens, width))]
        + [held((2, tokens, width))] * (group - 1)
        + [pl.BlockSpec((rows, 1, 3 * (width // rows), deep), lambda k: (0, k, 0, 0)), part],
        part,
        shaped((tokens, width), BF16),
        [pltpu.VMEM((3, tokens, width), BF16)],
        "input_back",
        6 * tokens * width * width,
        6 * width * width,
        (dq, dkv, *others, weight, dattn),
    )


class Layout:
    def __init__(self, tokens_in, doc_ids):
        self.micro, self.narrow, _ = tokens_in.shape
        self.seq_here, self.seq_len = doc_ids.shape[1:]
        self.rows = lax.axis_size("row")
        self.cols = lax.axis_size("high") * CORES
        self.width = self.narrow * self.rows
        self.places = self.rows * CORES
        self.sequences = self.micro * self.seq_here * CORES
        self.group = self.places // self.sequences
        self.part = self.seq_len // self.group
        self.row = lax.axis_index("row")
        place = self.row * CORES + lax.axis_index("core")
        self.sequence = place // self.group
        self.position = place % self.group
        self.block = (self.sequence // CORES) * self.group + self.position

    def routes(self, shift):
        pairs = []
        for source in range(self.places):
            row, core = divmod(source, CORES)
            block = (row + shift) % self.rows
            sequence = (block // self.group) * CORES + core
            pairs.append((source, sequence * self.group + block % self.group))
        return pairs

    def to_features(self, array):
        blocks = array.T.reshape(self.rows, self.narrow, self.part)
        got = []
        for shift in range(self.rows):
            block = lax.dynamic_index_in_dim(blocks, (self.block - shift) % self.rows, 0, False)
            pairs = [(there, here) for here, there in self.routes(shift)]
            got.append(lax.ppermute(block, ("row", "core"), pairs))
        order = (jnp.arange(self.rows) - self.row) % self.rows
        whole = jnp.take(jnp.stack(got), order, axis=0)
        whole = whole.reshape(self.micro, self.seq_here * self.group, self.narrow, self.part)
        return whole.transpose(0, 2, 1, 3).reshape(self.micro, self.narrow, self.seq_here * self.seq_len)

    def within(self, step):
        return [
            (place, place // self.group * self.group + (place + step) % self.group)
            for place in range(self.places)
        ]

    def share(self, array):
        return [array] + [
            lax.ppermute(array, ("row", "core"), self.within(step)) for step in range(1, self.group)
        ]

    def give_back(self, blocks):
        return [
            lax.ppermute(blocks[step], ("row", "core"), self.within(self.group - step))
            for step in range(1, self.group)
        ]


class Line:
    def __init__(self, axis, size):
        self.axis, self.size, self.here = axis, size, lax.axis_index(axis)

    def sends(self, step):
        last = self.size - 1
        return (
            (True, (self.here < step) & (self.here < last), self.size - step + self.here, self.here > 0),
            (False, (last - self.here < step) & (self.here > 0), step - self.size + self.here, self.here < last),
        )

    def gets(self, step):
        last = self.size - 1
        return (
            (True, (self.here >= 1) & (self.here <= step)),
            (False, (last - self.here >= 1) & (last - self.here <= step)),
        )

    def neighbour(self, right):
        return {self.axis: self.here + (1 if right else -1)}


def greet(lines, pairs, members=()):
    barrier = pltpu.get_barrier_semaphore()
    count = 0
    for line in lines:
        for right, there in ((True, line.here < line.size - 1), (False, line.here > 0)):

            @pl.when(there)
            def _(line=line, right=right):
                pl.semaphore_signal(barrier, 1, device_id=line.neighbour(right), device_id_type=MESH)

            count = count + there.astype(jnp.int32)
    for axis in pairs:
        pl.semaphore_signal(barrier, 1, device_id={axis: 1 - lax.axis_index(axis)}, device_id_type=MESH)
        count = count + 1
    for member in members:
        pl.semaphore_signal(barrier, 1, device_id=member, device_id_type=MESH)
        count = count + 1
    pl.semaphore_wait(barrier, count)


def add_into(target, other):
    lead = target.shape[:-2]
    rows = target.shape[-2]
    total = 1
    for size in lead:
        total *= size
    if total == 1:
        target[...] = target[...] + other[...]
        return

    @pl.loop(0, total)
    def _(i):
        index = []
        for size in reversed(lead):
            index.insert(0, lax.rem(i, size))
            i = lax.div(i, size)
        index = tuple(index)
        target[index] = target[index] + other[index]


class Scatter:
    def __init__(self, pieces, refs, highs, rows):
        self.pieces = pieces
        (self.landing, self.work, self.got, self.from_high, self.got_high, self.from_row, self.out, *sems) = refs
        self.sem_core, self.sem_load, self.sem_high, self.sem_row = sems
        self.high, self.row = Line("high", highs), Line("row", rows)
        self.core = lax.axis_index("core")
        self.slots = self.work.shape[0]
        self.sent = [[] for _ in pieces]

    def slot(self, q):
        return q % self.slots

    def cut(self, q, ref):
        return ref.at[..., pl.ds(0, self.pieces[q][2]), :]

    def source(self, q, y, core):
        ref, first, rows = self.pieces[q]
        return ref.at[:, y, core, pl.ds(first, rows)]

    def to_core(self, q, y):
        return pltpu.make_async_remote_copy(
            self.source(q, y, 1 - self.core),
            self.cut(q, self.landing.at[q, y]),
            self.sem_core.at[q, y, 0],
            self.sem_core.at[q, y, 1],
            device_id={"core": 1 - self.core},
            device_id_type=MESH,
        )

    def load(self, q, y):
        return pltpu.make_async_copy(
            self.source(q, y, self.core), self.cut(q, self.work.at[self.slot(q), y]), self.sem_load.at[q, y, 0]
        )

    def fetch(self, q, y):
        return pltpu.make_async_copy(
            self.cut(q, self.landing.at[q, y]), self.cut(q, self.got.at[q % 2, y]), self.sem_load.at[q, y, 1]
        )

    def begin(self, q):
        if q >= self.slots:
            self.finish_sends(q - self.slots)
        for y in range(self.high.size):
            self.to_core(q, y).start()
            self.load(q, y).start()

    def arrive(self, q):
        for y in range(self.high.size):
            copy = self.to_core(q, y)
            copy.wait()
            self.fetch(q, y).start()

    def merge(self, q):
        for y in range(self.high.size):
            self.load(q, y).wait()
            self.fetch(q, y).wait()
            add_into(self.cut(q, self.work.at[self.slot(q), y]), self.cut(q, self.got.at[q % 2, y]))
        self.push(q, self.high, 1)

    def parts(self, q, line):
        work = self.work.at[self.slot(q)]
        if line is self.high:
            return (lambda t: self.cut(q, work.at[t])), self.from_high.at[q], self.sem_high.at[q]
        return (lambda t: self.cut(q, work.at[self.high.here, t])), self.from_row.at[q], self.sem_row.at[q]

    def copy(self, q, line, step, right, block):
        where, landing, sems = self.parts(q, line)
        way = 0 if right else 1
        way_slot = 0 if line.size == 2 else way
        return pltpu.make_async_remote_copy(
            where(block),
            self.cut(q, landing.at[step - 1, way_slot]),
            sems.at[step - 1, way, 0],
            sems.at[step - 1, way, 1],
            device_id=line.neighbour(right),
            device_id_type=MESH,
        )

    def landed(self, q, line, step, right):
        way = 0 if line.size == 2 or right else 1
        if line is self.high:
            return self.cut(q, self.got_high.at[q % 2, way])
        return self.cut(q, self.from_row.at[q, step - 1, way])

    def push(self, q, line, step):
        where, _, _ = self.parts(q, line)
        for right, there, block, more in line.sends(step):

            @pl.when(there)
            def _(right=right, block=block, more=more):
                if step > 1:

                    @pl.when(more)
                    def _():
                        add_into(where(block), self.landed(q, line, step - 1, right))

                self.copy(q, line, step, right, block).start()

            self.sent[q].append((line, step, right, there, block))

    def pull(self, q, line, step):
        for right, there in line.gets(step):

            @pl.when(there)
            def _(right=right):
                self.copy(q, line, step, right, 0).wait_recv()
                if line is self.high:
                    way = 0 if line.size == 2 or right else 1
                    fetch = pltpu.make_async_copy(
                        self.cut(q, self.from_high.at[q, step - 1, way]),
                        self.landed(q, line, step, right),
                        self.sem_high.at[q, step - 1, way, 2],
                    )
                    fetch.start()
                    fetch.wait()

    def close(self, q, line):
        where, _, _ = self.parts(q, line)
        for right, there in line.gets(line.size - 1):

            @pl.when(there)
            def _(right=right):
                add_into(where(line.here), self.landed(q, line, line.size - 1, right))

    def give(self, q, at):
        where, _, _ = self.parts(q, self.row)
        rows = self.pieces[q][2]
        self.out[pl.ds(at, rows)] = where(self.row.here)[...].astype(F32)

    def finish_sends(self, q):
        for line, step, right, there, block in self.sent[q]:

            @pl.when(there)
            def _(line=line, step=step, right=right, block=block):
                self.copy(q, line, step, right, block).wait_send()

        self.sent[q] = []

    def stages(self):
        stages = [self.begin, self.arrive, self.merge, lambda q: None]
        for line in (self.high, self.row):
            for step in range(1, line.size):

                def one(q, line=line, step=step):
                    self.pull(q, line, step)
                    if step < line.size - 1:
                        self.push(q, line, step + 1)
                        return
                    self.close(q, line)
                    if line is self.high:
                        self.push(q, self.row, 1)
                    else:
                        self.give(q, self.at[q])

                stages.append(one)
        return stages

    def run(self, between=None):
        self.at, at = [], 0
        for _, _, rows in self.pieces:
            self.at.append(at)
            at += rows
        stages = self.stages()
        count = len(self.pieces)
        for tick in range(count + len(stages) - 1):
            for q in range(max(0, tick - len(stages) + 1), min(tick + 1, count)):
                stages[tick - q](q)
            if between is not None:
                between(tick)
        for q in range(count):
            self.finish_sends(q)


STAGES = 3


def low_kernel(*refs, highs, rows, group):
    (ddown_hbm, act_hbm, x1_hbm, dpre_hbm, dattn_hbm, q_hbm, mixed_hbm, log_hbm, x_hbm, w_hbm, *kv_hbm) = refs[: 10 + group]
    bias_doc_q, bias_doc_k, pre_ref, sums_ref = refs[10 + group : 14 + group]
    out_ref, dx_ref, landing, high_landing = refs[14 + group : 18 + group]
    (dattn, x, q, mixed, log, w_out, w_qkv, kv, dmixed, bias, dkv_got, stage, small, left, right,
     work, got, got_high, from_row, sem_in, sem_right, sem_core, sem_load, sem_high, sem_row, sem_kv) = refs[18 + group :]
    tokens, width = dattn.shape
    narrow, deep = stage.shape[-2:]
    dq, dkv = q, kv
    cols = highs * CORES

    row_at = lax.axis_index("row")
    place = row_at * CORES + lax.axis_index("core")
    position = lax.rem(place, group)

    def member(step):
        other = place - position + lax.rem(position + step, group)
        return {"row": lax.div(other, CORES), "core": lax.rem(other, CORES)}

    units = act_hbm.shape[1]
    feed_pieces = units // cols // deep
    tail = small.shape[3]
    order = [("down", i) for i in range(feed_pieces)] + [("out", 0)]
    order += [("unit", i) for i in range(feed_pieces)] + [("qkv", 0), ("qkv", 1), ("qkv", 2), ("small", 0)]
    pieces = [(stage.at[i % STAGES], 0, narrow) for i in range(len(order) - 1)] + [(small, 0, tail)]
    scatter = Scatter(
        pieces, (landing, work, got, high_landing, got_high, from_row, out_ref, sem_core, sem_load, sem_high, sem_row), highs, rows
    )

    inputs = [
        (ddown_hbm, dattn),
        (x1_hbm, x),
        (dattn_hbm, dattn),
        (w_hbm.at[:, :, pl.ds(OUT * narrow, narrow)], w_out),
        (mixed_hbm, mixed),
        (q_hbm.at[0], q),
        (log_hbm, log),
        *[(kv_hbm[i], kv.at[i]) for i in range(group)],
        (w_hbm.at[:, :, pl.ds(QKV * narrow, 3 * narrow)], w_qkv),
        (x_hbm, x),
    ]
    loads = [pltpu.make_async_copy(a, b, sem_in.at[i]) for i, (a, b) in enumerate(inputs)]
    early = 7 + group

    def share_grads(step):
        return pltpu.make_async_remote_copy(
            dkv.at[step], dkv_got.at[step - 1], sem_kv.at[step - 1, 0], sem_kv.at[step - 1, 1],
            device_id=member(group - step), device_id_type=MESH,
        )

    take = row_blocks(rows, narrow)

    def prepare():
        for load in loads[2:early]:
            load.wait()
        bias[...] = jnp.where(bias_doc_k[...] == bias_doc_q[...], 0.0, NEG_BIG).astype(BF16)

        @pl.loop(0, rows // take)
        def _(r):
            at = pl.ds(pl.multiple_of(r * take * narrow, take * narrow), take * narrow)
            dmixed[:, at] = nt(dattn[...], side_by_side(w_out[pl.ds(r * take, take)])).astype(BF16)

    def fill(slot, block, loaded=None):
        @pl.loop(0, cols)
        def _(k):
            grad = nn(left[...], block(k)).astype(BF16)
            stage[slot, :, lax.div(k, CORES), lax.rem(k, CORES)] = grad.reshape(rows, narrow, deep)

    def column(ref):
        return lambda k: ref[:, pl.ds(pl.multiple_of(k * deep, deep), deep)]

    def fetch(q):
        name, i = order[q]
        source = act_hbm if name == "down" else dpre_hbm
        return [
            pltpu.make_async_copy(
                source.at[:, pl.ds(k * feed_pieces * deep + i * deep, deep)],
                right.at[q % 2, :, pl.ds(k * deep, deep)],
                sem_right.at[q % 2, k],
            )
            for k in range(cols)
        ]

    def is_feed(q):
        return q < len(order) and order[q][0] in ("down", "unit")

    def make(q):
        name, i = order[q]
        slot = q % STAGES
        if q == 0:
            loads[0].wait()
            left[...] = dattn[...].T
            loads[2].start()
        if name in ("down", "unit"):
            if (name, i) == ("unit", 0):
                left[...] = x[...].T
                loads[-1].start()
            for copy in fetch(q):
                copy.wait()
            if is_feed(q + 1):
                for copy in fetch(q + 1):
                    copy.start()
            fill(slot, column(right.at[q % 2]))
        elif name == "out":
            if is_feed(q + 1):
                for copy in fetch(q + 1):
                    copy.start()
            left[...] = mixed[...].T
            fill(slot, column(dattn))
        elif name == "qkv":
            if i == 0:
                loads[-1].wait()
            left[...] = grads_of(i).T
            fill(slot, column(x))
        else:
            small_sums()

    pairs = width // PAIR

    def heads(first, count):
        @pl.loop(first, first + count)
        def _(p):
            at = pl.ds(pl.multiple_of(p * PAIR, PAIR), PAIR)
            keys = jnp.concatenate([kv[i, 0, :, at] for i in range(group)], axis=0)
            values = jnp.concatenate([kv[i, 1, :, at] for i in range(group)], axis=0)
            grad_query, grad_key, grad_value = pair_back(
                q[:, at], dmixed[:, at], mixed[:, at], [log[p, h : h + 1] for h in range(2)], keys, values, bias,
                min(256, tokens),
            )
            dq[:, at] = grad_query
            for part in range(group):
                dkv[part, 0, :, at] = grad_key[part * tokens : (part + 1) * tokens]
                dkv[part, 1, :, at] = grad_value[part * tokens : (part + 1) * tokens]

    def exchange():
        for step in range(1, group):
            share_grads(step).start()

    def join():
        for step in range(1, group):
            share_grads(step).wait()
        for load in loads[early:-1]:
            load.wait()

        @pl.loop(0, tokens, step=min(SLICE, tokens))
        def _(at):
            some = pl.ds(pl.multiple_of(at, min(SLICE, tokens)), min(SLICE, tokens))
            for j in range(2):
                total = dkv[0, j, some].astype(F32)
                for step in range(1, group):
                    total += dkv_got[step - 1, j, some].astype(F32)
                dkv[0, j, some] = total.astype(BF16)

    def grads_of(j):
        return dq[...] if j == 0 else dkv[0, j - 1]

    def input_gradient():
        for k in range(cols):
            at = slice(k * deep, (k + 1) * deep)
            total = dattn[:, at].astype(F32)
            for j in range(3):
                total += nn(grads_of(j), w_qkv[:, k, j * narrow : (j + 1) * narrow].reshape(width, deep))
            dx_ref[:, at] = total.astype(BF16)

    def small_sums():
        vectors = jnp.concatenate([column_sum(grads_of(j).astype(F32)) for j in (0, 2)] + [sums_ref[...]], axis=0)
        vectors = vectors.astype(BF16)
        small[...] = jnp.zeros_like(small)
        lines = pre_ref.shape[1] // cols // deep
        for r in range(rows):
            for k in range(cols):
                small[r, k // CORES, k % CORES, 0:8, 0:narrow] = vectors[:, r * narrow : (r + 1) * narrow]
                for i in range(lines):
                    at = (k * lines + i) * deep
                    small[r, k // CORES, k % CORES, 8 + i : 9 + i] = pre_ref[:, at : at + deep].astype(BF16)

    def between(tick):
        if tick + 1 < len(order):
            make(tick + 1)
        if tick == 1:
            prepare()
        if 2 <= tick < 6:
            heads((tick - 2) * (pairs // 4), pairs // 4)
        if tick == 5:
            exchange()
        if tick == 6:
            join()
        if tick == 7:
            input_gradient()

    for i, load in enumerate(loads[:-1]):
        if i != 2:
            load.start()
    for copy in fetch(0):
        copy.start()
    greet((scatter.high, scatter.row), ("core",), [member(step) for step in range(1, group)])
    loads[1].wait()
    make(0)
    scatter.run(between)


def low_back(ddown, act, x1_bf, dpre, dattn, query, mixed, log_total, x, weight, shared, doc_query, doc_key, pre_sum, sums):
    tokens, width = dattn.shape
    rows, cols, _, deep = weight.shape
    narrow = width // rows
    units = act.shape[1]
    feed_rows = narrow * units // cols // deep
    highs, group, keys = cols // CORES, len(shared), len(shared) * tokens
    apart = (rows, highs, CORES)
    tail = 16
    lines = 8 + pre_sum.shape[1] // cols // deep
    assert lines <= tail and narrow <= deep
    count = 2 * (feed_rows // narrow) + 5
    height = 2 * feed_rows + 4 * narrow + tail
    steps = 4 + highs - 1 + rows - 1
    slots = min(count, steps)
    in_any = pl.BlockSpec(memory_space=pl.ANY)
    in_vmem = pl.BlockSpec(memory_space=pltpu.VMEM)
    ways = {2: 1}
    block = (rows, narrow, deep)
    dma = pltpu.SemaphoreType.DMA
    args = [ddown, act, x1_bf, dpre, dattn, query, mixed, log_total, x, weight, *shared]
    out, dx, _, _ = pl.pallas_call(
        functools.partial(low_kernel, highs=highs, rows=rows, group=group),
        in_specs=[in_any] * len(args) + [in_vmem] * 4,
        out_specs=[in_vmem, in_vmem, in_any, in_any],
        out_shape=[
            shaped((height, deep), F32),
            shaped((tokens, width), BF16),
            shaped((count, highs) + block, BF16),
            shaped((count, highs - 1, ways.get(highs, 2)) + block, BF16),
        ],
        scratch_shapes=[
            pltpu.VMEM((tokens, width), BF16),
            pltpu.VMEM((tokens, width), BF16),
            pltpu.VMEM((tokens, width), BF16),
            pltpu.VMEM((tokens, width), BF16),
            pltpu.VMEM(log_total.shape, F32),
            pltpu.VMEM((rows, cols, narrow, deep), BF16),
            pltpu.VMEM((rows, cols, 3 * narrow, deep), BF16),
            pltpu.VMEM((group, 2, tokens, width), BF16),
            pltpu.VMEM((tokens, width), BF16),
            pltpu.VMEM((keys, tokens), BF16),
            pltpu.VMEM((group - 1, 2, tokens, width), BF16),
            pltpu.VMEM((STAGES,) + apart + (narrow, deep), BF16),
            pltpu.VMEM(apart + (tail, deep), BF16),
            pltpu.VMEM((width, tokens), BF16),
            pltpu.VMEM((2, tokens, cols * deep), BF16),
            pltpu.VMEM((slots, highs) + block, BF16),
            pltpu.VMEM((2, highs) + block, BF16),
            pltpu.VMEM((2, ways.get(highs, 2)) + block, BF16),
            pltpu.VMEM((count, rows - 1, ways.get(rows, 2), narrow, deep), BF16),
            dma((9 + group,)),
            dma((2, cols)),
            dma((count, highs, 2)),
            dma((count, highs, 2)),
            dma((count, highs - 1, 2, 3)),
            dma((count, rows - 1, 2, 2)),
            dma((max(1, group - 1), 2)),
        ],
        name="low_back",
        compiler_params=pltpu.CompilerParams(collective_id=1, has_side_effects=True, vmem_limit_bytes=LOW_VMEM),
        cost_estimate=pl.CostEstimate(
            flops=64 * tokens * width * width, bytes_accessed=height * deep * rows * cols * 4, transcendentals=0
        ),
    )(*args, doc_query, doc_key, pre_sum, sums)
    return dx, out


class Spread:
    def __init__(self, axis, size):
        self.axis, self.size, self.here = axis, size, lax.axis_index(axis)

    def sends(self, step):
        last = self.size - 1
        return (
            (True, (self.here < last) & (self.here >= step - 1), self.here - step + 1),
            (False, (self.here > 0) & (self.here + step - 1 <= last), self.here + step - 1),
        )

    def gets(self, step):
        last = self.size - 1
        return ((True, self.here >= step), (False, self.here + step <= last))

    def neighbour(self, right):
        return {self.axis: self.here + (1 if right else -1)}


class Gather:
    def __init__(self, pieces, sems, highs, rows):
        self.pieces = pieces
        self.sem_row, self.sem_high, self.sem_core = sems
        self.row, self.high = Spread("row", rows), Spread("high", highs)
        self.core = lax.axis_index("core")
        self.sent = []

    def block(self, q, line, i):
        ref, first, count, row_first = self.pieces[q]
        some = pl.ds(first, count)
        if line is self.row:
            return ref.at[i, self.high.here if row_first else slice(None), self.core, some]
        return ref.at[slice(None) if row_first else self.row.here, i, self.core, some]

    def copy(self, q, line, step, right, i):
        sems = (self.sem_row if line is self.row else self.sem_high).at[q, step - 1, 0 if right else 1]
        ref = self.block(q, line, i)
        return pltpu.make_async_remote_copy(
            ref, ref, sems.at[0], sems.at[1], device_id=line.neighbour(right), device_id_type=MESH
        )

    def push(self, q, line, step):
        for right, there, i in line.sends(step):

            @pl.when(there)
            def _(right=right, i=i):
                self.copy(q, line, step, right, i).start()

            self.sent.append((q, line, step, right, there, i))

    def pull(self, q, line, step):
        for right, there in line.gets(step):

            @pl.when(there)
            def _(right=right):
                self.copy(q, line, step, right, line.here).wait_recv()

    def to_core(self, q):
        ref, first, count, _ = self.pieces[q]
        ref = ref.at[:, :, self.core, pl.ds(first, count)]
        return pltpu.make_async_remote_copy(
            ref, ref, self.sem_core.at[q, 0], self.sem_core.at[q, 1],
            device_id={"core": 1 - self.core}, device_id_type=MESH,
        )

    def stages(self, q):
        first, second = (self.row, self.high) if self.pieces[q][3] else (self.high, self.row)
        steps = [lambda: self.push(q, first, 1)]
        lines = [(first, i) for i in range(1, first.size)] + [(second, i) for i in range(1, second.size)]
        for n, (line, step) in enumerate(lines):

            def one(n=n, line=line, step=step):
                self.pull(q, line, step)
                if n + 1 < len(lines):
                    self.push(q, *lines[n + 1])
                else:
                    self.to_core(q).start()

            if n == len(lines) - 1:
                steps.append(lambda: None)
            steps.append(one)
        steps.append(lambda: self.to_core(q).wait())
        return steps

    def run(self, between):
        stages = [self.stages(q) for q in range(len(self.pieces))]
        depth, count = len(stages[0]), len(stages)
        for tick in range(count + depth - 1):
            for q in range(max(0, tick - depth + 1), min(tick + 1, count)):
                stages[q][tick - q]()
            between(tick, tick - depth + 1)

    def finish(self):
        for q, line, step, right, there, i in self.sent:

            @pl.when(there)
            def _(q=q, line=line, step=step, right=right, i=i):
                self.copy(q, line, step, right, i).wait_send()


class Group:
    def __init__(self, size):
        self.size = size
        self.place = lax.axis_index("row") * CORES + lax.axis_index("core")
        self.position = lax.rem(self.place, size)

    def member(self, step):
        other = self.place - self.position + lax.rem(self.position + step, self.size)
        return {"row": lax.div(other, CORES), "core": lax.rem(other, CORES)}

    def members(self):
        return [self.member(step) for step in range(1, self.size)]


class Front:
    def __init__(self, w, vectors, shift, x, q, kv, mixed, mask, x1, x1_bf, acc, log=None):
        self.w, self.vectors, self.shift, self.x, self.q, self.kv = w, vectors, shift, x, q, kv
        self.mixed, self.mask, self.x1, self.x1_bf, self.acc, self.log = mixed, mask, x1, x1_bf, acc, log
        self.tokens, self.width = x.shape
        self.rows, self.highs, _, _, self.deep = w.shape
        self.cols = self.highs * CORES
        self.narrow = self.width // self.rows
        self.group = kv.shape[0]
        self.pairs = self.width // PAIR
        self.blocks = shift.shape[1] // self.cols // self.deep

    def matrix(self, block, k):
        at = pl.ds(block * self.narrow, self.narrow)
        return self.w[:, k // CORES, k % CORES, at].reshape(self.width, self.deep)

    def project(self, j):
        take = row_blocks(self.rows, self.narrow)
        for r in range(0, self.rows, take):
            at = slice(r * self.narrow, (r + take) * self.narrow)
            some = pl.ds((QKV + j) * self.narrow, self.narrow)
            weight = jnp.concatenate(
                [
                    self.w[r : r + take, k // CORES, k % CORES, some].reshape(take * self.narrow, self.deep)
                    for k in range(self.cols)
                ],
                axis=1,
            )
            out = nt(self.x[...], weight)
            if j == 0:
                self.q[:, at] = ((out + self.vectors[0:1, at]) * HD**-0.5).astype(BF16)
            elif j == 1:
                self.kv[0, 0, :, at] = out.astype(BF16)
            else:
                self.kv[0, 1, :, at] = (out + self.vectors[1:2, at]).astype(BF16)

    def attend(self, first, count):
        @pl.loop(first, first + count)
        def _(p):
            at = pl.ds(pl.multiple_of(p * PAIR, PAIR), PAIR)
            keys = jnp.concatenate([self.kv[i, 0, :, at] for i in range(self.group)], axis=0)
            values = jnp.concatenate([self.kv[i, 1, :, at] for i in range(self.group)], axis=0)
            mixed, log_rows = pair_front(self.q[:, at], keys, values, self.mask)
            self.mixed[:, at] = mixed
            if self.log is not None:
                for h in range(2):
                    self.log[p, h : h + 1] = log_rows[h]

    def out(self):
        for k in range(self.cols):
            at = slice(k * self.deep, (k + 1) * self.deep)
            self.acc[:, at] = nn(self.mixed[...], self.matrix(OUT, k))

    def norm_one(self, keep=None):
        def some(at):
            attn = self.acc[at] + self.vectors[2:3]
            normed, scale = normed_of(self.x[at].astype(F32) + attn)
            x1 = normed * self.vectors[6:7] + self.vectors[3:4]
            self.x1[at] = x1
            self.x1_bf[at] = x1.astype(BF16)
            if keep is not None:
                keep(at, normed, scale)

        by_tokens(self.tokens, some)

    def feed(self, block, ks, start, keep=None, at=slice(None)):
        up = jnp.concatenate([self.matrix(UNIT + block, k) for k in ks], axis=1)
        down = jnp.concatenate([self.matrix(UNIT + self.blocks + block, k) for k in ks], axis=1)
        hidden = self.blocks * self.deep
        begins = [k * hidden + block * self.deep for k in ks]
        shift = jnp.concatenate([self.shift[:, b : b + self.deep] for b in begins], axis=1)
        act, slope = gelu_parts(nn(self.x1_bf[at], up) + shift)
        act = act.astype(BF16)
        if keep is not None:
            keep(act, slope.astype(BF16))
        more = nt(act, down)
        if start:
            self.acc[at] = more
        else:
            self.acc[at] += more

    def norm_two(self, at, keep=None):
        normed, scale = normed_of(self.x1[at] + (self.acc[at] + self.vectors[4:5]))
        if keep is not None:
            keep(at, normed, scale)
        return normed * self.vectors[7:8] + self.vectors[5:6]


def share_keys(group, kv, sems):
    def copy(step):
        return pltpu.make_async_remote_copy(
            kv.at[0], kv.at[step], sems.at[step - 1, 0], sems.at[step - 1, 1],
            device_id=group.member(step), device_id_type=MESH,
        )

    return [copy(step) for step in range(1, group.size)]


def first_kernel(*refs, highs, rows, group, micro, seq_here, seq_len):
    (small_ref, tokens_hbm, cot_hbm, qkv_ref, out_ref, unit_ref, down_ref) = refs[:7]
    (next_hbm, start_ref, w_hbm, vectors, shift, doc_q, doc_k) = refs[7:14]
    (w, small, turned, x, q, kv, mixed, mask, x1, x1_bf, acc, y,
     sem_row, sem_high, sem_core, sem_x, sem_kv, sem_y, sem_w, sem_next) = refs[14:]
    tokens, width = x.shape
    narrow, deep = width // rows, w.shape[-1]
    cols = highs * CORES
    hidden = unit_ref.shape[2]
    blocks = hidden // deep
    row, high, core = lax.axis_index("row"), lax.axis_index("high"), lax.axis_index("core")
    section = lax.axis_index("section")
    sharing = Group(group)
    sequence = lax.div(sharing.place, group)
    front = Front(w, vectors, shift, x, q, kv, mixed, mask, x1, x1_bf, acc)

    w[row, high, core, 0 : 3 * narrow] = qkv_ref[0].reshape(3 * narrow, deep).astype(BF16)
    w[row, high, core, 3 * narrow : 4 * narrow] = out_ref[0].astype(BF16)
    for i in range(blocks):
        at = slice(i * deep, (i + 1) * deep)
        for j, ref in enumerate((unit_ref, down_ref)):
            first = (UNIT + j * blocks + i) * narrow
            w[row, high, core, first : first + narrow] = ref[0, :, at].astype(BF16)
    small[row, high, core] = small_ref[...]

    def goes(j):
        place = ((j // group) * CORES + core) * group + j % group
        return lax.div(place, CORES), lax.rem(place, CORES)

    source_core = lax.rem(sequence, CORES)
    mine_too = source_core == core

    def block_of(ref, j):
        m, rest = divmod(j // group, seq_here)
        return ref.at[m, :, pl.ds(rest * seq_len + (j % group) * tokens, tokens)]

    def send_block(ref, j):
        there_row, there_core = goes(j)
        return pltpu.make_async_remote_copy(
            block_of(ref, j), turned.at[row], sem_x.at[j, 0], sem_x.at[row, 1],
            device_id={"row": there_row, "core": there_core}, device_id_type=MESH,
        )

    def is_here(j):
        there_row, there_core = goes(j)
        return (there_row == row) & (there_core == core)

    barrier = pltpu.get_barrier_semaphore()
    count = 0
    for line in (Spread("row", rows), Spread("high", highs)):
        for right, there in ((True, line.here < line.size - 1), (False, line.here > 0)):

            @pl.when(there)
            def _(line=line, right=right):
                pl.semaphore_signal(barrier, 1, device_id=line.neighbour(right), device_id_type=MESH)

            count = count + there.astype(jnp.int32)
    others = [{"core": 1 - core}, {"section": 1 - section}] + sharing.members()
    for other in others:
        pl.semaphore_signal(barrier, 1, device_id=other, device_id_type=MESH)
    for r in range(rows):

        @pl.when(jnp.logical_not(mine_too & (row == r)))
        def _(r=r):
            pl.semaphore_signal(barrier, 1, device_id={"row": r, "core": source_core}, device_id_type=MESH)

    pl.semaphore_wait(barrier, count + len(others) + rows - mine_too.astype(jnp.int32))

    row_first = [True] * (4 + 2 * blocks)
    for i in (4, 4 + blocks):
        row_first[i] = False
    order = [0, 1, 2, 3] + [UNIT + j * blocks + i for i in range(blocks) for j in range(2)]
    pieces = [(small, 0, small.shape[3], True)]
    pieces += [(w, i * narrow, narrow, row_first[n]) for n, i in enumerate(order)]
    gather = Gather(pieces, (sem_row, sem_high, sem_core), highs, rows)

    def to_hbm(q):
        at = pl.ds(order[q - 1] * narrow, narrow)
        return pltpu.make_async_copy(w.at[:, :, :, at], w_hbm.at[:, :, :, at], sem_w.at[q])

    keys = share_keys(sharing, kv, sem_kv)

    def begin():
        for j in range(rows):
            for which, ref in ((0, tokens_hbm), (1, cot_hbm)):

                @pl.when((section == which) & is_here(j))
                def _(ref=ref, j=j):
                    pltpu.make_async_copy(block_of(ref, j), turned.at[row], sem_x.at[row, 1]).start()

                @pl.when((section == which) & jnp.logical_not(is_here(j)))
                def _(ref=ref, j=j):
                    send_block(ref, j).start()

    def use_small():
        for r in range(rows):
            vectors[:, r * narrow : (r + 1) * narrow] = small[r, 0, 0, 0:8, 0:narrow]
        for k in range(cols):
            for i in range(blocks):
                at = k * hidden + i * deep
                shift[:, at : at + deep] = small[0, k // CORES, k % CORES, 8 + i : 9 + i]
        lines = tokens // deep
        for slot in range(group):
            part = lax.rem(sharing.position + group - slot, group)
            base = 8 + blocks + (lax.div(sequence, CORES) * group + part) * lines
            doc = jnp.concatenate([small[row, high, source_core, pl.ds(base + i, 1)] for i in range(lines)], axis=1)
            if slot == 0:
                doc_q[...] = doc
            doc_k[slot * tokens : (slot + 1) * tokens] = jnp.broadcast_to(doc, (128, tokens)).T[:, :1]
        mask[...] = jnp.where(doc_k[...] == doc_q[...], 0.0, NEG_BIG)

    def turn():
        for r in range(rows):
            pltpu.make_async_copy(turned.at[r], turned.at[r], sem_x.at[r, 1]).wait()
        for r in range(rows):
            x[:, r * narrow : (r + 1) * narrow] = turned[r].T
        start_ref[...] = x[...]

    half = max(1, cols // 2)
    chunks = min(4, tokens // 8)
    chunk = tokens // chunks

    def send_out(i):
        at = pl.ds(i * chunk, chunk)
        return pltpu.make_async_remote_copy(
            y.at[at], next_hbm.at[at], sem_y.at[i, 0], sem_y.at[i, 1],
            device_id={"section": 1 - section}, device_id_type=MESH,
        )

    stay = pltpu.make_async_copy(x, next_hbm, sem_next.at[0])
    base = 3

    def between(tick, done):
        if done >= 1:
            to_hbm(done).start()
        if done == 0:
            use_small()
        if done == 1:
            turn()

            @pl.when(section == 0)
            def _():
                stay.start()

            front.project(0)
        if done == 2:
            front.project(1)
        if done == base:
            front.project(2)
            for copy in keys:
                copy.start()
        if done == base + 1:
            for copy in keys:
                copy.wait()
        if base + 1 <= done < base + 5:
            front.attend((done - base - 1) * (front.pairs // 4), front.pairs // 4)
        if done == base + 5:
            front.out()
            front.norm_one()
        if done >= base + 5:
            first = done == base + 5
            ready = (done - 4) // 2
            from_block = 0 if first else (done - 1 - 4) // 2
            for block in range(from_block, min(ready, blocks)):
                if block < blocks - 1:
                    for k in range(0, cols, half):
                        front.feed(block, range(k, k + half), block == 0 and k == 0)

    begin()
    gather.run(between)
    for i in range(chunks):
        at = pl.ds(i * chunk, chunk)
        for k in range(0, cols, half):
            front.feed(blocks - 1, range(k, k + half), blocks == 1 and k == 0, at=at)
        y[at] = front.norm_two(at).astype(BF16)

        @pl.when(section == 0)
        def _(i=i):
            send_out(i).start()

    gather.finish()
    for j in range(rows):

        @pl.when(jnp.logical_not(is_here(j)))
        def _(j=j):
            send_block(tokens_hbm, j).wait_send()

    for q in range(1, len(pieces)):
        to_hbm(q).wait()

    @pl.when(section == 0)
    def _():
        stay.wait()
        for i in range(chunks):
            send_out(i).wait_send()

    @pl.when(section == 1)
    def _():
        for i in range(chunks):
            send_out(i).wait_recv()


def first_forward(small, tokens_in, cotangent, qkv, out, unit, down, rows, highs, group, seq_here, seq_len):
    micro, narrow, _ = tokens_in.shape
    deep, hidden = out.shape[2], unit.shape[2]
    width, cols, blocks = narrow * rows, highs * CORES, hidden // deep
    tokens = seq_len // group
    tall = (4 + 2 * blocks) * narrow
    apart = (rows, highs, CORES)
    in_any = pl.BlockSpec(memory_space=pl.ANY)
    in_vmem = pl.BlockSpec(memory_space=pltpu.VMEM)
    count = 1 + 4 + 2 * blocks
    dma = pltpu.SemaphoreType.DMA
    flat, flat_f32 = pltpu.VMEM((tokens, width), BF16), pltpu.VMEM((tokens, width), F32)
    return pl.pallas_call(
        functools.partial(
            first_kernel, highs=highs, rows=rows, group=group, micro=micro, seq_here=seq_here, seq_len=seq_len
        ),
        in_specs=[in_vmem, in_any, in_any] + [in_vmem] * 4,
        out_specs=[in_any, in_vmem, in_any] + [in_vmem] * 4,
        out_shape=[
            shaped((tokens, width), BF16),
            shaped((tokens, width), BF16),
            shaped(apart + (tall, deep), BF16),
            shaped((8, width), F32),
            shaped((1, hidden * cols), F32),
            shaped((1, tokens), F32),
            shaped((group * tokens, 1), F32),
        ],
        scratch_shapes=[
            pltpu.VMEM(apart + (tall, deep), BF16),
            pltpu.VMEM(apart + small.shape, F32),
            pltpu.VMEM((rows, narrow, tokens), BF16),
            flat,
            flat,
            pltpu.VMEM((group, 2, tokens, width), BF16),
            flat,
            pltpu.VMEM((group * tokens, tokens), F32),
            flat_f32,
            flat,
            flat_f32,
            flat,
            dma((count, rows - 1, 2, 2)),
            dma((count, highs - 1, 2, 2)),
            dma((count, 2)),
            dma((rows, 2)),
            dma((max(1, group - 1), 2)),
            dma((4, 2)),
            dma((count,)),
            dma((1,)),
        ],
        name="first_forward",
        compiler_params=pltpu.CompilerParams(collective_id=2, has_side_effects=True, vmem_limit_bytes=LOW_VMEM),
        cost_estimate=pl.CostEstimate(
            flops=24 * tokens * width * width, bytes_accessed=2 * tall * deep * rows * cols, transcendentals=0
        ),
    )(small, tokens_in, cotangent, qkv, out, unit, down)


def local(tokens_in, doc_ids, cotangent, qkv_master, out_master, unit_master, down_master, unit_bias, width_bias, norm_gain):
    at = Layout(tokens_in, doc_ids)
    section = lax.axis_index("section")
    rows, cols, width, narrow = at.rows, at.cols, at.width, at.narrow
    deep, hidden = out_master.shape[2], unit_master.shape[2]

    vectors = jnp.concatenate([width_bias[0], norm_gain[0]])
    vectors = jnp.pad(vectors, ((0, 0), (0, deep - narrow)))
    small = jnp.concatenate([vectors, unit_bias.reshape(-1, deep), doc_ids.astype(F32).reshape(-1, deep)])
    small = jnp.pad(small, ((0, -small.shape[0] % 8), (0, 0)))
    second_in, start, weights, vectors, unit_shift, doc_query, doc_key = first_forward(
        small, tokens_in, cotangent, qkv_master, out_master, unit_master, down_master, rows, cols // CORES, at.group,
        at.seq_here, at.seq_len,
    )
    weights = weights.reshape(rows, cols, -1, deep)
    bias, gain = vectors[:6], vectors[6:]
    kv_bias = jnp.stack([jnp.zeros_like(bias[1]), bias[1]])[:, None]

    def forward(layer_in, saving):
        kv = project(layer_in, weights, kv_bias, 1, 2, 1.0)
        shared = at.share(kv)
        query = project(layer_in, weights, bias[0:1][None], 0, 1, HD**-0.5)
        mixed, log_total = attend(query, shared, doc_query, doc_key)
        x1, x1_bf, hat_one, scale_one = out_norm(mixed, weights, layer_in, bias, gain)
        y, *rest = feed(x1_bf, weights, unit_shift, x1, bias, gain, saving)
        return y, (layer_in, query, shared, mixed, log_total, x1_bf, hat_one, scale_one, *rest)

    def backward(dy, saved, weights_too):
        layer_in, query, shared, mixed, log_total, x1_bf, hat_one, scale_one, act, slope, hat_two, scale_two = saved
        dh2, ddown, *top = top_back(dy, hat_two, scale_two, gain, weights_too)
        dattn, *fed = feed_back(dh2, ddown, hat_one, scale_one, slope, weights, gain, weights_too)
        if not weights_too:
            dmixed = mixed_back(dattn, weights)
            dq, dkv = attend_back(query, dmixed, mixed, log_total, shared, doc_query, doc_key)
            others = at.give_back([dkv[j] for j in range(at.group)])
            return input_back(dq, dkv, others, weights, dattn)
        (top_sums,), (dpre, pre_sum, feed_sums) = top, fed
        sums = jnp.concatenate([feed_sums[:2], top_sums[:2], feed_sums[2:3], top_sums[2:3]])
        return low_back(
            ddown, act, x1_bf, dpre, dattn, query, mixed, log_total, layer_in, weights, shared, doc_query, doc_key,
            pre_sum, sums,
        )

    layer_out, saved = forward(second_in, True)
    early_grad = backward(start, saved, False)
    passed = lax.ppermute(early_grad, "section", [(1, 0)])
    input_grad, total = backward(jnp.where(section == 0, passed, start), saved, True)

    def whole_columns(grad):
        return grad.reshape(-1, narrow, deep).transpose(1, 0, 2).reshape(narrow, hidden)

    feed_rows = narrow * hidden // deep
    heights = (feed_rows, narrow, feed_rows, 3 * narrow, 16)
    ends = [0]
    for height in heights:
        ends.append(ends[-1] + height)
    down_sum, out_sum, unit_sum, qkv_sum, sums = (total[a:b] for a, b in zip(ends, ends[1:]))
    vectors, pre_sum = sums[:8, :narrow], sums[8 : 8 + hidden // deep].reshape(-1)
    layer_out = at.to_features(layer_out).astype(F32)
    input_grad = at.to_features(input_grad).astype(F32)
    return (
        layer_out[None],
        input_grad[None],
        qkv_sum.reshape(qkv_master.shape),
        out_sum[None],
        whole_columns(unit_sum)[None],
        whole_columns(down_sum)[None],
        pre_sum[None],
        vectors[:6][None],
        vectors[6:][None],
    )


def solution(mesh):
    sections, rows, cols = (mesh.shape[name] for name in ("section", "row", "col"))
    fine = Mesh(
        mesh.devices.reshape(sections, rows, cols // CORES, CORES), ("section", "row", "high", "core")
    )
    col = ("high", "core")
    block = P("section", "row", col)
    stream = P("section", None, "row", col)
    return jax.shard_map(
        local,
        mesh=fine,
        in_specs=(
            P(None, "row", col),
            P(None, col, None),
            P(None, "row", col),
            P("section", None, "row", col),
            block,
            block,
            block,
            P("section", col),
            P("section", None, "row"),
            P("section", None, "row"),
        ),
        out_specs=(
            stream,
            stream,
            stream,
            block,
            block,
            block,
            P("section", col),
            P("section", None, "row"),
            P("section", None, "row"),
        ),
        check_vma=False,
    )
```

```python
import functools

import jax
import jax.numpy as jnp
from jax import lax
from jax.experimental import pallas as pl
from jax.experimental.pallas import tpu as pltpu
from jax.sharding import Mesh
from jax.sharding import PartitionSpec as P

HD = 64
EPSILON = 1e-05
NEG_BIG = -1e30
CORES = 2
PAIR = 128
PLANE = ("row", "high", "core")
MESH = pl.DeviceIdType.MESH

QKV, OUT, UNIT = 0, 3, 4
FEED_BLOCKS = 2

F32 = jnp.float32
BF16 = jnp.bfloat16
VMEM_BYTES = 56 * 1024 * 1024
LOW_VMEM = 63 * 1024 * 1024


def nn(left, right):
    return lax.dot_general(left, right, (((1,), (0,)), ((), ())), preferred_element_type=F32)


def nt(left, right):
    return lax.dot_general(left, right, (((1,), (1,)), ((), ())), preferred_element_type=F32)


def held(shape):
    return pl.BlockSpec(shape, lambda *_: (0,) * len(shape), pipeline_mode=pl.Buffered(1))


def call(kernel, grid, in_specs, out_specs, out_shape, scratch, name, flops, moved, args):
    return pl.pallas_call(
        kernel,
        grid=grid,
        in_specs=in_specs,
        out_specs=out_specs,
        out_shape=out_shape,
        scratch_shapes=scratch,
        name=name,
        compiler_params=pltpu.CompilerParams(
            vmem_limit_bytes=VMEM_BYTES, dimension_semantics=("arbitrary",) * len(grid)
        ),
        cost_estimate=pl.CostEstimate(flops=flops, bytes_accessed=moved, transcendentals=0),
    )(*args)


def shaped(shape, dtype):
    return jax.ShapeDtypeStruct(shape, dtype)


def row_blocks(rows, narrow):
    take = min(rows, max(1, 256 // narrow))
    while rows % take:
        take += 1
    return take


def side_by_side(blocks):
    take, cols, narrow, deep = blocks.shape
    return jnp.concatenate([blocks[:, k].reshape(take * narrow, deep) for k in range(cols)], axis=1)


def head_lanes(shape, axis):
    return lax.broadcasted_iota(jnp.int32, shape, axis) < HD


def pair_front(query, keys, values, bias_ref):
    values_t = values.T
    lanes = head_lanes(query.shape, 1)
    outs, log_rows = [], []
    for h in range(2):
        mine = jnp.where(lanes if h == 0 else ~lanes, query, 0)
        scores = nt(keys, mine) + bias_ref[...]
        top = jnp.max(scores, axis=0, keepdims=True)
        expo = jnp.exp(scores - top)
        total = jnp.sum(expo, axis=0, keepdims=True)
        outs.append(nn(values_t, expo.astype(BF16)) / total)
        log_rows.append(top + jnp.log(total))
    mixed_t = jnp.where(head_lanes(outs[0].shape, 0), outs[0], outs[1])
    return mixed_t.T.astype(BF16), log_rows


def pair_back(query, grad, mixed, log_rows, keys, values, bias_ref, tile):
    tokens = query.shape[0]
    keys_t = keys.T
    lanes = head_lanes((tile, PAIR), 1)
    low_t = head_lanes(keys_t.shape, 0)
    products = (grad.astype(F32) * mixed.astype(F32)).T
    grad_query = []
    grad_key = jnp.zeros(keys.shape, F32)
    grad_value = jnp.zeros(keys.shape, F32)
    for at in range(0, tokens, tile):
        some = slice(at, at + tile)
        grad_some = jnp.zeros((PAIR, tile), F32)
        for h in range(2):
            here = lanes if h == 0 else ~lanes
            mine = jnp.where(here, query[some], 0)
            grad_mine = jnp.where(here, grad[some], 0)
            inner = jnp.sum(products[h * HD : (h + 1) * HD, some], axis=0, keepdims=True)
            prob = jnp.exp(nt(keys, mine) + bias_ref[:, some] - log_rows[h][:, some])
            grad_value += nn(prob.astype(BF16), grad_mine)
            grad_scores = (prob * (nt(values, grad_mine) - inner)).astype(BF16)
            grad_key += nn(grad_scores, mine)
            keys_mine = jnp.where(low_t if h == 0 else ~low_t, keys_t, 0)
            grad_some += nn(keys_mine, grad_scores)
        grad_query.append(grad_some)
    grad_query = jnp.concatenate(grad_query, axis=1).T.astype(BF16) * HD**-0.5
    return grad_query, grad_key.astype(BF16), grad_value.astype(BF16)


def normed_of(hidden):
    center = hidden - jnp.mean(hidden, axis=1, keepdims=True)
    scale = lax.rsqrt(jnp.mean(center * center, axis=1, keepdims=True) + EPSILON)
    return center * scale, scale


def norm_back(grad_out, normed, scale, gain):
    scaled = grad_out * gain
    first = jnp.mean(scaled, axis=1, keepdims=True)
    second = jnp.mean(scaled * normed, axis=1, keepdims=True)
    return scale * (scaled - first - normed * second)


SLICE = 128


def by_tokens(tokens, body):
    step = min(SLICE, tokens)
    for at in range(0, tokens, step):
        body(pl.ds(at, step))


def gelu_parts(pre):
    below = 0.5 * (1.0 + lax.erf(pre * 0.5**0.5))
    return pre * below, below + pre * jnp.exp(-0.5 * pre * pre) * (2.0 * jnp.pi) ** -0.5


def hidden_columns(block, width):
    rows, _, tall, deep = block.shape
    narrow = width // rows
    parts = [block[:, 0, i * narrow : (i + 1) * narrow].reshape(width, deep) for i in range(FEED_BLOCKS)]
    return jnp.concatenate(parts, axis=1)


def feed_specs(weight, tokens, width, units):
    rows, cols, _, deep = weight.shape
    tall = FEED_BLOCKS * (width // rows)
    block = FEED_BLOCKS * deep
    per = units // cols // block

    def at(first):
        return pl.BlockSpec((rows, 1, tall, deep), lambda s: (0, s // per, first // FEED_BLOCKS + s % per, 0))

    wide = pl.BlockSpec((tokens, block), lambda s: (0, s))
    line = pl.BlockSpec((1, block), lambda s: (0, s))
    return cols * per, at(UNIT), at(UNIT + per * FEED_BLOCKS), wide, line


def column_sum(value):
    return jnp.sum(value, axis=0, keepdims=True)


def top_back_kernel(dy_ref, hat_ref, scale_ref, n_ref, dh2_ref, ddown_ref, *sums_ref):
    for ref in sums_ref:
        ref[...] = jnp.zeros_like(ref)

    def some(at):
        dy, hat = dy_ref[at].astype(F32), hat_ref[at]
        dh2 = norm_back(dy, hat, scale_ref[at][:, :1], n_ref[1:2])
        dh2_ref[at] = dh2
        ddown = dh2.astype(BF16)
        ddown_ref[at] = ddown
        for ref in sums_ref:
            ref[0:1] += column_sum(ddown.astype(F32))
            ref[1:2] += column_sum(dy)
            ref[2:3] += column_sum(dy * hat)

    by_tokens(dy_ref.shape[0], some)


def top_back(dy, hat2, scale2, gain, sums_too):
    tokens, width = hat2.shape
    flat = held((tokens, width))
    return call(
        top_back_kernel,
        (1,),
        [flat, flat, held((tokens, 128)), held(gain.shape)],
        [flat, flat] + [held((8, width))] * sums_too,
        [shaped((tokens, width), F32), shaped((tokens, width), BF16)] + [shaped((8, width), F32)] * sums_too,
        [],
        "top_back",
        20 * tokens * width,
        12 * tokens * width,
        (dy, hat2, scale2, gain),
    )


def feed_back_kernel(*refs, steps, sums_too):
    dh2_ref, ddown_ref, hat1_ref, scale1_ref, slope_ref, wu_ref, wd_ref, n_ref, dattn_ref = refs[:9]
    acc_ref = refs[-1]
    s = pl.program_id(0)
    tokens, width = dh2_ref.shape
    dact = nn(ddown_ref[...], hidden_columns(wd_ref[...], width))
    dpre = (dact * slope_ref[...].astype(F32)).astype(BF16)
    back = nt(dpre, hidden_columns(wu_ref[...], width))
    if sums_too:
        dpre_ref, pre_ref, sums_ref = refs[9:12]
        dpre_ref[...] = dpre
        pre_ref[...] = column_sum(dpre.astype(F32))

    @pl.when(s == 0)
    def _():
        acc_ref[...] = back

    @pl.when(s > 0)
    def _():
        acc_ref[...] += back

    @pl.when(s == steps - 1)
    def _():
        if sums_too:
            sums_ref[...] = jnp.zeros_like(sums_ref)

        def some(at):
            dx1, hat = dh2_ref[at] + acc_ref[at], hat1_ref[at]
            dattn = norm_back(dx1, hat, scale1_ref[at][:, :1], n_ref[0:1]).astype(BF16)
            dattn_ref[at] = dattn
            if sums_too:
                sums_ref[0:1] += column_sum(dattn.astype(F32))
                sums_ref[1:2] += column_sum(dx1)
                sums_ref[2:3] += column_sum(dx1 * hat)

        by_tokens(tokens, some)


def feed_back(dh2, ddown, hat1, scale1, slope, weight, gain, sums_too):
    tokens, width = dh2.shape
    units = slope.shape[1]
    steps, first, second, wide, line = feed_specs(weight, tokens, width, units)
    flat = held((tokens, width))
    out_specs, out_shape = [flat], [shaped((tokens, width), BF16)]
    if sums_too:
        out_specs += [wide, line, held((8, width))]
        out_shape += [shaped((tokens, units), BF16), shaped((1, units), F32), shaped((8, width), F32)]
    return call(
        functools.partial(feed_back_kernel, steps=steps, sums_too=sums_too),
        (steps,),
        [flat, flat, flat, held((tokens, 128)), wide, first, second, held(gain.shape)],
        out_specs,
        out_shape,
        [pltpu.VMEM((tokens, width), F32)],
        "feed_back",
        4 * tokens * width * units,
        4 * width * units,
        (dh2, ddown, hat1, scale1, slope, weight, weight, gain),
    )


class Layout:
    def __init__(self, tokens_in, doc_ids):
        self.micro, self.narrow, _ = tokens_in.shape
        self.seq_here, self.seq_len = doc_ids.shape[1:]
        self.rows = lax.axis_size("row")
        self.cols = lax.axis_size("high") * CORES
        self.width = self.narrow * self.rows
        self.places = self.rows * CORES
        self.sequences = self.micro * self.seq_here * CORES
        self.group = self.places // self.sequences
        self.part = self.seq_len // self.group
        self.row = lax.axis_index("row")
        place = self.row * CORES + lax.axis_index("core")
        self.sequence = place // self.group
        self.position = place % self.group
        self.block = (self.sequence // CORES) * self.group + self.position


class Line:
    def __init__(self, axis, size):
        self.axis, self.size, self.here = axis, size, lax.axis_index(axis)

    def sends(self, step):
        last = self.size - 1
        return (
            (True, (self.here < step) & (self.here < last), self.size - step + self.here, self.here > 0),
            (False, (last - self.here < step) & (self.here > 0), step - self.size + self.here, self.here < last),
        )

    def gets(self, step):
        last = self.size - 1
        return (
            (True, (self.here >= 1) & (self.here <= step)),
            (False, (last - self.here >= 1) & (last - self.here <= step)),
        )

    def neighbour(self, right):
        return {self.axis: self.here + (1 if right else -1)}


def greet(lines, pairs, members=(), some=()):
    barrier = pltpu.get_barrier_semaphore()
    count = 0
    for line in lines:
        for right, there in ((True, line.here < line.size - 1), (False, line.here > 0)):

            @pl.when(there)
            def _(line=line, right=right):
                pl.semaphore_signal(barrier, 1, device_id=line.neighbour(right), device_id_type=MESH)

            count = count + there.astype(jnp.int32)
    for axis in pairs:
        pl.semaphore_signal(barrier, 1, device_id={axis: 1 - lax.axis_index(axis)}, device_id_type=MESH)
        count = count + 1
    for member in members:
        pl.semaphore_signal(barrier, 1, device_id=member, device_id_type=MESH)
        count = count + 1
    for member, there in some:

        @pl.when(there)
        def _(member=member):
            pl.semaphore_signal(barrier, 1, device_id=member, device_id_type=MESH)

        count = count + there.astype(jnp.int32)
    pl.semaphore_wait(barrier, count)


def add_into(target, other):
    lead = target.shape[:-2]
    rows = target.shape[-2]
    total = 1
    for size in lead:
        total *= size
    if total == 1:
        target[...] = target[...] + other[...]
        return

    @pl.loop(0, total)
    def _(i):
        index = []
        for size in reversed(lead):
            index.insert(0, lax.rem(i, size))
            i = lax.div(i, size)
        index = tuple(index)
        target[index] = target[index] + other[index]


class Scatter:
    def __init__(self, pieces, refs, highs, rows, give):
        self.pieces, self.give = pieces, give
        (self.landing, self.work, self.got, self.from_high, self.got_high, self.from_row, self.from_wide, *sems) = refs
        self.sem_core, self.sem_load, self.sem_high, self.sem_row = sems
        self.high, self.row = Line("high", highs), Line("row", rows)
        self.core = lax.axis_index("core")
        self.slots = self.work.shape[0]
        self.sent = [[] for _ in pieces]
        self.place, wide, thin = [], 0, 0
        for _, _, row_last in pieces:
            self.place.append(thin if row_last else wide)
            thin, wide = thin + row_last, wide + (not row_last)

    def slot(self, q):
        return q % self.slots

    def cut(self, q, ref):
        return ref.at[..., pl.ds(0, self.pieces[q][1]), :]

    def to_core(self, q, y):
        return pltpu.make_async_remote_copy(
            self.pieces[q][0].at[:, y, 1 - self.core],
            self.cut(q, self.landing.at[q, y]),
            self.sem_core.at[q, y, 0],
            self.sem_core.at[q, y, 1],
            device_id={"core": 1 - self.core},
            device_id_type=MESH,
        )

    def load(self, q, y):
        return pltpu.make_async_copy(
            self.pieces[q][0].at[:, y, self.core],
            self.cut(q, self.work.at[self.slot(q), y]),
            self.sem_load.at[q, y, 0],
        )

    def fetch(self, q, y):
        return pltpu.make_async_copy(
            self.cut(q, self.landing.at[q, y]), self.cut(q, self.got.at[q % 2, y]), self.sem_load.at[q, y, 1]
        )

    def begin(self, q):
        if q >= self.slots:
            self.finish_sends(q - self.slots)
        for y in range(self.high.size):
            self.to_core(q, y).start()
            self.load(q, y).start()

    def arrive(self, q):
        for y in range(self.high.size):
            self.to_core(q, y).wait()
            self.fetch(q, y).start()

    def merge(self, q):
        for y in range(self.high.size):
            self.load(q, y).wait()
            self.fetch(q, y).wait()
            add_into(self.cut(q, self.work.at[self.slot(q), y]), self.cut(q, self.got.at[q % 2, y]))

    def lines(self, q):
        return (self.high, self.row) if self.pieces[q][2] else (self.row, self.high)

    def block(self, q, line, i):
        first = line is self.lines(q)[0]
        if line is self.high:
            ref = self.work.at[self.slot(q), i, slice(None) if first else self.row.here]
        else:
            ref = self.work.at[self.slot(q), slice(None) if first else self.high.here, i]
        return self.cut(q, ref)

    def arrival(self, q, line, step, right):
        way = 0 if line.size == 2 or right else 1
        first = line is self.lines(q)[0]
        if line is self.high:
            index = (slice(None),) if first else (0,)
            return (
                self.cut(q, self.from_high.at[(q, step - 1, way) + index]),
                self.cut(q, self.got_high.at[(q % 2, way) + index]),
            )
        ref = (self.from_wide if first else self.from_row).at[self.place[q], step - 1, way]
        return (self.cut(q, ref),) * 2

    def copy(self, q, line, step, right, i):
        sems = (self.sem_high if line is self.high else self.sem_row).at[q, step - 1, 0 if right else 1]
        return pltpu.make_async_remote_copy(
            self.block(q, line, i),
            self.arrival(q, line, step, right)[0],
            sems.at[0],
            sems.at[1],
            device_id=line.neighbour(right),
            device_id_type=MESH,
        )

    def push(self, q, line, step):
        for right, there, i, more in line.sends(step):

            @pl.when(there)
            def _(right=right, i=i, more=more):
                if step > 1:

                    @pl.when(more)
                    def _():
                        add_into(self.block(q, line, i), self.arrival(q, line, step - 1, right)[1])

                self.copy(q, line, step, right, i).start()

            self.sent[q].append((line, step, right, there, i))

    def pull(self, q, line, step):
        for right, there in line.gets(step):

            @pl.when(there)
            def _(right=right):
                self.copy(q, line, step, right, 0).wait_recv()
                if line is self.high:
                    landed, got = self.arrival(q, line, step, right)
                    way = 0 if line.size == 2 or right else 1
                    fetch = pltpu.make_async_copy(landed, got, self.sem_high.at[q, step - 1, way, 2])
                    fetch.start()
                    fetch.wait()

    def close(self, q, line):
        for right, there in line.gets(line.size - 1):

            @pl.when(there)
            def _(right=right):
                add_into(self.block(q, line, line.here), self.arrival(q, line, line.size - 1, right)[1])

    def finish_sends(self, q):
        for line, step, right, there, i in self.sent[q]:

            @pl.when(there)
            def _(line=line, step=step, right=right, i=i):
                self.copy(q, line, step, right, i).wait_send()

        self.sent[q] = []

    def stages(self, q):
        lines = [(line, step) for line in self.lines(q) for step in range(1, line.size)]

        def merge():
            self.merge(q)
            self.push(q, *lines[0])

        stages = [lambda: self.begin(q), lambda: self.arrive(q), merge]
        for n, (line, step) in enumerate(lines):

            def one(n=n, line=line, step=step):
                self.pull(q, line, step)
                if step == line.size - 1:
                    self.close(q, line)
                if n + 1 < len(lines):
                    self.push(q, *lines[n + 1])
                else:
                    self.give(q, self.block(q, line, line.here))

            if line is self.high and step == 1:
                stages.append(lambda: None)
            stages.append(one)
        return stages

    def run(self, between):
        stages = [self.stages(q) for q in range(len(self.pieces))]
        depth, count = len(stages[0]), len(stages)
        for tick in range(count + depth - 1):
            for q in range(max(0, tick - depth + 1), min(tick + 1, count)):
                stages[q][tick - q]()
            between(tick)
        for q in range(count):
            self.finish_sends(q)


class Spread:
    def __init__(self, axis, size):
        self.axis, self.size, self.here = axis, size, lax.axis_index(axis)

    def sends(self, step):
        last = self.size - 1
        return (
            (True, (self.here < last) & (self.here >= step - 1), self.here - step + 1),
            (False, (self.here > 0) & (self.here + step - 1 <= last), self.here + step - 1),
        )

    def gets(self, step):
        last = self.size - 1
        return ((True, self.here >= step), (False, self.here + step <= last))

    def neighbour(self, right):
        return {self.axis: self.here + (1 if right else -1)}


class Gather:
    def __init__(self, pieces, sems, highs, rows):
        self.pieces = pieces
        self.sem_row, self.sem_high, self.sem_core = sems
        self.row, self.high = Spread("row", rows), Spread("high", highs)
        self.core = lax.axis_index("core")
        self.sent = []

    def block(self, q, line, i):
        ref, first, count, row_first = self.pieces[q]
        some = pl.ds(first, count)
        if line is self.row:
            return ref.at[i, self.high.here if row_first else slice(None), self.core, some]
        return ref.at[slice(None) if row_first else self.row.here, i, self.core, some]

    def copy(self, q, line, step, right, i):
        sems = (self.sem_row if line is self.row else self.sem_high).at[q, step - 1, 0 if right else 1]
        ref = self.block(q, line, i)
        return pltpu.make_async_remote_copy(
            ref, ref, sems.at[0], sems.at[1], device_id=line.neighbour(right), device_id_type=MESH
        )

    def push(self, q, line, step):
        for right, there, i in line.sends(step):

            @pl.when(there)
            def _(right=right, i=i):
                self.copy(q, line, step, right, i).start()

            self.sent.append((q, line, step, right, there, i))

    def pull(self, q, line, step):
        for right, there in line.gets(step):

            @pl.when(there)
            def _(right=right):
                self.copy(q, line, step, right, line.here).wait_recv()

    def to_core(self, q):
        ref, first, count, _ = self.pieces[q]
        ref = ref.at[:, :, self.core, pl.ds(first, count)]
        return pltpu.make_async_remote_copy(
            ref, ref, self.sem_core.at[q, 0], self.sem_core.at[q, 1],
            device_id={"core": 1 - self.core}, device_id_type=MESH,
        )

    def stages(self, q):
        first, second = (self.row, self.high) if self.pieces[q][3] else (self.high, self.row)
        steps = [lambda: self.push(q, first, 1)]
        lines = [(first, i) for i in range(1, first.size)] + [(second, i) for i in range(1, second.size)]
        for n, (line, step) in enumerate(lines):

            def one(n=n, line=line, step=step):
                self.pull(q, line, step)
                if n + 1 < len(lines):
                    self.push(q, *lines[n + 1])
                else:
                    self.to_core(q).start()

            steps.append(lambda: None)
            steps.append(one)
        steps.append(lambda: self.to_core(q).wait())
        return steps

    def run(self, between):
        stages = [self.stages(q) for q in range(len(self.pieces))]
        depth, count = len(stages[0]), len(stages)
        for tick in range(count + depth - 1):
            for q in range(max(0, tick - depth + 1), min(tick + 1, count)):
                stages[q][tick - q]()
            between(tick, tick - depth + 1)

    def finish(self):
        for q, line, step, right, there, i in self.sent:

            @pl.when(there)
            def _(q=q, line=line, step=step, right=right, i=i):
                self.copy(q, line, step, right, i).wait_send()


class Group:
    def __init__(self, size):
        self.size = size
        self.place = lax.axis_index("row") * CORES + lax.axis_index("core")
        self.position = lax.rem(self.place, size)

    def member(self, step):
        other = self.place - self.position + lax.rem(self.position + step, self.size)
        return {"row": lax.div(other, CORES), "core": lax.rem(other, CORES)}

    def members(self):
        return [self.member(step) for step in range(1, self.size)]


class Front:
    def __init__(self, w, vectors, shift, x, q, kv, mixed, mask, x1, x1_bf, acc, log=None):
        self.w, self.vectors, self.shift, self.x, self.q, self.kv = w, vectors, shift, x, q, kv
        self.mixed, self.mask, self.x1, self.x1_bf, self.acc, self.log = mixed, mask, x1, x1_bf, acc, log
        self.tokens, self.width = x.shape
        self.rows, self.highs, _, _, self.deep = w.shape
        self.cols = self.highs * CORES
        self.narrow = self.width // self.rows
        self.group = kv.shape[0]
        self.pairs = self.width // PAIR
        self.blocks = shift.shape[1] // self.cols // self.deep

    def matrix(self, block, k):
        at = pl.ds(block * self.narrow, self.narrow)
        return self.w[:, k // CORES, k % CORES, at].reshape(self.width, self.deep)

    def project(self, j):
        take = row_blocks(self.rows, self.narrow)
        for r in range(0, self.rows, take):
            at = slice(r * self.narrow, (r + take) * self.narrow)
            some = pl.ds((QKV + j) * self.narrow, self.narrow)
            weight = jnp.concatenate(
                [
                    self.w[r : r + take, k // CORES, k % CORES, some].reshape(take * self.narrow, self.deep)
                    for k in range(self.cols)
                ],
                axis=1,
            )
            out = nt(self.x[...], weight)
            if j == 0:
                self.q[:, at] = ((out + self.vectors[0:1, at]) * HD**-0.5).astype(BF16)
            elif j == 1:
                self.kv[0, 0, :, at] = out.astype(BF16)
            else:
                self.kv[0, 1, :, at] = (out + self.vectors[1:2, at]).astype(BF16)

    def attend(self, first, count):
        @pl.loop(first, first + count)
        def _(p):
            at = pl.ds(pl.multiple_of(p * PAIR, PAIR), PAIR)
            keys = jnp.concatenate([self.kv[i, 0, :, at] for i in range(self.group)], axis=0)
            values = jnp.concatenate([self.kv[i, 1, :, at] for i in range(self.group)], axis=0)
            mixed, log_rows = pair_front(self.q[:, at], keys, values, self.mask)
            self.mixed[:, at] = mixed
            if self.log is not None:
                for h in range(2):
                    self.log[p, h : h + 1] = log_rows[h]

    def out(self):
        for k in range(self.cols):
            at = slice(k * self.deep, (k + 1) * self.deep)
            self.acc[:, at] = nn(self.mixed[...], self.matrix(OUT, k))

    def norm_one(self, keep=None):
        def some(at):
            attn = self.acc[at] + self.vectors[2:3]
            normed, scale = normed_of(self.x[at].astype(F32) + attn)
            x1 = normed * self.vectors[6:7] + self.vectors[3:4]
            self.x1[at] = x1
            self.x1_bf[at] = x1.astype(BF16)
            if keep is not None:
                keep(at, normed, scale)

        by_tokens(self.tokens, some)

    def feed(self, block, ks, start, keep=None, at=slice(None)):
        up = jnp.concatenate([self.matrix(UNIT + block, k) for k in ks], axis=1)
        down = jnp.concatenate([self.matrix(UNIT + self.blocks + block, k) for k in ks], axis=1)
        hidden = self.blocks * self.deep
        begins = [k * hidden + block * self.deep for k in ks]
        shift = jnp.concatenate([self.shift[:, b : b + self.deep] for b in begins], axis=1)
        act, slope = gelu_parts(nn(self.x1_bf[at], up) + shift)
        act = act.astype(BF16)
        if keep is not None:
            keep(act, slope.astype(BF16))
        more = nt(act, down)
        if start:
            self.acc[at] = more
        else:
            self.acc[at] += more

    def norm_two(self, at, keep=None):
        normed, scale = normed_of(self.x1[at] + (self.acc[at] + self.vectors[4:5]))
        if keep is not None:
            keep(at, normed, scale)
        return normed * self.vectors[7:8] + self.vectors[5:6]


def share_keys(group, kv, sems):
    def copy(step):
        return pltpu.make_async_remote_copy(
            kv.at[0], kv.at[step], sems.at[step - 1, 0], sems.at[step - 1, 1],
            device_id=group.member(step), device_id_type=MESH,
        )

    return [copy(step) for step in range(1, group.size)]


def first_kernel(*refs, highs, rows, group, micro, seq_here, seq_len):
    (small_ref, tokens_hbm, cot_hbm, qkv_ref, out_ref, unit_ref, down_ref) = refs[:7]
    (next_hbm, start_ref, w_hbm, vectors, shift, doc_q, doc_k) = refs[7:14]
    (w, small, turned, x, q, kv, mixed, mask, x1, x1_bf, acc, y,
     sem_row, sem_high, sem_core, sem_x, sem_kv, sem_y, sem_w, sem_next) = refs[14:]
    tokens, width = x.shape
    narrow, deep = width // rows, w.shape[-1]
    cols = highs * CORES
    hidden = unit_ref.shape[2]
    blocks = hidden // deep
    row, high, core = lax.axis_index("row"), lax.axis_index("high"), lax.axis_index("core")
    section = lax.axis_index("section")
    sharing = Group(group)
    sequence = lax.div(sharing.place, group)
    front = Front(w, vectors, shift, x, q, kv, mixed, mask, x1, x1_bf, acc)

    w[row, high, core, 0 : 3 * narrow] = qkv_ref[0].reshape(3 * narrow, deep).astype(BF16)
    w[row, high, core, 3 * narrow : 4 * narrow] = out_ref[0].astype(BF16)
    for i in range(blocks):
        at = slice(i * deep, (i + 1) * deep)
        for j, ref in enumerate((unit_ref, down_ref)):
            first = (UNIT + j * blocks + i) * narrow
            w[row, high, core, first : first + narrow] = ref[0, :, at].astype(BF16)
    small[row, high, core] = small_ref[...]

    def goes(j):
        place = ((j // group) * CORES + core) * group + j % group
        return lax.div(place, CORES), lax.rem(place, CORES)

    source_core = lax.rem(sequence, CORES)
    mine_too = source_core == core

    def block_of(ref, j):
        m, rest = divmod(j // group, seq_here)
        return ref.at[m, :, pl.ds(rest * seq_len + (j % group) * tokens, tokens)]

    def send_block(ref, j):
        there_row, there_core = goes(j)
        return pltpu.make_async_remote_copy(
            block_of(ref, j), turned.at[row], sem_x.at[j, 0], sem_x.at[row, 1],
            device_id={"row": there_row, "core": there_core}, device_id_type=MESH,
        )

    def is_here(j):
        there_row, there_core = goes(j)
        return (there_row == row) & (there_core == core)

    barrier = pltpu.get_barrier_semaphore()
    count = 0
    for line in (Spread("row", rows), Spread("high", highs)):
        for right, there in ((True, line.here < line.size - 1), (False, line.here > 0)):

            @pl.when(there)
            def _(line=line, right=right):
                pl.semaphore_signal(barrier, 1, device_id=line.neighbour(right), device_id_type=MESH)

            count = count + there.astype(jnp.int32)
    others = [{"core": 1 - core}, {"section": 1 - section}] + sharing.members()
    for other in others:
        pl.semaphore_signal(barrier, 1, device_id=other, device_id_type=MESH)
    for r in range(rows):

        @pl.when(jnp.logical_not(mine_too & (row == r)))
        def _(r=r):
            pl.semaphore_signal(barrier, 1, device_id={"row": r, "core": source_core}, device_id_type=MESH)

    pl.semaphore_wait(barrier, count + len(others) + rows - mine_too.astype(jnp.int32))

    row_first = [True] * (4 + 2 * blocks)
    row_first[4 + blocks] = False
    order = [0, 1, 2, 3] + [UNIT + j * blocks + i for i in range(blocks) for j in range(2)]
    pieces = [(small, 0, small.shape[3], True)]
    pieces += [(w, i * narrow, narrow, row_first[n]) for n, i in enumerate(order)]
    gather = Gather(pieces, (sem_row, sem_high, sem_core), highs, rows)

    def to_hbm(q):
        at = pl.ds(order[q - 1] * narrow, narrow)
        return pltpu.make_async_copy(w.at[:, :, :, at], w_hbm.at[:, :, :, at], sem_w.at[q])

    keys = share_keys(sharing, kv, sem_kv)

    def begin():
        for j in range(rows):
            for which, ref in ((0, tokens_hbm), (1, cot_hbm)):

                @pl.when((section == which) & is_here(j))
                def _(ref=ref, j=j):
                    pltpu.make_async_copy(block_of(ref, j), turned.at[row], sem_x.at[row, 1]).start()

                @pl.when((section == which) & jnp.logical_not(is_here(j)))
                def _(ref=ref, j=j):
                    send_block(ref, j).start()

    def use_small():
        for r in range(rows):
            vectors[:, r * narrow : (r + 1) * narrow] = small[r, 0, 0, 0:8, 0:narrow]
        for k in range(cols):
            for i in range(blocks):
                at = k * hidden + i * deep
                shift[:, at : at + deep] = small[0, k // CORES, k % CORES, 8 + i : 9 + i]
        lines = tokens // deep
        for slot in range(group):
            part = lax.rem(sharing.position + group - slot, group)
            base = 8 + blocks + (lax.div(sequence, CORES) * group + part) * lines
            doc = jnp.concatenate([small[row, high, source_core, pl.ds(base + i, 1)] for i in range(lines)], axis=1)
            if slot == 0:
                doc_q[...] = doc
            doc_k[slot * tokens : (slot + 1) * tokens] = jnp.broadcast_to(doc, (128, tokens)).T[:, :1]
        mask[...] = jnp.where(doc_k[...] == doc_q[...], 0.0, NEG_BIG)

    def turn():
        for r in range(rows):
            pltpu.make_async_copy(turned.at[r], turned.at[r], sem_x.at[r, 1]).wait()
        for r in range(rows):
            x[:, r * narrow : (r + 1) * narrow] = turned[r].T
        start_ref[...] = x[...]

    half = max(1, cols // 2)
    chunks = min(4, tokens // 8)
    chunk = tokens // chunks

    def send_out(i):
        at = pl.ds(i * chunk, chunk)
        return pltpu.make_async_remote_copy(
            y.at[at], next_hbm.at[at], sem_y.at[i, 0], sem_y.at[i, 1],
            device_id={"section": 1 - section}, device_id_type=MESH,
        )

    stay = pltpu.make_async_copy(x, next_hbm, sem_next.at[0])
    base = 3

    def between(tick, done):
        if done >= 1:
            to_hbm(done).start()
        if done == 0:
            use_small()
        if done == 1:
            turn()

            @pl.when(section == 0)
            def _():
                stay.start()

            front.project(0)
        if done == 2:
            front.project(1)
        if done == base:
            front.project(2)
            for copy in keys:
                copy.start()
        if done == base + 1:
            for copy in keys:
                copy.wait()
        if base + 1 <= done < base + 5:
            front.attend((done - base - 1) * (front.pairs // 4), front.pairs // 4)
        if done == base + 5:
            front.out()
            front.norm_one()
        if done >= base + 5:
            first = done == base + 5
            ready = (done - 4) // 2
            from_block = 0 if first else (done - 1 - 4) // 2
            for block in range(from_block, min(ready, blocks)):
                if block < blocks - 1:
                    for k in range(0, cols, half):
                        front.feed(block, range(k, k + half), block == 0 and k == 0)

    begin()
    gather.run(between)
    for i in range(chunks):
        at = pl.ds(i * chunk, chunk)
        for k in range(0, cols, half):
            front.feed(blocks - 1, range(k, k + half), blocks == 1 and k == 0, at=at)
        y[at] = front.norm_two(at).astype(BF16)

        @pl.when(section == 0)
        def _(i=i):
            send_out(i).start()

    gather.finish()
    for j in range(rows):

        @pl.when(jnp.logical_not(is_here(j)))
        def _(j=j):
            send_block(tokens_hbm, j).wait_send()

    for q in range(1, len(pieces)):
        to_hbm(q).wait()

    @pl.when(section == 0)
    def _():
        stay.wait()
        for i in range(chunks):
            send_out(i).wait_send()

    @pl.when(section == 1)
    def _():
        for i in range(chunks):
            send_out(i).wait_recv()


def first_forward(small, tokens_in, cotangent, qkv, out, unit, down, rows, highs, group, seq_here, seq_len):
    micro, narrow, _ = tokens_in.shape
    deep, hidden = out.shape[2], unit.shape[2]
    width, cols, blocks = narrow * rows, highs * CORES, hidden // deep
    tokens = seq_len // group
    tall = (4 + 2 * blocks) * narrow
    apart = (rows, highs, CORES)
    in_any = pl.BlockSpec(memory_space=pl.ANY)
    in_vmem = pl.BlockSpec(memory_space=pltpu.VMEM)
    count = 1 + 4 + 2 * blocks
    dma = pltpu.SemaphoreType.DMA
    flat, flat_f32 = pltpu.VMEM((tokens, width), BF16), pltpu.VMEM((tokens, width), F32)
    return pl.pallas_call(
        functools.partial(
            first_kernel, highs=highs, rows=rows, group=group, micro=micro, seq_here=seq_here, seq_len=seq_len
        ),
        in_specs=[in_vmem, in_any, in_any] + [in_vmem] * 4,
        out_specs=[in_any, in_vmem, in_any] + [in_vmem] * 4,
        out_shape=[
            shaped((tokens, width), BF16),
            shaped((tokens, width), BF16),
            shaped(apart + (tall, deep), BF16),
            shaped((8, width), F32),
            shaped((1, hidden * cols), F32),
            shaped((1, tokens), F32),
            shaped((group * tokens, 1), F32),
        ],
        scratch_shapes=[
            pltpu.VMEM(apart + (tall, deep), BF16),
            pltpu.VMEM(apart + small.shape, F32),
            pltpu.VMEM((rows, narrow, tokens), BF16),
            flat,
            flat,
            pltpu.VMEM((group, 2, tokens, width), BF16),
            flat,
            pltpu.VMEM((group * tokens, tokens), F32),
            flat_f32,
            flat,
            flat_f32,
            flat,
            dma((count, rows - 1, 2, 2)),
            dma((count, highs - 1, 2, 2)),
            dma((count, 2)),
            dma((rows, 2)),
            dma((max(1, group - 1), 2)),
            dma((4, 2)),
            dma((count,)),
            dma((1,)),
        ],
        name="first_forward",
        compiler_params=pltpu.CompilerParams(collective_id=2, has_side_effects=True, vmem_limit_bytes=LOW_VMEM),
        cost_estimate=pl.CostEstimate(
            flops=24 * tokens * width * width, bytes_accessed=2 * tall * deep * rows * cols, transcendentals=0
        ),
    )(small, tokens_in, cotangent, qkv, out, unit, down)


class Streams:
    def __init__(self, landing, sems, group):
        self.landing, self.sems, self.rows = landing, sems, landing.shape[0]
        self.row, self.core = lax.axis_index("row"), lax.axis_index("core")
        self.place, self.size = group.place, group.size
        sequence = lax.div(group.place, group.size)
        self.to = lax.rem(sequence, CORES)
        self.slot = lax.div(sequence, CORES) * group.size + group.position

    def here(self, r):
        return (self.to == self.core) & (self.row == r)

    def sources(self):
        found = []
        for r in range(self.rows):
            place = ((r // self.size) * CORES + self.core) * self.size + r % self.size
            found.append(({"row": lax.div(place, CORES), "core": lax.rem(place, CORES)}, place != self.place))
        return found

    def copy(self, ref, r):
        return pltpu.make_async_remote_copy(
            ref.at[r], self.landing.at[self.slot], self.sems.at[r, 0], self.sems.at[self.slot, 1],
            device_id={"row": r, "core": self.to}, device_id_type=MESH,
        )

    def start(self, ref):
        for r in range(self.rows):

            @pl.when(self.here(r))
            def _(r=r):
                pltpu.make_async_copy(ref.at[r], self.landing.at[self.slot], self.sems.at[self.slot, 1]).start()

            @pl.when(jnp.logical_not(self.here(r)))
            def _(r=r):
                self.copy(ref, r).start()

    def wait_sent(self, ref):
        for r in range(self.rows):

            @pl.when(jnp.logical_not(self.here(r)))
            def _(r=r):
                self.copy(ref, r).wait_send()

    def wait_here(self):
        for r in range(self.rows):
            pltpu.make_async_copy(self.landing.at[r], self.landing.at[r], self.sems.at[r, 1]).wait()


def share_key_grads(group, dkv, got, sems):
    def copy(step):
        return pltpu.make_async_remote_copy(
            dkv.at[step], got.at[step - 1], sems.at[step - 1, 0], sems.at[step - 1, 1],
            device_id=group.member(group.size - step), device_id_type=MESH,
        )

    return [copy(step) for step in range(1, group.size)]


def join_key_grads(dkv, got):
    group, _, tokens, _ = dkv.shape
    step = min(SLICE, tokens)

    @pl.loop(0, tokens, step=step)
    def _(at):
        some = pl.ds(pl.multiple_of(at, step), step)
        for j in range(2):
            total = dkv[0, j, some].astype(F32)
            for i in range(group - 1):
                total += got[i, j, some].astype(F32)
            dkv[0, j, some] = total.astype(BF16)


def heads_back(q, dmixed, mixed, log, kv, mask, first, count):
    group, _, tokens, _ = kv.shape

    @pl.loop(first, first + count)
    def _(p):
        at = pl.ds(pl.multiple_of(p * PAIR, PAIR), PAIR)
        keys = jnp.concatenate([kv[i, 0, :, at] for i in range(group)], axis=0)
        values = jnp.concatenate([kv[i, 1, :, at] for i in range(group)], axis=0)
        grad_query, grad_key, grad_value = pair_back(
            q[:, at], dmixed[:, at], mixed[:, at], [log[p, h : h + 1] for h in range(2)], keys, values, mask,
            min(256, tokens),
        )
        q[:, at] = grad_query
        for part in range(group):
            kv[part, 0, :, at] = grad_key[part * tokens : (part + 1) * tokens]
            kv[part, 1, :, at] = grad_value[part * tokens : (part + 1) * tokens]


def middle_kernel(*refs, group):
    (in_hbm, start_hbm, w_hbm, vectors, shift, doc_q, doc_k) = refs[:7]
    (next_hbm, q_hbm, kv_hbm, mixed_hbm, log_hbm, x1_hbm, hat1_hbm, scale1_hbm, hat2_hbm, scale2_hbm, act_hbm, slope_hbm,
     landing) = refs[7:20]
    (w, x, q, kv, mixed, log, mask, x1, x1_bf, acc, slope, act, hat1, hat2, scale1, scale2, y_t, got,
     sem_w, sem_in, sem_kv, sem_dkv, sem_keep, sem_act, sem_next, sem_out) = refs[20:]
    tokens, width = x.shape
    rows, highs, _, _, deep = w.shape
    narrow, cols = width // rows, highs * CORES
    section = lax.axis_index("section")
    sharing = Group(group)
    front = Front(w, vectors, shift, x, q, kv, mixed, mask, x1, x1_bf, acc, log)
    blocks = front.blocks
    hidden = blocks * deep
    streams = Streams(landing, sem_out, sharing)

    cuts = [(QKV, 3), (OUT, 1)] + [(UNIT + j * blocks + i, 1) for i in range(blocks) for j in range(2)]

    def load_w(i):
        first, count = cuts[i]
        at = pl.ds(first * narrow, count * narrow)
        return pltpu.make_async_copy(w_hbm.at[:, :, :, at], w.at[:, :, :, at], sem_w.at[i])

    get_x = pltpu.make_async_copy(in_hbm, x, sem_in.at[0])
    get_dy = pltpu.make_async_copy(start_hbm, x, sem_in.at[1])
    get_x.start()
    for i in range(len(cuts)):
        load_w(i).start()
    kept = {}

    def keep(i, ref, there):
        kept[i] = pltpu.make_async_copy(ref, there, sem_keep.at[i])
        kept[i].start()

    greet((), ("section",), sharing.members(), streams.sources())
    mask[...] = jnp.where(doc_k[...] == doc_q[...], 0.0, NEG_BIG)
    get_x.wait()
    load_w(0).wait()
    front.project(1)
    front.project(2)
    keys = share_keys(sharing, kv, sem_kv)
    for copy in keys:
        copy.start()
    front.project(0)
    keep(0, q, q_hbm)
    for copy in keys:
        copy.wait()
    keep(1, kv, kv_hbm)
    front.attend(0, front.pairs)
    keep(2, mixed, mixed_hbm)
    keep(3, log, log_hbm)
    load_w(1).wait()
    front.out()

    def keep_one(at, normed, scale):
        hat1[at] = normed.astype(BF16)
        scale1[at] = jnp.broadcast_to(scale, scale1[at].shape)

    front.norm_one(keep_one)
    get_dy.start()
    keep(4, x1_bf, x1_hbm)
    keep(5, hat1, hat1_hbm)
    keep(6, scale1, scale1_hbm)
    half = max(1, cols // 2)
    turns = [(block, range(k, k + half)) for block in range(blocks) for k in range(0, cols, half)]

    def keep_act(n):
        block, ks = turns[n]
        return [
            pltpu.make_async_copy(
                act.at[n % 2, :, pl.ds(i * deep, deep)],
                act_hbm.at[:, pl.ds(k * hidden + block * deep, deep)],
                sem_act.at[n % 2, i],
            )
            for i, k in enumerate(ks)
        ]

    for n, (block, ks) in enumerate(turns):
        if n % (cols // half) == 0:
            load_w(2 + 2 * block).wait()
            load_w(3 + 2 * block).wait()

        def keep_both(value, value_slope, n=n, block=block, ks=ks):
            if n >= 2:
                for copy in keep_act(n - 2):
                    copy.wait()
            act[n % 2] = value
            for copy in keep_act(n):
                copy.start()
            for i, k in enumerate(ks):
                begin = k * hidden + block * deep
                slope[:, begin : begin + deep] = value_slope[:, i * deep : (i + 1) * deep]

        front.feed(block, ks, n == 0, keep_both)
    keep(7, slope, slope_hbm)

    def keep_two(at, normed, scale):
        hat2[at] = normed.astype(BF16)
        scale2[at] = jnp.broadcast_to(scale, scale2[at].shape)

    step = min(SLICE, tokens)
    for begin in range(0, tokens, step):
        y = front.norm_two(pl.ds(begin, step), keep_two)
        y_t[:, :, begin : begin + step] = y.T.astype(BF16).reshape(rows, narrow, step)
    streams.start(y_t)
    keep(8, hat2, hat2_hbm)
    keep(9, scale2, scale2_hbm)

    for i in (4, 5):
        kept[i].wait()
    get_dy.wait()
    ddown, dattn, dmixed, dx = x1_bf, x, hat2, hat1

    def top(at):
        ddown[at] = norm_back(x[at].astype(F32), hat2[at].astype(F32), scale2[at][:, :1], vectors[7:8]).astype(BF16)

    by_tokens(tokens, top)
    for n, (block, ks) in enumerate(turns):
        up = jnp.concatenate([front.matrix(UNIT + block, k) for k in ks], axis=1)
        down = jnp.concatenate([front.matrix(UNIT + blocks + block, k) for k in ks], axis=1)
        begins = [k * hidden + block * deep for k in ks]
        slopes = jnp.concatenate([slope[:, b : b + deep] for b in begins], axis=1)
        dpre = (nn(ddown[...], down) * slopes.astype(F32)).astype(BF16)
        more = nt(dpre, up)
        if n == 0:
            acc[...] = more
        else:
            acc[...] += more
    kept[8].wait()

    def bottom(at):
        dx1 = ddown[at].astype(F32) + acc[at]
        dattn[at] = norm_back(dx1, hat1[at].astype(F32), scale1[at][:, :1], vectors[6:7]).astype(BF16)

    by_tokens(tokens, bottom)
    take = row_blocks(rows, narrow)
    for r in range(0, rows, take):
        some = pl.ds(OUT * narrow, narrow)
        weight = jnp.concatenate(
            [w[r : r + take, k // CORES, k % CORES, some].reshape(take * narrow, deep) for k in range(cols)], axis=1
        )
        dmixed[:, r * narrow : (r + take) * narrow] = nt(dattn[...], weight).astype(BF16)
    kept[0].wait()
    kept[1].wait()
    heads_back(q, dmixed, mixed, log, kv, mask, 0, front.pairs)
    grads = share_key_grads(sharing, kv, got, sem_dkv)
    for copy in grads:
        copy.start()
    for copy in grads:
        copy.wait()
    join_key_grads(kv, got)
    chunks = 2
    chunk = tokens // chunks

    def send_on(i):
        at = pl.ds(i * chunk, chunk)
        return pltpu.make_async_remote_copy(
            dx.at[at], next_hbm.at[at], sem_next.at[i, 0], sem_next.at[i, 1],
            device_id={"section": 1 - section}, device_id_type=MESH,
        )

    stay = pltpu.make_async_copy(start_hbm, next_hbm, sem_in.at[0])

    @pl.when(section == 1)
    def _():
        stay.start()

    for i in range(chunks):
        at = pl.ds(i * chunk, chunk)
        for k in range(cols):
            there = slice(k * deep, (k + 1) * deep)
            total = dattn[at, there].astype(F32)
            for j in range(3):
                total += nn(q[at] if j == 0 else kv[0, j - 1, at], front.matrix(QKV + j, k))
            dx[at, there] = total.astype(BF16)

        @pl.when(section == 1)
        def _(i=i):
            send_on(i).start()

    for n in range(len(turns) - 2, len(turns)):
        for copy in keep_act(n):
            copy.wait()
    for i in (2, 3, 6, 7, 9):
        kept[i].wait()
    streams.wait_sent(y_t)
    streams.wait_here()

    @pl.when(section == 1)
    def _():
        stay.wait()
        for i in range(chunks):
            send_on(i).wait_send()

    @pl.when(section == 0)
    def _():
        for i in range(chunks):
            send_on(i).wait_recv()


def middle(second_in, start, weight, vectors, shift, doc_query, doc_key, group):
    tokens, width = second_in.shape
    rows, highs, _, tall, deep = weight.shape
    cols, narrow, units = highs * CORES, width // rows, shift.shape[1]
    pairs, blocks = width // PAIR, units // cols // deep
    in_any = pl.BlockSpec(memory_space=pl.ANY)
    in_vmem = pl.BlockSpec(memory_space=pltpu.VMEM)
    dma = pltpu.SemaphoreType.DMA
    flat = shaped((tokens, width), BF16)
    thin = shaped((tokens, 128), F32)
    kv = shaped((group, 2, tokens, width), BF16)
    log = shaped((pairs, 2, tokens), F32)
    wide = shaped((tokens, units), BF16)
    turned = shaped((rows, narrow, tokens), BF16)
    half = max(1, cols // 2)

    def vmem(shape):
        return pltpu.VMEM(shape.shape, shape.dtype)

    whole = pltpu.VMEM((tokens, width), F32)
    return pl.pallas_call(
        functools.partial(middle_kernel, group=group),
        in_specs=[in_any] * 3 + [in_vmem] * 4,
        out_specs=[in_any] * 13,
        out_shape=[flat, flat, kv, flat, log, flat, flat, thin, flat, thin, wide, wide, turned],
        scratch_shapes=[
            vmem(weight), vmem(flat), vmem(flat), vmem(kv), vmem(flat), vmem(log),
            pltpu.VMEM((group * tokens, tokens), F32),
            whole, vmem(flat), whole, vmem(wide),
            pltpu.VMEM((2, tokens, half * deep), BF16),
            vmem(flat), vmem(flat), vmem(thin), vmem(thin), vmem(turned),
            pltpu.VMEM((max(1, group - 1), 2, tokens, width), BF16),
            dma((2 + 2 * blocks,)), dma((2,)), dma((max(1, group - 1), 2)), dma((max(1, group - 1), 2)), dma((10,)),
            dma((2, half)), dma((2, 2)), dma((rows, 2)),
        ],
        name="middle",
        compiler_params=pltpu.CompilerParams(collective_id=3, has_side_effects=True, vmem_limit_bytes=LOW_VMEM),
        cost_estimate=pl.CostEstimate(
            flops=72 * tokens * width * width, bytes_accessed=2 * tall * deep * rows * cols, transcendentals=0
        ),
    )(second_in, start, weight, vectors, shift, doc_query, doc_key)


STAGES = 3


def low_kernel(*refs, highs, rows, group):
    (y_hbm, ddown_hbm, act_hbm, x1_hbm, dpre_hbm, dattn_hbm, q_hbm, mixed_hbm, log_hbm, x_hbm, w_hbm, kv_hbm) = refs[:12]
    bias_doc_q, bias_doc_k, pre_ref, sums_ref = refs[12:16]
    down_out, out_out, unit_out, qkv_out, small_out, layer_out, input_out, landed, landing, high_landing = refs[16:26]
    (dattn, x, q, mixed, log, w_out, w_qkv, kv, dmixed, bias, dkv_got, dx, stage, small, left, right,
     work, got, got_high, from_row, from_wide, sem_in, sem_right, sem_core, sem_load, sem_high, sem_row, sem_kv, sem_out, block, block_f32, sem_block) = refs[26:]
    tokens, width = dattn.shape
    narrow, deep = stage.shape[-2:]
    dq, dkv = q, kv
    cols = highs * CORES

    sharing = Group(group)
    streams = Streams(landed, sem_out, sharing)

    def emit(ref, out, r):
        load = pltpu.make_async_copy(ref.at[r], block, sem_block.at[0])
        load.start()
        load.wait()
        block_f32[...] = block[...].astype(F32)
        m, rest = divmod(r, rows // out.shape[1])
        store = pltpu.make_async_copy(block_f32, out.at[0, m, :, pl.ds(rest * tokens, tokens)], sem_block.at[1])
        store.start()
        store.wait()

    units = act_hbm.shape[1]
    feed_pieces = units // cols // deep
    tail = small.shape[3]
    order = [("down", i) for i in range(feed_pieces)] + [("out", 0)]
    order += [("unit", i) for i in range(feed_pieces)] + [("qkv", 0), ("qkv", 1), ("qkv", 2), ("small", 0)]
    row_first = (("down", 1), ("unit", 1))
    pieces = [(stage.at[i % STAGES], narrow, order[i] not in row_first) for i in range(len(order) - 1)]
    pieces += [(small, tail, True)]

    def give(q, ref):
        name, i = order[q]
        value = ref[...].astype(F32)
        if name in ("down", "unit"):
            (down_out if name == "down" else unit_out)[0, :, i * deep : (i + 1) * deep] = value
        elif name == "out":
            out_out[0] = value
        elif name == "qkv":
            qkv_out[0, i] = value
        else:
            small_out[...] = value

    scatter = Scatter(
        pieces, (landing, work, got, high_landing, got_high, from_row, from_wide, sem_core, sem_load, sem_high, sem_row), highs, rows, give,
    )

    inputs = [
        (ddown_hbm, dattn),
        (x1_hbm, x),
        (dattn_hbm, dattn),
        (w_hbm.at[:, :, pl.ds(OUT * narrow, narrow)], w_out),
        (mixed_hbm, mixed),
        (q_hbm, q),
        (log_hbm, log),
        (kv_hbm, kv),
        (w_hbm.at[:, :, pl.ds(QKV * narrow, 3 * narrow)], w_qkv),
        (x_hbm, x),
    ]
    loads = [pltpu.make_async_copy(a, b, sem_in.at[i]) for i, (a, b) in enumerate(inputs)]
    early = 8

    key_grads = share_key_grads(sharing, kv, dkv_got, sem_kv)
    take = row_blocks(rows, narrow)

    def prepare():
        for load in loads[2:early]:
            load.wait()
        bias[...] = jnp.where(bias_doc_k[...] == bias_doc_q[...], 0.0, NEG_BIG).astype(BF16)

        @pl.loop(0, rows // take)
        def _(r):
            at = pl.ds(pl.multiple_of(r * take * narrow, take * narrow), take * narrow)
            dmixed[:, at] = nt(dattn[...], side_by_side(w_out[pl.ds(r * take, take)])).astype(BF16)

    def fill(slot, block, loaded=None):
        @pl.loop(0, cols)
        def _(k):
            grad = nn(left[...], block(k)).astype(BF16)
            stage[slot, :, lax.div(k, CORES), lax.rem(k, CORES)] = grad.reshape(rows, narrow, deep)

    def column(ref):
        return lambda k: ref[:, pl.ds(pl.multiple_of(k * deep, deep), deep)]

    def fetch(q):
        name, i = order[q]
        source = act_hbm if name == "down" else dpre_hbm
        return [
            pltpu.make_async_copy(
                source.at[:, pl.ds(k * feed_pieces * deep + i * deep, deep)],
                right.at[q % 2, :, pl.ds(k * deep, deep)],
                sem_right.at[q % 2, k],
            )
            for k in range(cols)
        ]

    def is_feed(q):
        return q < len(order) and order[q][0] in ("down", "unit")

    def make(q):
        name, i = order[q]
        slot = q % STAGES
        if q == 0:
            loads[0].wait()
            left[...] = dattn[...].T
            loads[2].start()
        if name in ("down", "unit"):
            if (name, i) == ("unit", 0):
                left[...] = x[...].T
                loads[-1].start()
            for copy in fetch(q):
                copy.wait()
            if is_feed(q + 1):
                for copy in fetch(q + 1):
                    copy.start()
            fill(slot, column(right.at[q % 2]))
        elif name == "out":
            if is_feed(q + 1):
                for copy in fetch(q + 1):
                    copy.start()
            left[...] = mixed[...].T
            fill(slot, column(dattn))
        elif name == "qkv":
            if i == 0:
                loads[-1].wait()
            left[...] = grads_of(i).T
            fill(slot, column(x))
        else:
            small_sums()

    pairs = width // PAIR

    def heads(first, count):
        heads_back(q, dmixed, mixed, log, kv, bias, first, count)

    def exchange():
        for copy in key_grads:
            copy.start()

    def join():
        for copy in key_grads:
            copy.wait()
        for load in loads[early:-1]:
            load.wait()
        join_key_grads(kv, dkv_got)

    def grads_of(j):
        return dq[...] if j == 0 else dkv[0, j - 1]

    def input_gradient():
        for k in range(cols):
            at = slice(k * deep, (k + 1) * deep)
            total = dattn[:, at].astype(F32)
            for j in range(3):
                total += nn(grads_of(j), w_qkv[:, k, j * narrow : (j + 1) * narrow].reshape(width, deep))
            for piece in range(0, deep, min(narrow, deep)):
                r, inside = divmod(k * deep + piece, narrow)
                dx[r, inside : inside + min(narrow, deep)] = total[:, piece : piece + min(narrow, deep)].T.astype(BF16)

    def small_sums():
        vectors = jnp.concatenate([column_sum(grads_of(j).astype(F32)) for j in (0, 2)] + [sums_ref[...]], axis=0)
        vectors = vectors.astype(BF16)
        small[...] = jnp.zeros_like(small)
        lines = pre_ref.shape[1] // cols // deep
        for r in range(rows):
            for k in range(cols):
                small[r, k // CORES, k % CORES, 0:8, 0:narrow] = vectors[:, r * narrow : (r + 1) * narrow]
                for i in range(lines):
                    at = (k * lines + i) * deep
                    small[r, k // CORES, k % CORES, 8 + i : 9 + i] = pre_ref[:, at : at + deep].astype(BF16)

    def between(tick):
        if tick + 1 < len(order):
            make(tick + 1)
        if tick == 1:
            prepare()
        if 2 <= tick < 6:
            heads((tick - 2) * (pairs // 4), pairs // 4)
        if tick == 5:
            exchange()
        if tick == 6:
            join()
        if tick == 7:
            input_gradient()
            streams.start(dx)
        if tick in (8, 9, 10, 11):
            for r in range((tick - 8) * rows // 4, (tick - 7) * rows // 4):
                emit(y_hbm, layer_out, r)
        if tick == 13:
            streams.wait_here()
        if tick in (13, 14, 15, 16):
            for r in range((tick - 13) * rows // 4, (tick - 12) * rows // 4):
                emit(landed, input_out, r)

    for i, load in enumerate(loads[:-1]):
        if i != 2:
            load.start()
    for copy in fetch(0):
        copy.start()
    greet((scatter.high, scatter.row), ("core",), sharing.members(), streams.sources())
    loads[1].wait()
    make(0)
    scatter.run(between)
    streams.wait_sent(dx)


def low_back(stream, ddown, act, x1_bf, dpre, dattn, query, mixed, log_total, x, weight, shared, doc_query, doc_key, pre_sum, sums, micro):
    tokens, width = dattn.shape
    rows, cols, _, deep = weight.shape
    narrow = width // rows
    units = act.shape[1]
    feed_rows = narrow * units // cols // deep
    highs, group = cols // CORES, shared.shape[0]
    keys = group * tokens
    apart = (rows, highs, CORES)
    tail = 16
    lines = 8 + pre_sum.shape[1] // cols // deep
    assert lines <= tail and narrow <= deep
    count = 2 * (feed_rows // narrow) + 5
    wide = 2
    steps = 4 + highs - 1 + rows - 1
    slots = min(count, steps)
    in_any = pl.BlockSpec(memory_space=pl.ANY)
    in_vmem = pl.BlockSpec(memory_space=pltpu.VMEM)
    ways = {2: 1}
    block = (rows, narrow, deep)
    dma = pltpu.SemaphoreType.DMA
    args = [stream, ddown, act, x1_bf, dpre, dattn, query, mixed, log_total, x, weight, shared]
    *outs, _, _, _ = pl.pallas_call(
        functools.partial(low_kernel, highs=highs, rows=rows, group=group),
        in_specs=[in_any] * len(args) + [in_vmem] * 4,
        out_specs=[in_vmem] * 5 + [in_any] * 5,
        out_shape=[
            shaped((1, narrow, units // cols), F32),
            shaped((1, narrow, deep), F32),
            shaped((1, narrow, units // cols), F32),
            shaped((1, 3, narrow, deep), F32),
            shaped((tail, deep), F32),
            shaped((1, micro, narrow, rows // micro * tokens), F32),
            shaped((1, micro, narrow, rows // micro * tokens), F32),
            shaped((rows, narrow, tokens), BF16),
            shaped((count, highs) + block, BF16),
            shaped((count, highs - 1, ways.get(highs, 2)) + block, BF16),
        ],
        scratch_shapes=[
            pltpu.VMEM((tokens, width), BF16),
            pltpu.VMEM((tokens, width), BF16),
            pltpu.VMEM((tokens, width), BF16),
            pltpu.VMEM((tokens, width), BF16),
            pltpu.VMEM(log_total.shape, F32),
            pltpu.VMEM((rows, cols, narrow, deep), BF16),
            pltpu.VMEM((rows, cols, 3 * narrow, deep), BF16),
            pltpu.VMEM((group, 2, tokens, width), BF16),
            pltpu.VMEM((tokens, width), BF16),
            pltpu.VMEM((keys, tokens), BF16),
            pltpu.VMEM((group - 1, 2, tokens, width), BF16),
            pltpu.VMEM((rows, narrow, tokens), BF16),
            pltpu.VMEM((STAGES,) + apart + (narrow, deep), BF16),
            pltpu.VMEM(apart + (tail, deep), BF16),
            pltpu.VMEM((width, tokens), BF16),
            pltpu.VMEM((2, tokens, cols * deep), BF16),
            pltpu.VMEM((slots, highs) + block, BF16),
            pltpu.VMEM((2, highs) + block, BF16),
            pltpu.VMEM((2, ways.get(highs, 2)) + block, BF16),
            pltpu.VMEM((count - wide, rows - 1, ways.get(rows, 2), narrow, deep), BF16),
            pltpu.VMEM((wide, rows - 1, ways.get(rows, 2), highs, narrow, deep), BF16),
            dma((10,)),
            dma((2, cols)),
            dma((count, highs, 2)),
            dma((count, highs, 2)),
            dma((count, highs - 1, 2, 3)),
            dma((count, rows - 1, 2, 2)),
            dma((max(1, group - 1), 2)),
            dma((rows, 2)),
            pltpu.VMEM((narrow, tokens), BF16),
            pltpu.VMEM((narrow, tokens), F32),
            dma((2,)),
        ],
        name="low_back",
        compiler_params=pltpu.CompilerParams(collective_id=1, has_side_effects=True, vmem_limit_bytes=LOW_VMEM),
        cost_estimate=pl.CostEstimate(
            flops=64 * tokens * width * width, bytes_accessed=12 * width * units, transcendentals=0
        ),
    )(*args, doc_query, doc_key, pre_sum, sums)
    return outs


def local(tokens_in, doc_ids, cotangent, qkv_master, out_master, unit_master, down_master, unit_bias, width_bias, norm_gain):
    at = Layout(tokens_in, doc_ids)
    rows, cols, narrow = at.rows, at.cols, at.narrow
    deep, hidden = out_master.shape[2], unit_master.shape[2]

    vectors = jnp.concatenate([width_bias[0], norm_gain[0]])
    vectors = jnp.pad(vectors, ((0, 0), (0, deep - narrow)))
    small = jnp.concatenate([vectors, unit_bias.reshape(-1, deep), doc_ids.astype(F32).reshape(-1, deep)])
    small = jnp.pad(small, ((0, -small.shape[0] % 8), (0, 0)))
    second_in, start, weights, vectors, unit_shift, doc_query, doc_key = first_forward(
        small, tokens_in, cotangent, qkv_master, out_master, unit_master, down_master, rows, cols // CORES, at.group,
        at.seq_here, at.seq_len,
    )
    (
        dy, query, shared, mixed, log_total, x1_bf, hat_one, scale_one, hat_two, scale_two, act, slope, stream,
    ) = middle(second_in, start, weights, vectors, unit_shift, doc_query, doc_key, at.group)
    weights = weights.reshape(rows, cols, -1, deep)
    gain = vectors[6:]
    dh2, ddown, top_sums = top_back(dy, hat_two, scale_two, gain, True)
    dattn, dpre, pre_sum, feed_sums = feed_back(dh2, ddown, hat_one, scale_one, slope, weights, gain, True)
    sums = jnp.concatenate([feed_sums[:2], top_sums[:2], feed_sums[2:3], top_sums[2:3]])
    down_sum, out_sum, unit_sum, qkv_sum, sums, layer_out, input_grad = low_back(
        stream, ddown, act, x1_bf, dpre, dattn, query, mixed, log_total, second_in, weights, shared, doc_query, doc_key,
        pre_sum, sums, at.micro,
    )
    vectors, pre_sum = sums[:8, :narrow], sums[8 : 8 + hidden // deep].reshape(-1)
    return (
        layer_out,
        input_grad,
        qkv_sum,
        out_sum,
        unit_sum,
        down_sum,
        pre_sum[None],
        vectors[:6][None],
        vectors[6:][None],
    )


def solution(mesh):
    sections, rows, cols = (mesh.shape[name] for name in ("section", "row", "col"))
    fine = Mesh(
        mesh.devices.reshape(sections, rows, cols // CORES, CORES), ("section", "row", "high", "core")
    )
    col = ("high", "core")
    block = P("section", "row", col)
    stream = P("section", None, "row", col)
    return jax.shard_map(
        local,
        mesh=fine,
        in_specs=(
            P(None, "row", col),
            P(None, col, None),
            P(None, "row", col),
            P("section", None, "row", col),
            block,
            block,
            block,
            P("section", col),
            P("section", None, "row"),
            P("section", None, "row"),
        ),
        out_specs=(
            stream,
            stream,
            stream,
            block,
            block,
            block,
            P("section", col),
            P("section", None, "row"),
            P("section", None, "row"),
        ),
        check_vma=False,
    )
```

```python
import functools

import jax
import jax.numpy as jnp
from jax import lax
from jax.experimental import pallas as pl
from jax.experimental.pallas import tpu as pltpu
from jax.sharding import Mesh
from jax.sharding import PartitionSpec as P

HD = 64
EPSILON = 1e-05
NEG_BIG = -1e30
CORES = 2
PAIR = 128
PLANE = ("row", "high", "core")
MESH = pl.DeviceIdType.MESH

QKV, OUT, UNIT = 0, 3, 4
FEED_BLOCKS = 4

F32 = jnp.float32
BF16 = jnp.bfloat16
VMEM_BYTES = 56 * 1024 * 1024
LOW_VMEM = 63 * 1024 * 1024


def nn(left, right):
    return lax.dot_general(left, right, (((1,), (0,)), ((), ())), preferred_element_type=F32)


def nt(left, right):
    return lax.dot_general(left, right, (((1,), (1,)), ((), ())), preferred_element_type=F32)


def held(shape):
    return pl.BlockSpec(shape, lambda *_: (0,) * len(shape), pipeline_mode=pl.Buffered(1))


def call(kernel, grid, in_specs, out_specs, out_shape, scratch, name, flops, moved, args):
    return pl.pallas_call(
        kernel,
        grid=grid,
        in_specs=in_specs,
        out_specs=out_specs,
        out_shape=out_shape,
        scratch_shapes=scratch,
        name=name,
        compiler_params=pltpu.CompilerParams(
            vmem_limit_bytes=VMEM_BYTES, dimension_semantics=("arbitrary",) * len(grid)
        ),
        cost_estimate=pl.CostEstimate(flops=flops, bytes_accessed=moved, transcendentals=0),
    )(*args)


def shaped(shape, dtype):
    return jax.ShapeDtypeStruct(shape, dtype)


def row_blocks(rows, narrow):
    take = min(rows, max(1, 256 // narrow))
    while rows % take:
        take += 1
    return take


def side_by_side(blocks):
    take, cols, narrow, deep = blocks.shape
    return jnp.concatenate([blocks[:, k].reshape(take * narrow, deep) for k in range(cols)], axis=1)


def head_lanes(shape, axis):
    return lax.broadcasted_iota(jnp.int32, shape, axis) < HD


def pair_front(query, keys, values, bias_ref):
    values_t = values.T
    lanes = head_lanes(query.shape, 1)
    outs, log_rows = [], []
    for h in range(2):
        mine = jnp.where(lanes if h == 0 else ~lanes, query, 0)
        scores = nt(keys, mine) + bias_ref[...]
        top = jnp.max(scores, axis=0, keepdims=True)
        expo = jnp.exp(scores - top)
        total = jnp.sum(expo, axis=0, keepdims=True)
        outs.append(nn(values_t, expo.astype(BF16)) / total)
        log_rows.append(top + jnp.log(total))
    mixed_t = jnp.where(head_lanes(outs[0].shape, 0), outs[0], outs[1])
    return mixed_t.T.astype(BF16), log_rows


def pair_back(query, grad, mixed, log_rows, keys, values, bias_ref, tile):
    tokens = query.shape[0]
    keys_t = keys.T
    lanes = head_lanes((tile, PAIR), 1)
    low_t = head_lanes(keys_t.shape, 0)
    products = (grad.astype(F32) * mixed.astype(F32)).T
    grad_query = []
    grad_key = jnp.zeros(keys.shape, F32)
    grad_value = jnp.zeros(keys.shape, F32)
    for at in range(0, tokens, tile):
        some = slice(at, at + tile)
        grad_some = jnp.zeros((PAIR, tile), F32)
        for h in range(2):
            here = lanes if h == 0 else ~lanes
            mine = jnp.where(here, query[some], 0)
            grad_mine = jnp.where(here, grad[some], 0)
            inner = jnp.sum(products[h * HD : (h + 1) * HD, some], axis=0, keepdims=True)
            prob = jnp.exp(nt(keys, mine) + bias_ref[:, some] - log_rows[h][:, some])
            grad_value += nn(prob.astype(BF16), grad_mine)
            grad_scores = (prob * (nt(values, grad_mine) - inner)).astype(BF16)
            grad_key += nn(grad_scores, mine)
            keys_mine = jnp.where(low_t if h == 0 else ~low_t, keys_t, 0)
            grad_some += nn(keys_mine, grad_scores)
        grad_query.append(grad_some)
    grad_query = jnp.concatenate(grad_query, axis=1).T.astype(BF16) * HD**-0.5
    return grad_query, grad_key.astype(BF16), grad_value.astype(BF16)


def normed_of(hidden):
    center = hidden - jnp.mean(hidden, axis=1, keepdims=True)
    scale = lax.rsqrt(jnp.mean(center * center, axis=1, keepdims=True) + EPSILON)
    return center * scale, scale


def norm_back(grad_out, normed, scale, gain):
    scaled = grad_out * gain
    first = jnp.mean(scaled, axis=1, keepdims=True)
    second = jnp.mean(scaled * normed, axis=1, keepdims=True)
    return scale * (scaled - first - normed * second)


SLICE = 128


def by_tokens(tokens, body):
    step = min(SLICE, tokens)
    for at in range(0, tokens, step):
        body(pl.ds(at, step))


def gelu_parts(pre):
    below = 0.5 * (1.0 + lax.erf(pre * 0.5**0.5))
    return pre * below, below + pre * jnp.exp(-0.5 * pre * pre) * (2.0 * jnp.pi) ** -0.5


def hidden_columns(block, width):
    rows, _, tall, deep = block.shape
    narrow = width // rows
    parts = [block[:, 0, i * narrow : (i + 1) * narrow].reshape(width, deep) for i in range(FEED_BLOCKS)]
    return jnp.concatenate(parts, axis=1)


def feed_specs(weight, tokens, width, units):
    rows, cols, _, deep = weight.shape
    tall = FEED_BLOCKS * (width // rows)
    block = FEED_BLOCKS * deep
    per = units // cols // block

    def at(first):
        return pl.BlockSpec((rows, 1, tall, deep), lambda s: (0, s // per, first // FEED_BLOCKS + s % per, 0))

    wide = pl.BlockSpec((tokens, block), lambda s: (0, s))
    line = pl.BlockSpec((1, block), lambda s: (0, s))
    return cols * per, at(UNIT), at(UNIT + per * FEED_BLOCKS), wide, line


def column_sum(value):
    return jnp.sum(value, axis=0, keepdims=True)


def feed_back_kernel(*refs, steps):
    (dy_ref, hat2_ref, scale2_ref, hat1_ref, scale1_ref, slope_ref, wu_ref, wd_ref, v_ref) = refs[:9]
    (ddown_ref, dattn_ref, dpre_ref, pre_ref, top_ref, feed_ref, acc_ref) = refs[9:]
    s = pl.program_id(0)
    tokens, width = dy_ref.shape

    @pl.when(s == 0)
    def _():
        top_ref[...] = jnp.zeros_like(top_ref)
        feed_ref[...] = jnp.zeros_like(feed_ref)

        def some(at):
            dy, hat = dy_ref[at].astype(F32), hat2_ref[at].astype(F32)
            ddown = norm_back(dy, hat, scale2_ref[at][:, :1], v_ref[7:8]).astype(BF16)
            ddown_ref[at] = ddown
            top_ref[0:1] += column_sum(ddown.astype(F32))
            top_ref[1:2] += column_sum(dy)
            top_ref[2:3] += column_sum(dy * hat)

        by_tokens(tokens, some)

    dact = nn(ddown_ref[...], hidden_columns(wd_ref[...], width))
    dpre = (dact * slope_ref[...].astype(F32)).astype(BF16)
    back = nt(dpre, hidden_columns(wu_ref[...], width))
    dpre_ref[...] = dpre
    pre_ref[...] = column_sum(dpre.astype(F32))

    @pl.when(s == 0)
    def _():
        acc_ref[...] = back

    @pl.when(s > 0)
    def _():
        acc_ref[...] += back

    @pl.when(s == steps - 1)
    def _():
        def some(at):
            dx1, hat = ddown_ref[at].astype(F32) + acc_ref[at], hat1_ref[at].astype(F32)
            dattn = norm_back(dx1, hat, scale1_ref[at][:, :1], v_ref[6:7]).astype(BF16)
            dattn_ref[at] = dattn
            feed_ref[0:1] += column_sum(dattn.astype(F32))
            feed_ref[1:2] += column_sum(dx1)
            feed_ref[2:3] += column_sum(dx1 * hat)

        by_tokens(tokens, some)


def feed_back(dy, hat2, scale2, hat1, scale1, slope, weight, vectors):
    tokens, width = dy.shape
    units = slope.shape[1]
    steps, first, second, wide, line = feed_specs(weight, tokens, width, units)
    flat, thin = held((tokens, width)), held((tokens, 128))
    return call(
        functools.partial(feed_back_kernel, steps=steps),
        (steps,),
        [flat, flat, thin, flat, thin, wide, first, second, held(vectors.shape)],
        [flat, flat, wide, line, held((8, width)), held((8, width))],
        [
            shaped((tokens, width), BF16),
            shaped((tokens, width), BF16),
            shaped((tokens, units), BF16),
            shaped((1, units), F32),
            shaped((8, width), F32),
            shaped((8, width), F32),
        ],
        [pltpu.VMEM((tokens, width), F32)],
        "feed_back",
        4 * tokens * width * units,
        4 * width * units,
        (dy, hat2, scale2, hat1, scale1, slope, weight, weight, vectors),
    )


class Layout:
    def __init__(self, tokens_in, doc_ids):
        self.micro, self.narrow, _ = tokens_in.shape
        self.seq_here, self.seq_len = doc_ids.shape[1:]
        self.rows = lax.axis_size("row")
        self.cols = lax.axis_size("high") * CORES
        self.width = self.narrow * self.rows
        self.places = self.rows * CORES
        self.sequences = self.micro * self.seq_here * CORES
        self.group = self.places // self.sequences
        self.part = self.seq_len // self.group
        self.row = lax.axis_index("row")
        place = self.row * CORES + lax.axis_index("core")
        self.sequence = place // self.group
        self.position = place % self.group
        self.block = (self.sequence // CORES) * self.group + self.position


class Line:
    def __init__(self, axis, size):
        self.axis, self.size, self.here = axis, size, lax.axis_index(axis)

    def sends(self, step):
        last = self.size - 1
        return (
            (True, (self.here < step) & (self.here < last), self.size - step + self.here, self.here > 0),
            (False, (last - self.here < step) & (self.here > 0), step - self.size + self.here, self.here < last),
        )

    def gets(self, step):
        last = self.size - 1
        return (
            (True, (self.here >= 1) & (self.here <= step)),
            (False, (last - self.here >= 1) & (last - self.here <= step)),
        )

    def neighbour(self, right):
        return {self.axis: self.here + (1 if right else -1)}


def greet(lines, pairs, members=(), some=()):
    barrier = pltpu.get_barrier_semaphore()
    count = 0
    for line in lines:
        for right, there in ((True, line.here < line.size - 1), (False, line.here > 0)):

            @pl.when(there)
            def _(line=line, right=right):
                pl.semaphore_signal(barrier, 1, device_id=line.neighbour(right), device_id_type=MESH)

            count = count + there.astype(jnp.int32)
    for axis in pairs:
        pl.semaphore_signal(barrier, 1, device_id={axis: 1 - lax.axis_index(axis)}, device_id_type=MESH)
        count = count + 1
    for member in members:
        pl.semaphore_signal(barrier, 1, device_id=member, device_id_type=MESH)
        count = count + 1
    for member, there in some:

        @pl.when(there)
        def _(member=member):
            pl.semaphore_signal(barrier, 1, device_id=member, device_id_type=MESH)

        count = count + there.astype(jnp.int32)
    pl.semaphore_wait(barrier, count)


def add_into(target, other):
    lead = target.shape[:-2]
    rows = target.shape[-2]
    total = 1
    for size in lead:
        total *= size
    if total == 1:
        target[...] = target[...] + other[...]
        return

    @pl.loop(0, total)
    def _(i):
        index = []
        for size in reversed(lead):
            index.insert(0, lax.rem(i, size))
            i = lax.div(i, size)
        index = tuple(index)
        target[index] = target[index] + other[index]


class Scatter:
    def __init__(self, pieces, refs, highs, rows, give):
        self.pieces, self.give = pieces, give
        (self.landing, self.work, self.got, self.from_high, self.got_high, self.from_row, self.from_wide, *sems) = refs
        self.sem_core, self.sem_load, self.sem_high, self.sem_row = sems
        self.high, self.row = Line("high", highs), Line("row", rows)
        self.core = lax.axis_index("core")
        self.slots = self.work.shape[0]
        self.sent = [[] for _ in pieces]
        self.place, wide, thin = [], 0, 0
        for _, _, row_last in pieces:
            self.place.append(thin if row_last else wide)
            thin, wide = thin + row_last, wide + (not row_last)

    def slot(self, q):
        return q % self.slots

    def cut(self, q, ref):
        return ref.at[..., pl.ds(0, self.pieces[q][1]), :]

    def to_core(self, q, y):
        return pltpu.make_async_remote_copy(
            self.pieces[q][0].at[:, y, 1 - self.core],
            self.cut(q, self.landing.at[q, y]),
            self.sem_core.at[q, y, 0],
            self.sem_core.at[q, y, 1],
            device_id={"core": 1 - self.core},
            device_id_type=MESH,
        )

    def load(self, q, y):
        return pltpu.make_async_copy(
            self.pieces[q][0].at[:, y, self.core],
            self.cut(q, self.work.at[self.slot(q), y]),
            self.sem_load.at[q, y, 0],
        )

    def fetch(self, q, y):
        return pltpu.make_async_copy(
            self.cut(q, self.landing.at[q, y]), self.cut(q, self.got.at[q % 2, y]), self.sem_load.at[q, y, 1]
        )

    def begin(self, q):
        if q >= self.slots:
            self.finish_sends(q - self.slots)
        for y in range(self.high.size):
            self.to_core(q, y).start()
            self.load(q, y).start()

    def arrive(self, q):
        for y in range(self.high.size):
            self.to_core(q, y).wait()
            self.fetch(q, y).start()

    def merge(self, q):
        for y in range(self.high.size):
            self.load(q, y).wait()
            self.fetch(q, y).wait()
            add_into(self.cut(q, self.work.at[self.slot(q), y]), self.cut(q, self.got.at[q % 2, y]))

    def lines(self, q):
        return (self.high, self.row) if self.pieces[q][2] else (self.row, self.high)

    def block(self, q, line, i):
        first = line is self.lines(q)[0]
        if line is self.high:
            ref = self.work.at[self.slot(q), i, slice(None) if first else self.row.here]
        else:
            ref = self.work.at[self.slot(q), slice(None) if first else self.high.here, i]
        return self.cut(q, ref)

    def arrival(self, q, line, step, right):
        way = 0 if line.size == 2 or right else 1
        first = line is self.lines(q)[0]
        if line is self.high:
            index = (slice(None),) if first else (0,)
            return (
                self.cut(q, self.from_high.at[(q, step - 1, way) + index]),
                self.cut(q, self.got_high.at[(q % 2, way) + index]),
            )
        ref = (self.from_wide if first else self.from_row).at[self.place[q], step - 1, way]
        return (self.cut(q, ref),) * 2

    def copy(self, q, line, step, right, i):
        sems = (self.sem_high if line is self.high else self.sem_row).at[q, step - 1, 0 if right else 1]
        return pltpu.make_async_remote_copy(
            self.block(q, line, i),
            self.arrival(q, line, step, right)[0],
            sems.at[0],
            sems.at[1],
            device_id=line.neighbour(right),
            device_id_type=MESH,
        )

    def push(self, q, line, step):
        for right, there, i, more in line.sends(step):

            @pl.when(there)
            def _(right=right, i=i, more=more):
                if step > 1:

                    @pl.when(more)
                    def _():
                        add_into(self.block(q, line, i), self.arrival(q, line, step - 1, right)[1])

                self.copy(q, line, step, right, i).start()

            self.sent[q].append((line, step, right, there, i))

    def pull(self, q, line, step):
        for right, there in line.gets(step):

            @pl.when(there)
            def _(right=right):
                self.copy(q, line, step, right, 0).wait_recv()
                if line is self.high:
                    landed, got = self.arrival(q, line, step, right)
                    way = 0 if line.size == 2 or right else 1
                    fetch = pltpu.make_async_copy(landed, got, self.sem_high.at[q, step - 1, way, 2])
                    fetch.start()
                    fetch.wait()

    def close(self, q, line):
        for right, there in line.gets(line.size - 1):

            @pl.when(there)
            def _(right=right):
                add_into(self.block(q, line, line.here), self.arrival(q, line, line.size - 1, right)[1])

    def finish_sends(self, q):
        for line, step, right, there, i in self.sent[q]:

            @pl.when(there)
            def _(line=line, step=step, right=right, i=i):
                self.copy(q, line, step, right, i).wait_send()

        self.sent[q] = []

    def stages(self, q):
        lines = [(line, step) for line in self.lines(q) for step in range(1, line.size)]

        def merge():
            self.merge(q)
            self.push(q, *lines[0])

        stages = [lambda: self.begin(q), lambda: self.arrive(q), merge]
        for n, (line, step) in enumerate(lines):

            def one(n=n, line=line, step=step):
                self.pull(q, line, step)
                if step == line.size - 1:
                    self.close(q, line)
                if n + 1 < len(lines):
                    self.push(q, *lines[n + 1])
                else:
                    self.give(q, self.block(q, line, line.here))

            if line is self.high and step == 1:
                stages.append(lambda: None)
            stages.append(one)
        return stages

    def run(self, between):
        stages = [self.stages(q) for q in range(len(self.pieces))]
        depth, count = len(stages[0]), len(stages)
        for tick in range(count + depth - 1):
            for q in range(max(0, tick - depth + 1), min(tick + 1, count)):
                stages[q][tick - q]()
            between(tick)
        for q in range(count):
            self.finish_sends(q)


class Spread:
    def __init__(self, axis, size):
        self.axis, self.size, self.here = axis, size, lax.axis_index(axis)

    def sends(self, step):
        last = self.size - 1
        return (
            (True, (self.here < last) & (self.here >= step - 1), self.here - step + 1),
            (False, (self.here > 0) & (self.here + step - 1 <= last), self.here + step - 1),
        )

    def gets(self, step):
        last = self.size - 1
        return ((True, self.here >= step), (False, self.here + step <= last))

    def neighbour(self, right):
        return {self.axis: self.here + (1 if right else -1)}


class Gather:
    def __init__(self, pieces, sems, highs, rows):
        self.pieces = pieces
        self.sem_row, self.sem_high, self.sem_core, self.sem_one = sems
        self.row, self.high = Spread("row", rows), Spread("high", highs)
        self.core = lax.axis_index("core")
        self.sent = []

    def block(self, q, line, i):
        ref, first, count, row_first = self.pieces[q]
        some = pl.ds(first, count)
        if line is self.row:
            return ref.at[i, self.high.here if row_first else slice(None), self.core, some]
        return ref.at[slice(None) if row_first else self.row.here, i, self.core, some]

    def copy(self, q, line, step, right, i):
        sems = (self.sem_row if line is self.row else self.sem_high).at[q, step - 1, 0 if right else 1]
        ref = self.block(q, line, i)
        return pltpu.make_async_remote_copy(
            ref, ref, sems.at[0], sems.at[1], device_id=line.neighbour(right), device_id_type=MESH
        )

    def one(self, q, right, i):
        ref, first, count, _ = self.pieces[q]
        ref = ref.at[i, self.high.here, self.core, pl.ds(first, count)]
        sems = self.sem_one.at[q, i, 0 if right else 1]
        return pltpu.make_async_remote_copy(
            ref, ref, sems.at[0], sems.at[1], device_id=self.high.neighbour(right), device_id_type=MESH
        )

    def start(self, there, copy):
        @pl.when(there)
        def _():
            copy().start()

        self.sent.append((there, copy))

    def over(self, q, i, there=True):
        for right, also, _ in self.high.sends(1):
            self.start(also & there, functools.partial(self.one, q, right, i))

    def push(self, q, line, step):
        if line is self.high and step == 1 and self.pieces[q][3]:
            return
        for right, there, i in line.sends(step):
            self.start(there, functools.partial(self.copy, q, line, step, right, i))

    def pull(self, q, line, step):
        row_first = self.pieces[q][3]
        for right, there in line.gets(step):

            @pl.when(there)
            def _(right=right):
                if line is self.high and step == 1 and row_first:
                    for i in range(self.row.size):
                        self.one(q, right, i).wait_recv()
                else:
                    self.copy(q, line, step, right, line.here).wait_recv()

            if line is self.row and row_first:
                self.over(q, line.here - step if right else line.here + step, there)

    def to_core(self, q):
        ref, first, count, _ = self.pieces[q]
        ref = ref.at[:, :, self.core, pl.ds(first, count)]
        return pltpu.make_async_remote_copy(
            ref, ref, self.sem_core.at[q, 0], self.sem_core.at[q, 1],
            device_id={"core": 1 - self.core}, device_id_type=MESH,
        )

    def stages(self, q):
        first, second = (self.row, self.high) if self.pieces[q][3] else (self.high, self.row)
        def begin():
            self.push(q, first, 1)
            if first is self.row:
                self.over(q, self.row.here)

        steps = [begin]
        lines = [(first, i) for i in range(1, first.size)] + [(second, i) for i in range(1, second.size)]
        for n, (line, step) in enumerate(lines):

            def one(n=n, line=line, step=step):
                self.pull(q, line, step)
                if n + 1 < len(lines):
                    self.push(q, *lines[n + 1])
                else:
                    self.to_core(q).start()

            steps.append(lambda: None)
            steps.append(one)
        steps.append(lambda: self.to_core(q).wait())
        return steps

    def run(self, between):
        stages = [self.stages(q) for q in range(len(self.pieces))]
        depth, count = len(stages[0]), len(stages)
        for tick in range(count + depth - 1):
            for q in range(max(0, tick - depth + 1), min(tick + 1, count)):
                stages[q][tick - q]()
            between(tick, tick - depth + 1)

    def finish(self):
        for there, copy in self.sent:

            @pl.when(there)
            def _(copy=copy):
                copy().wait_send()


class Group:
    def __init__(self, size):
        self.size = size
        self.place = lax.axis_index("row") * CORES + lax.axis_index("core")
        self.position = lax.rem(self.place, size)

    def member(self, step):
        other = self.place - self.position + lax.rem(self.position + step, self.size)
        return {"row": lax.div(other, CORES), "core": lax.rem(other, CORES)}

    def members(self):
        return [self.member(step) for step in range(1, self.size)]


class Front:
    def __init__(self, w, vectors, shift, x, q, kv, mixed, mask, x1, x1_bf, acc, log=None):
        self.w, self.vectors, self.shift, self.x, self.q, self.kv = w, vectors, shift, x, q, kv
        self.mixed, self.mask, self.x1, self.x1_bf, self.acc, self.log = mixed, mask, x1, x1_bf, acc, log
        self.tokens, self.width = x.shape
        self.rows, self.highs, _, _, self.deep = w.shape
        self.cols = self.highs * CORES
        self.narrow = self.width // self.rows
        self.group = kv.shape[0]
        self.pairs = self.width // PAIR
        self.blocks = shift.shape[1] // self.cols // self.deep

    def matrix(self, block, k):
        at = pl.ds(block * self.narrow, self.narrow)
        return self.w[:, k // CORES, k % CORES, at].reshape(self.width, self.deep)

    def project(self, j):
        take = row_blocks(self.rows, self.narrow)
        for r in range(0, self.rows, take):
            at = slice(r * self.narrow, (r + take) * self.narrow)
            some = pl.ds((QKV + j) * self.narrow, self.narrow)
            weight = jnp.concatenate(
                [
                    self.w[r : r + take, k // CORES, k % CORES, some].reshape(take * self.narrow, self.deep)
                    for k in range(self.cols)
                ],
                axis=1,
            )
            out = nt(self.x[...], weight)
            if j == 0:
                self.q[:, at] = ((out + self.vectors[0:1, at]) * HD**-0.5).astype(BF16)
            elif j == 1:
                self.kv[0, 0, :, at] = out.astype(BF16)
            else:
                self.kv[0, 1, :, at] = (out + self.vectors[1:2, at]).astype(BF16)

    def attend(self, first, count):
        @pl.loop(first, first + count)
        def _(p):
            at = pl.ds(pl.multiple_of(p * PAIR, PAIR), PAIR)
            keys = jnp.concatenate([self.kv[i, 0, :, at] for i in range(self.group)], axis=0)
            values = jnp.concatenate([self.kv[i, 1, :, at] for i in range(self.group)], axis=0)
            mixed, log_rows = pair_front(self.q[:, at], keys, values, self.mask)
            self.mixed[:, at] = mixed
            if self.log is not None:
                for h in range(2):
                    self.log[p, h : h + 1] = log_rows[h]

    def out(self):
        for k in range(self.cols):
            at = slice(k * self.deep, (k + 1) * self.deep)
            self.acc[:, at] = nn(self.mixed[...], self.matrix(OUT, k))

    def norm_one(self, keep=None):
        def some(at):
            attn = self.acc[at] + self.vectors[2:3]
            normed, scale = normed_of(self.x[at].astype(F32) + attn)
            x1 = normed * self.vectors[6:7] + self.vectors[3:4]
            self.x1[at] = x1
            self.x1_bf[at] = x1.astype(BF16)
            if keep is not None:
                keep(at, normed, scale)

        by_tokens(self.tokens, some)

    def feed(self, block, ks, start, keep=None, at=slice(None)):
        up = jnp.concatenate([self.matrix(UNIT + block, k) for k in ks], axis=1)
        down = jnp.concatenate([self.matrix(UNIT + self.blocks + block, k) for k in ks], axis=1)
        hidden = self.blocks * self.deep
        begins = [k * hidden + block * self.deep for k in ks]
        shift = jnp.concatenate([self.shift[:, b : b + self.deep] for b in begins], axis=1)
        act, slope = gelu_parts(nn(self.x1_bf[at], up) + shift)
        act = act.astype(BF16)
        if keep is not None:
            keep(act, slope.astype(BF16))
        more = nt(act, down)
        if start:
            self.acc[at] = more
        else:
            self.acc[at] += more

    def norm_two(self, at, keep=None):
        normed, scale = normed_of(self.x1[at] + (self.acc[at] + self.vectors[4:5]))
        if keep is not None:
            keep(at, normed, scale)
        return normed * self.vectors[7:8] + self.vectors[5:6]


def share_keys(group, kv, sems):
    def copy(step):
        return pltpu.make_async_remote_copy(
            kv.at[0], kv.at[step], sems.at[step - 1, 0], sems.at[step - 1, 1],
            device_id=group.member(step), device_id_type=MESH,
        )

    return [copy(step) for step in range(1, group.size)]


def first_kernel(*refs, highs, rows, group, micro, seq_here, seq_len):
    (tokens_hbm, cot_hbm, qkv_ref, out_ref, unit_ref, down_ref, unit_bias, width_bias, gain, docs) = refs[:10]
    (next_hbm, start_ref, w_hbm, vectors, shift, doc_q, doc_k) = refs[10:17]
    (w, small, turned, x, q, kv, mixed, mask, x1, x1_bf, acc, y,
     sem_row, sem_high, sem_core, sem_one, sem_x, sem_kv, sem_y, sem_w, sem_next) = refs[17:]
    tokens, width = x.shape
    narrow, deep = width // rows, w.shape[-1]
    cols = highs * CORES
    hidden = unit_ref.shape[2]
    blocks = hidden // deep
    row, high, core = lax.axis_index("row"), lax.axis_index("high"), lax.axis_index("core")
    section = lax.axis_index("section")
    sharing = Group(group)
    sequence = lax.div(sharing.place, group)
    front = Front(w, vectors, shift, x, q, kv, mixed, mask, x1, x1_bf, acc)

    w[row, high, core, 0 : 3 * narrow] = qkv_ref[0].reshape(3 * narrow, deep).astype(BF16)
    w[row, high, core, 3 * narrow : 4 * narrow] = out_ref[0].astype(BF16)
    for i in range(blocks):
        at = slice(i * deep, (i + 1) * deep)
        for j, ref in enumerate((unit_ref, down_ref)):
            first = (UNIT + j * blocks + i) * narrow
            w[row, high, core, first : first + narrow] = ref[0, :, at].astype(BF16)
    small[row, high, core, 0:6, 0:narrow] = width_bias[0]
    small[row, high, core, 6:8, 0:narrow] = gain[0]
    for i in range(blocks):
        small[row, high, core, 8 + i : 9 + i] = unit_bias[:, i * deep : (i + 1) * deep]
    lines = seq_len // deep
    for m in range(micro):
        for i in range(seq_here):
            for j in range(lines):
                at = 8 + blocks + (m * seq_here + i) * lines + j
                small[row, high, core, at : at + 1] = docs[m, i : i + 1, j * deep : (j + 1) * deep].astype(F32)

    def goes(j):
        place = ((j // group) * CORES + core) * group + j % group
        return lax.div(place, CORES), lax.rem(place, CORES)

    source_core = lax.rem(sequence, CORES)
    mine_too = source_core == core

    def block_of(ref, j):
        m, rest = divmod(j // group, seq_here)
        return ref.at[m, :, pl.ds(rest * seq_len + (j % group) * tokens, tokens)]

    def send_block(ref, j):
        there_row, there_core = goes(j)
        return pltpu.make_async_remote_copy(
            block_of(ref, j), turned.at[row], sem_x.at[j, 0], sem_x.at[row, 1],
            device_id={"row": there_row, "core": there_core}, device_id_type=MESH,
        )

    def is_here(j):
        there_row, there_core = goes(j)
        return (there_row == row) & (there_core == core)

    barrier = pltpu.get_barrier_semaphore()
    count = 0
    for line in (Spread("row", rows), Spread("high", highs)):
        for right, there in ((True, line.here < line.size - 1), (False, line.here > 0)):

            @pl.when(there)
            def _(line=line, right=right):
                pl.semaphore_signal(barrier, 1, device_id=line.neighbour(right), device_id_type=MESH)

            count = count + there.astype(jnp.int32)
    others = [{"core": 1 - core}, {"section": 1 - section}] + sharing.members()
    for other in others:
        pl.semaphore_signal(barrier, 1, device_id=other, device_id_type=MESH)
    for r in range(rows):

        @pl.when(jnp.logical_not(mine_too & (row == r)))
        def _(r=r):
            pl.semaphore_signal(barrier, 1, device_id={"row": r, "core": source_core}, device_id_type=MESH)

    pl.semaphore_wait(barrier, count + len(others) + rows - mine_too.astype(jnp.int32))

    row_first = [True] * (4 + 2 * blocks)
    row_first[4 + blocks] = False
    order = [0, 1, 2, 3] + [UNIT + j * blocks + i for i in range(blocks) for j in range(2)]
    pieces = [(small, 0, small.shape[3], True)]
    pieces += [(w, i * narrow, narrow, row_first[n]) for n, i in enumerate(order)]
    gather = Gather(pieces, (sem_row, sem_high, sem_core, sem_one), highs, rows)

    def to_hbm(q):
        at = pl.ds(order[q - 1] * narrow, narrow)
        return pltpu.make_async_copy(w.at[:, :, :, at], w_hbm.at[:, :, :, at], sem_w.at[q])

    keys = share_keys(sharing, kv, sem_kv)

    def begin():
        for j in range(rows):
            for which, ref in ((0, tokens_hbm), (1, cot_hbm)):

                @pl.when((section == which) & is_here(j))
                def _(ref=ref, j=j):
                    pltpu.make_async_copy(block_of(ref, j), turned.at[row], sem_x.at[row, 1]).start()

                @pl.when((section == which) & jnp.logical_not(is_here(j)))
                def _(ref=ref, j=j):
                    send_block(ref, j).start()

    def use_small():
        for r in range(rows):
            vectors[:, r * narrow : (r + 1) * narrow] = small[r, 0, 0, 0:8, 0:narrow]
        for k in range(cols):
            for i in range(blocks):
                at = k * hidden + i * deep
                shift[:, at : at + deep] = small[0, k // CORES, k % CORES, 8 + i : 9 + i]
        lines = tokens // deep
        for slot in range(group):
            part = lax.rem(sharing.position + group - slot, group)
            base = 8 + blocks + (lax.div(sequence, CORES) * group + part) * lines
            doc = jnp.concatenate([small[row, high, source_core, pl.ds(base + i, 1)] for i in range(lines)], axis=1)
            if slot == 0:
                doc_q[...] = doc
            doc_k[slot * tokens : (slot + 1) * tokens] = jnp.broadcast_to(doc, (128, tokens)).T[:, :1]
        mask[...] = jnp.where(doc_k[...] == doc_q[...], 0.0, NEG_BIG)

    def turn():
        for r in range(rows):
            pltpu.make_async_copy(turned.at[r], turned.at[r], sem_x.at[r, 1]).wait()
        for r in range(rows):
            x[:, r * narrow : (r + 1) * narrow] = turned[r].T
        start_ref[...] = x[...]

    half = max(1, cols // 2)
    chunks = min(4, tokens // 8)
    chunk = tokens // chunks

    def send_out(i):
        at = pl.ds(i * chunk, chunk)
        return pltpu.make_async_remote_copy(
            y.at[at], next_hbm.at[at], sem_y.at[i, 0], sem_y.at[i, 1],
            device_id={"section": 1 - section}, device_id_type=MESH,
        )

    stay = pltpu.make_async_copy(x, next_hbm, sem_next.at[0])
    base = 3

    def between(tick, done):
        if tick == 2:
            begin()
        if done >= 1:
            to_hbm(done).start()
        if done == 0:
            use_small()
        if done == 1:
            turn()

            @pl.when(section == 0)
            def _():
                stay.start()

            front.project(0)
        if done == 2:
            front.project(1)
        if done == base:
            front.project(2)
            for copy in keys:
                copy.start()
        if done == base + 1:
            for copy in keys:
                copy.wait()
        if base + 1 <= done < base + 5:
            front.attend((done - base - 1) * (front.pairs // 4), front.pairs // 4)
        if done == base + 5:
            front.out()
            front.norm_one()
        if done >= base + 5:
            first = done == base + 5
            ready = (done - 4) // 2
            from_block = 0 if first else (done - 1 - 4) // 2
            for block in range(from_block, min(ready, blocks)):
                if block < blocks - 1:
                    for k in range(0, cols, half):
                        front.feed(block, range(k, k + half), block == 0 and k == 0)

    gather.run(between)
    for i in range(chunks):
        at = pl.ds(i * chunk, chunk)
        for k in range(0, cols, half):
            front.feed(blocks - 1, range(k, k + half), blocks == 1 and k == 0, at=at)
        y[at] = front.norm_two(at).astype(BF16)

        @pl.when(section == 0)
        def _(i=i):
            send_out(i).start()

    gather.finish()
    for j in range(rows):

        @pl.when(jnp.logical_not(is_here(j)))
        def _(j=j):
            send_block(tokens_hbm, j).wait_send()

    for q in range(1, len(pieces)):
        to_hbm(q).wait()

    @pl.when(section == 0)
    def _():
        stay.wait()
        for i in range(chunks):
            send_out(i).wait_send()

    @pl.when(section == 1)
    def _():
        for i in range(chunks):
            send_out(i).wait_recv()


def first_forward(tokens_in, cotangent, qkv, out, unit, down, unit_bias, width_bias, gain, docs, rows, highs, group):
    micro, narrow, _ = tokens_in.shape
    _, seq_here, seq_len = docs.shape
    deep, hidden = out.shape[2], unit.shape[2]
    width, cols, blocks = narrow * rows, highs * CORES, hidden // deep
    tokens = seq_len // group
    tall = (4 + 2 * blocks) * narrow
    apart = (rows, highs, CORES)
    in_any = pl.BlockSpec(memory_space=pl.ANY)
    in_vmem = pl.BlockSpec(memory_space=pltpu.VMEM)
    count = 1 + 4 + 2 * blocks
    small_rows = 8 + blocks + micro * seq_here * seq_len // deep
    small_rows += -small_rows % 8
    dma = pltpu.SemaphoreType.DMA
    flat, flat_f32 = pltpu.VMEM((tokens, width), BF16), pltpu.VMEM((tokens, width), F32)
    return pl.pallas_call(
        functools.partial(
            first_kernel, highs=highs, rows=rows, group=group, micro=micro, seq_here=seq_here, seq_len=seq_len
        ),
        in_specs=[in_any] * 2 + [in_vmem] * 8,
        out_specs=[in_any, in_vmem, in_any] + [in_vmem] * 4,
        out_shape=[
            shaped((tokens, width), BF16),
            shaped((tokens, width), BF16),
            shaped(apart + (tall, deep), BF16),
            shaped((8, width), F32),
            shaped((1, hidden * cols), F32),
            shaped((1, tokens), F32),
            shaped((group * tokens, 1), F32),
        ],
        scratch_shapes=[
            pltpu.VMEM(apart + (tall, deep), BF16),
            pltpu.VMEM(apart + (small_rows, deep), F32),
            pltpu.VMEM((rows, narrow, tokens), BF16),
            flat,
            flat,
            pltpu.VMEM((group, 2, tokens, width), BF16),
            flat,
            pltpu.VMEM((group * tokens, tokens), F32),
            flat_f32,
            flat,
            flat_f32,
            flat,
            dma((count, rows - 1, 2, 2)),
            dma((count, highs - 1, 2, 2)),
            dma((count, 2)),
            dma((count, rows, 2, 2)),
            dma((rows, 2)),
            dma((max(1, group - 1), 2)),
            dma((4, 2)),
            dma((count,)),
            dma((1,)),
        ],
        name="first_forward",
        compiler_params=pltpu.CompilerParams(collective_id=2, has_side_effects=True, vmem_limit_bytes=LOW_VMEM),
        cost_estimate=pl.CostEstimate(
            flops=24 * tokens * width * width, bytes_accessed=2 * tall * deep * rows * cols, transcendentals=0
        ),
    )(tokens_in, cotangent, qkv, out, unit, down, unit_bias, width_bias, gain, docs)


class Streams:
    def __init__(self, landing, sems, group):
        self.landing, self.sems, self.rows = landing, sems, landing.shape[0]
        self.row, self.core = lax.axis_index("row"), lax.axis_index("core")
        self.place, self.size = group.place, group.size
        sequence = lax.div(group.place, group.size)
        self.to = lax.rem(sequence, CORES)
        self.slot = lax.div(sequence, CORES) * group.size + group.position

    def here(self, r):
        return (self.to == self.core) & (self.row == r)

    def sources(self):
        found = []
        for r in range(self.rows):
            place = ((r // self.size) * CORES + self.core) * self.size + r % self.size
            found.append(({"row": lax.div(place, CORES), "core": lax.rem(place, CORES)}, place != self.place))
        return found

    def copy(self, ref, r):
        return pltpu.make_async_remote_copy(
            ref.at[r], self.landing.at[self.slot], self.sems.at[r, 0], self.sems.at[self.slot, 1],
            device_id={"row": r, "core": self.to}, device_id_type=MESH,
        )

    def start(self, ref):
        for r in range(self.rows):

            @pl.when(self.here(r))
            def _(r=r):
                pltpu.make_async_copy(ref.at[r], self.landing.at[self.slot], self.sems.at[self.slot, 1]).start()

            @pl.when(jnp.logical_not(self.here(r)))
            def _(r=r):
                self.copy(ref, r).start()

    def wait_sent(self, ref):
        for r in range(self.rows):

            @pl.when(jnp.logical_not(self.here(r)))
            def _(r=r):
                self.copy(ref, r).wait_send()

    def wait_here(self):
        for r in range(self.rows):
            pltpu.make_async_copy(self.landing.at[r], self.landing.at[r], self.sems.at[r, 1]).wait()


def share_key_grads(group, dkv, got, sems):
    def copy(step):
        return pltpu.make_async_remote_copy(
            dkv.at[step], got.at[step - 1], sems.at[step - 1, 0], sems.at[step - 1, 1],
            device_id=group.member(group.size - step), device_id_type=MESH,
        )

    return [copy(step) for step in range(1, group.size)]


def join_key_grads(dkv, got):
    group, _, tokens, _ = dkv.shape
    step = min(SLICE, tokens)

    @pl.loop(0, tokens, step=step)
    def _(at):
        some = pl.ds(pl.multiple_of(at, step), step)
        for j in range(2):
            total = dkv[0, j, some].astype(F32)
            for i in range(group - 1):
                total += got[i, j, some].astype(F32)
            dkv[0, j, some] = total.astype(BF16)


def heads_back(q, dmixed, mixed, log, kv, mask, first, count):
    group, _, tokens, _ = kv.shape

    @pl.loop(first, first + count)
    def _(p):
        at = pl.ds(pl.multiple_of(p * PAIR, PAIR), PAIR)
        keys = jnp.concatenate([kv[i, 0, :, at] for i in range(group)], axis=0)
        values = jnp.concatenate([kv[i, 1, :, at] for i in range(group)], axis=0)
        grad_query, grad_key, grad_value = pair_back(
            q[:, at], dmixed[:, at], mixed[:, at], [log[p, h : h + 1] for h in range(2)], keys, values, mask,
            min(256, tokens),
        )
        q[:, at] = grad_query
        for part in range(group):
            kv[part, 0, :, at] = grad_key[part * tokens : (part + 1) * tokens]
            kv[part, 1, :, at] = grad_value[part * tokens : (part + 1) * tokens]


def middle_kernel(*refs, group):
    (in_hbm, start_hbm, w_hbm, vectors, shift, doc_q, doc_k) = refs[:7]
    (next_hbm, q_hbm, kv_hbm, mixed_hbm, log_hbm, x1_hbm, hat1_hbm, scale1_hbm, hat2_hbm, scale2_hbm, act_hbm, slope_hbm,
     landing) = refs[7:20]
    (w, x, q, kv, mixed, log, mask, x1, x1_bf, acc, slope, act, hat1, hat2, scale1, scale2, y_t, got,
     sem_w, sem_in, sem_kv, sem_dkv, sem_keep, sem_act, sem_next, sem_out) = refs[20:]
    tokens, width = x.shape
    rows, highs, _, _, deep = w.shape
    narrow, cols = width // rows, highs * CORES
    section = lax.axis_index("section")
    sharing = Group(group)
    front = Front(w, vectors, shift, x, q, kv, mixed, mask, x1, x1_bf, acc, log)
    blocks = front.blocks
    hidden = blocks * deep
    streams = Streams(landing, sem_out, sharing)

    cuts = [(QKV, 3), (OUT, 1)] + [(UNIT + j * blocks + i, 1) for i in range(blocks) for j in range(2)]

    def load_w(i):
        first, count = cuts[i]
        at = pl.ds(first * narrow, count * narrow)
        return pltpu.make_async_copy(w_hbm.at[:, :, :, at], w.at[:, :, :, at], sem_w.at[i])

    get_x = pltpu.make_async_copy(in_hbm, x, sem_in.at[0])
    get_dy = pltpu.make_async_copy(start_hbm, x, sem_in.at[1])
    get_x.start()
    for i in range(len(cuts)):
        load_w(i).start()
    kept = {}

    def keep(i, ref, there):
        kept[i] = pltpu.make_async_copy(ref, there, sem_keep.at[i])
        kept[i].start()

    greet((), ("section",), sharing.members(), streams.sources())
    mask[...] = jnp.where(doc_k[...] == doc_q[...], 0.0, NEG_BIG)
    get_x.wait()
    load_w(0).wait()
    front.project(1)
    front.project(2)
    keys = share_keys(sharing, kv, sem_kv)
    for copy in keys:
        copy.start()
    front.project(0)
    keep(0, q, q_hbm)
    for copy in keys:
        copy.wait()
    keep(1, kv, kv_hbm)
    front.attend(0, front.pairs)
    keep(2, mixed, mixed_hbm)
    keep(3, log, log_hbm)
    load_w(1).wait()
    front.out()

    def keep_one(at, normed, scale):
        hat1[at] = normed.astype(BF16)
        scale1[at] = jnp.broadcast_to(scale, scale1[at].shape)

    front.norm_one(keep_one)
    get_dy.start()
    keep(4, x1_bf, x1_hbm)
    keep(5, hat1, hat1_hbm)
    keep(6, scale1, scale1_hbm)
    half = cols if tokens * cols * deep <= 1 << 19 else max(1, cols // 2)
    turns = [(block, range(k, k + half)) for block in range(blocks) for k in range(0, cols, half)]

    def keep_act(n):
        block, ks = turns[n]
        return [
            pltpu.make_async_copy(
                act.at[n % 2, :, pl.ds(i * deep, deep)],
                act_hbm.at[:, pl.ds(k * hidden + block * deep, deep)],
                sem_act.at[n % 2, i],
            )
            for i, k in enumerate(ks)
        ]

    for n, (block, ks) in enumerate(turns):
        if n % (cols // half) == 0:
            load_w(2 + 2 * block).wait()
            load_w(3 + 2 * block).wait()

        def keep_both(value, value_slope, n=n, block=block, ks=ks):
            if n >= 2:
                for copy in keep_act(n - 2):
                    copy.wait()
            act[n % 2] = value
            for copy in keep_act(n):
                copy.start()
            for i, k in enumerate(ks):
                begin = k * hidden + block * deep
                slope[:, begin : begin + deep] = value_slope[:, i * deep : (i + 1) * deep]

        front.feed(block, ks, n == 0, keep_both)
    keep(7, slope, slope_hbm)

    def keep_two(at, normed, scale):
        hat2[at] = normed.astype(BF16)
        scale2[at] = jnp.broadcast_to(scale, scale2[at].shape)

    step = min(SLICE, tokens)
    for begin in range(0, tokens, step):
        y = front.norm_two(pl.ds(begin, step), keep_two)
        y_t[:, :, begin : begin + step] = y.T.astype(BF16).reshape(rows, narrow, step)
    streams.start(y_t)
    keep(8, hat2, hat2_hbm)
    keep(9, scale2, scale2_hbm)

    for i in (4, 5):
        kept[i].wait()
    get_dy.wait()
    ddown, dattn, dmixed, dx = x1_bf, x, hat2, hat1

    def top(at):
        ddown[at] = norm_back(x[at].astype(F32), hat2[at].astype(F32), scale2[at][:, :1], vectors[7:8]).astype(BF16)

    by_tokens(tokens, top)
    for n, (block, ks) in enumerate(turns):
        up = jnp.concatenate([front.matrix(UNIT + block, k) for k in ks], axis=1)
        down = jnp.concatenate([front.matrix(UNIT + blocks + block, k) for k in ks], axis=1)
        begins = [k * hidden + block * deep for k in ks]
        slopes = jnp.concatenate([slope[:, b : b + deep] for b in begins], axis=1)
        dpre = (nn(ddown[...], down) * slopes.astype(F32)).astype(BF16)
        more = nt(dpre, up)
        if n == 0:
            acc[...] = more
        else:
            acc[...] += more
    kept[8].wait()

    def bottom(at):
        dx1 = ddown[at].astype(F32) + acc[at]
        dattn[at] = norm_back(dx1, hat1[at].astype(F32), scale1[at][:, :1], vectors[6:7]).astype(BF16)

    by_tokens(tokens, bottom)
    take = row_blocks(rows, narrow)
    for r in range(0, rows, take):
        some = pl.ds(OUT * narrow, narrow)
        weight = jnp.concatenate(
            [w[r : r + take, k // CORES, k % CORES, some].reshape(take * narrow, deep) for k in range(cols)], axis=1
        )
        dmixed[:, r * narrow : (r + take) * narrow] = nt(dattn[...], weight).astype(BF16)
    kept[0].wait()
    kept[1].wait()
    heads_back(q, dmixed, mixed, log, kv, mask, 0, front.pairs)
    grads = share_key_grads(sharing, kv, got, sem_dkv)
    for copy in grads:
        copy.start()
    for copy in grads:
        copy.wait()
    join_key_grads(kv, got)
    chunks = 2
    chunk = tokens // chunks

    def send_on(i):
        at = pl.ds(i * chunk, chunk)
        return pltpu.make_async_remote_copy(
            dx.at[at], next_hbm.at[at], sem_next.at[i, 0], sem_next.at[i, 1],
            device_id={"section": 1 - section}, device_id_type=MESH,
        )

    stay = pltpu.make_async_copy(start_hbm, next_hbm, sem_in.at[0])

    @pl.when(section == 1)
    def _():
        stay.start()

    for i in range(chunks):
        at = pl.ds(i * chunk, chunk)
        for k in range(cols):
            there = slice(k * deep, (k + 1) * deep)
            total = dattn[at, there].astype(F32)
            for j in range(3):
                total += nn(q[at] if j == 0 else kv[0, j - 1, at], front.matrix(QKV + j, k))
            dx[at, there] = total.astype(BF16)

        @pl.when(section == 1)
        def _(i=i):
            send_on(i).start()

    for n in range(len(turns) - 2, len(turns)):
        for copy in keep_act(n):
            copy.wait()
    for i in (2, 3, 6, 7, 9):
        kept[i].wait()
    streams.wait_sent(y_t)
    streams.wait_here()

    @pl.when(section == 1)
    def _():
        stay.wait()
        for i in range(chunks):
            send_on(i).wait_send()

    @pl.when(section == 0)
    def _():
        for i in range(chunks):
            send_on(i).wait_recv()


def middle(second_in, start, weight, vectors, shift, doc_query, doc_key, group):
    tokens, width = second_in.shape
    rows, highs, _, tall, deep = weight.shape
    cols, narrow, units = highs * CORES, width // rows, shift.shape[1]
    pairs, blocks = width // PAIR, units // cols // deep
    in_any = pl.BlockSpec(memory_space=pl.ANY)
    in_vmem = pl.BlockSpec(memory_space=pltpu.VMEM)
    dma = pltpu.SemaphoreType.DMA
    flat = shaped((tokens, width), BF16)
    thin = shaped((tokens, 128), F32)
    kv = shaped((group, 2, tokens, width), BF16)
    log = shaped((pairs, 2, tokens), F32)
    wide = shaped((tokens, units), BF16)
    turned = shaped((rows, narrow, tokens), BF16)
    half = cols if tokens * cols * deep <= 1 << 19 else max(1, cols // 2)

    def vmem(shape):
        return pltpu.VMEM(shape.shape, shape.dtype)

    whole = pltpu.VMEM((tokens, width), F32)
    return pl.pallas_call(
        functools.partial(middle_kernel, group=group),
        in_specs=[in_any] * 3 + [in_vmem] * 4,
        out_specs=[in_any] * 13,
        out_shape=[flat, flat, kv, flat, log, flat, flat, thin, flat, thin, wide, wide, turned],
        scratch_shapes=[
            vmem(weight), vmem(flat), vmem(flat), vmem(kv), vmem(flat), vmem(log),
            pltpu.VMEM((group * tokens, tokens), F32),
            whole, vmem(flat), whole, vmem(wide),
            pltpu.VMEM((2, tokens, half * deep), BF16),
            vmem(flat), vmem(flat), vmem(thin), vmem(thin), vmem(turned),
            pltpu.VMEM((max(1, group - 1), 2, tokens, width), BF16),
            dma((2 + 2 * blocks,)), dma((2,)), dma((max(1, group - 1), 2)), dma((max(1, group - 1), 2)), dma((10,)),
            dma((2, half)), dma((2, 2)), dma((rows, 2)),
        ],
        name="middle",
        compiler_params=pltpu.CompilerParams(collective_id=3, has_side_effects=True, vmem_limit_bytes=LOW_VMEM),
        cost_estimate=pl.CostEstimate(
            flops=72 * tokens * width * width, bytes_accessed=2 * tall * deep * rows * cols, transcendentals=0
        ),
    )(second_in, start, weight, vectors, shift, doc_query, doc_key)


STAGES = 3


def low_kernel(*refs, highs, rows, group):
    (ddown_hbm, act_hbm, x1_hbm, dpre_hbm, dattn_hbm, q_hbm, mixed_hbm, log_hbm, x_hbm, w_hbm, kv_hbm) = refs[:11]
    bias_doc_q, bias_doc_k, pre_ref, top_sums, feed_sums = refs[11:16]
    down_out, out_out, unit_out, qkv_out, small_out, landed, landing, high_landing = refs[16:24]
    (dattn, x, q, mixed, log, w_out, w_qkv, kv, dmixed, bias, dkv_got, dx, stage, small, left, right,
     work, got, got_high, from_row, from_wide, sem_in, sem_right, sem_core, sem_load, sem_high, sem_row, sem_kv, sem_out) = refs[24:]
    tokens, width = dattn.shape
    narrow, deep = stage.shape[-2:]
    dq, dkv = q, kv
    cols = highs * CORES

    sharing = Group(group)
    streams = Streams(landed, sem_out, sharing)

    units = act_hbm.shape[1]
    feed_pieces = units // cols // deep
    tail = small.shape[3]
    order = [("down", i) for i in range(feed_pieces)] + [("out", 0)]
    order += [("unit", i) for i in range(feed_pieces)] + [("qkv", 0), ("qkv", 1), ("qkv", 2), ("small", 0)]
    row_first = (("unit", 0),)
    pieces = [(stage.at[i % STAGES], narrow, order[i] not in row_first) for i in range(len(order) - 1)]
    pieces += [(small, tail, True)]

    def give(q, ref):
        name, i = order[q]
        value = ref[...]
        if name in ("down", "unit"):
            (down_out if name == "down" else unit_out)[0, :, i * deep : (i + 1) * deep] = value
        elif name == "out":
            out_out[0] = value
        elif name == "qkv":
            qkv_out[0, i] = value
        else:
            small_out[...] = value

    scatter = Scatter(
        pieces, (landing, work, got, high_landing, got_high, from_row, from_wide, sem_core, sem_load, sem_high, sem_row), highs, rows, give,
    )

    inputs = [
        (ddown_hbm, dattn),
        (x1_hbm, x),
        (dattn_hbm, dattn),
        (w_hbm.at[:, :, pl.ds(OUT * narrow, narrow)], w_out),
        (mixed_hbm, mixed),
        (q_hbm, q),
        (log_hbm, log),
        (kv_hbm, kv),
        (w_hbm.at[:, :, pl.ds(QKV * narrow, 3 * narrow)], w_qkv),
        (x_hbm, x),
    ]
    loads = [pltpu.make_async_copy(a, b, sem_in.at[i]) for i, (a, b) in enumerate(inputs)]
    early = 8

    key_grads = share_key_grads(sharing, kv, dkv_got, sem_kv)
    take = row_blocks(rows, narrow)

    def prepare():
        for load in loads[2:early]:
            load.wait()
        bias[...] = jnp.where(bias_doc_k[...] == bias_doc_q[...], 0.0, NEG_BIG).astype(BF16)

        @pl.loop(0, rows // take)
        def _(r):
            at = pl.ds(pl.multiple_of(r * take * narrow, take * narrow), take * narrow)
            dmixed[:, at] = nt(dattn[...], side_by_side(w_out[pl.ds(r * take, take)])).astype(BF16)

    def fill(slot, block, loaded=None):
        @pl.loop(0, cols)
        def _(k):
            grad = nn(left[...], block(k)).astype(BF16)
            stage[slot, :, lax.div(k, CORES), lax.rem(k, CORES)] = grad.reshape(rows, narrow, deep)

    def column(ref):
        return lambda k: ref[:, pl.ds(pl.multiple_of(k * deep, deep), deep)]

    def fetch(q):
        name, i = order[q]
        source = act_hbm if name == "down" else dpre_hbm
        return [
            pltpu.make_async_copy(
                source.at[:, pl.ds(k * feed_pieces * deep + i * deep, deep)],
                right.at[q % 2, :, pl.ds(k * deep, deep)],
                sem_right.at[q % 2, k],
            )
            for k in range(cols)
        ]

    def is_feed(q):
        return q < len(order) and order[q][0] in ("down", "unit")

    def make(q):
        name, i = order[q]
        slot = q % STAGES
        if q == 0:
            loads[0].wait()
            left[...] = dattn[...].T
            loads[2].start()
        if name in ("down", "unit"):
            if (name, i) == ("unit", 0):
                left[...] = x[...].T
                loads[-1].start()
            for copy in fetch(q):
                copy.wait()
            if is_feed(q + 1):
                for copy in fetch(q + 1):
                    copy.start()
            fill(slot, column(right.at[q % 2]))
        elif name == "out":
            if is_feed(q + 1):
                for copy in fetch(q + 1):
                    copy.start()
            left[...] = mixed[...].T
            fill(slot, column(dattn))
        elif name == "qkv":
            if i == 0:
                loads[-1].wait()
            left[...] = grads_of(i).T
            fill(slot, column(x))
        else:
            small_sums()

    pairs = width // PAIR

    def heads(first, count):
        heads_back(q, dmixed, mixed, log, kv, bias, first, count)

    def exchange():
        for copy in key_grads:
            copy.start()

    def join():
        for copy in key_grads:
            copy.wait()
        for load in loads[early:-1]:
            load.wait()
        join_key_grads(kv, dkv_got)

    def grads_of(j):
        return dq[...] if j == 0 else dkv[0, j - 1]

    def input_gradient():
        for k in range(cols):
            at = slice(k * deep, (k + 1) * deep)
            total = dattn[:, at].astype(F32)
            for j in range(3):
                total += nn(grads_of(j), w_qkv[:, k, j * narrow : (j + 1) * narrow].reshape(width, deep))
            for piece in range(0, deep, min(narrow, deep)):
                r, inside = divmod(k * deep + piece, narrow)
                dx[r, inside : inside + min(narrow, deep)] = total[:, piece : piece + min(narrow, deep)].T.astype(BF16)

    def small_sums():
        vectors = [column_sum(grads_of(j).astype(F32)) for j in (0, 2)]
        vectors += [feed_sums[0:2], top_sums[0:2], feed_sums[2:3], top_sums[2:3]]
        vectors = jnp.concatenate(vectors, axis=0)
        vectors = vectors.astype(BF16)
        small[...] = jnp.zeros_like(small)
        lines = pre_ref.shape[1] // cols // deep
        for r in range(rows):
            for k in range(cols):
                small[r, k // CORES, k % CORES, 0:8, 0:narrow] = vectors[:, r * narrow : (r + 1) * narrow]
                for i in range(lines):
                    at = (k * lines + i) * deep
                    small[r, k // CORES, k % CORES, 8 + i : 9 + i] = pre_ref[:, at : at + deep].astype(BF16)

    share = max(1, pairs // 8)

    def between(tick):
        if tick == 1:
            prepare()
        if 2 <= tick < 9:
            heads((tick - 2) * share, share if tick < 8 else pairs - 6 * share)
        if tick == 8:
            exchange()
        if tick == 9:
            join()
        if tick + 1 < len(order):
            make(tick + 1)
        if tick == 9:
            input_gradient()
            streams.start(dx)

    for i, load in enumerate(loads[:-1]):
        if i != 2:
            load.start()
    for copy in fetch(0):
        copy.start()
    greet((scatter.high, scatter.row), ("core",), sharing.members(), streams.sources())
    loads[1].wait()
    make(0)
    scatter.run(between)
    streams.wait_sent(dx)
    streams.wait_here()


def low_back(ddown, act, x1_bf, dpre, dattn, query, mixed, log_total, x, weight, shared, doc_query, doc_key, pre_sum, top_sums, feed_sums):
    tokens, width = dattn.shape
    rows, cols, _, deep = weight.shape
    narrow = width // rows
    units = act.shape[1]
    feed_rows = narrow * units // cols // deep
    highs, group = cols // CORES, shared.shape[0]
    keys = group * tokens
    apart = (rows, highs, CORES)
    tail = 16
    lines = 8 + pre_sum.shape[1] // cols // deep
    assert lines <= tail and narrow <= deep
    count = 2 * (feed_rows // narrow) + 5
    wide = 1
    steps = 4 + highs - 1 + rows - 1
    slots = min(count, steps)
    in_any = pl.BlockSpec(memory_space=pl.ANY)
    in_vmem = pl.BlockSpec(memory_space=pltpu.VMEM)
    ways = {2: 1}
    block = (rows, narrow, deep)
    dma = pltpu.SemaphoreType.DMA
    args = [ddown, act, x1_bf, dpre, dattn, query, mixed, log_total, x, weight, shared]
    *outs, _, _ = pl.pallas_call(
        functools.partial(low_kernel, highs=highs, rows=rows, group=group),
        in_specs=[in_any] * len(args) + [in_vmem] * 5,
        out_specs=[in_vmem] * 5 + [in_any] * 3,
        out_shape=[
            shaped((1, narrow, units // cols), BF16),
            shaped((1, narrow, deep), BF16),
            shaped((1, narrow, units // cols), BF16),
            shaped((1, 3, narrow, deep), BF16),
            shaped((tail, deep), BF16),
            shaped((rows, narrow, tokens), BF16),
            shaped((count, highs) + block, BF16),
            shaped((count, highs - 1, ways.get(highs, 2)) + block, BF16),
        ],
        scratch_shapes=[
            pltpu.VMEM((tokens, width), BF16),
            pltpu.VMEM((tokens, width), BF16),
            pltpu.VMEM((tokens, width), BF16),
            pltpu.VMEM((tokens, width), BF16),
            pltpu.VMEM(log_total.shape, F32),
            pltpu.VMEM((rows, cols, narrow, deep), BF16),
            pltpu.VMEM((rows, cols, 3 * narrow, deep), BF16),
            pltpu.VMEM((group, 2, tokens, width), BF16),
            pltpu.VMEM((tokens, width), BF16),
            pltpu.VMEM((keys, tokens), BF16),
            pltpu.VMEM((group - 1, 2, tokens, width), BF16),
            pltpu.VMEM((rows, narrow, tokens), BF16),
            pltpu.VMEM((STAGES,) + apart + (narrow, deep), BF16),
            pltpu.VMEM(apart + (tail, deep), BF16),
            pltpu.VMEM((width, tokens), BF16),
            pltpu.VMEM((2, tokens, cols * deep), BF16),
            pltpu.VMEM((slots, highs) + block, BF16),
            pltpu.VMEM((2, highs) + block, BF16),
            pltpu.VMEM((2, ways.get(highs, 2)) + block, BF16),
            pltpu.VMEM((count - wide, rows - 1, ways.get(rows, 2), narrow, deep), BF16),
            pltpu.VMEM((wide, rows - 1, ways.get(rows, 2), highs, narrow, deep), BF16),
            dma((10,)),
            dma((2, cols)),
            dma((count, highs, 2)),
            dma((count, highs, 2)),
            dma((count, highs - 1, 2, 3)),
            dma((count, rows - 1, 2, 2)),
            dma((max(1, group - 1), 2)),
            dma((rows, 2)),
        ],
        name="low_back",
        compiler_params=pltpu.CompilerParams(collective_id=1, has_side_effects=True, vmem_limit_bytes=LOW_VMEM),
        cost_estimate=pl.CostEstimate(
            flops=64 * tokens * width * width, bytes_accessed=12 * width * units, transcendentals=0
        ),
    )(*args, doc_query, doc_key, pre_sum, top_sums, feed_sums)
    return outs


def finish_kernel(down, out, unit, qkv, small, first, second, *outs):
    layer_out, input_grad, qkv_out, out_out, unit_out, down_out, bias_out, width_out, gain_out = outs
    for ref, to in ((down, down_out), (out, out_out), (unit, unit_out), (qkv, qkv_out)):
        to[...] = ref[...].astype(F32)
    rows, narrow, tokens = first.shape
    for ref, to in ((first, layer_out), (second, input_grad)):
        per = rows // to.shape[1]
        for r in range(rows):
            to[0, r // per, :, r % per * tokens : (r % per + 1) * tokens] = ref[r].astype(F32)
    values = small[...].astype(F32)
    width_out[0] = values[0:6, :narrow]
    gain_out[0] = values[6:8, :narrow]
    deep = values.shape[1]
    for i in range(bias_out.shape[1] // deep):
        bias_out[:, i * deep : (i + 1) * deep] = values[8 + i : 9 + i]


def finish(down, out, unit, qkv, small, first, second, micro):
    rows, narrow, tokens = first.shape
    stream = shaped((1, micro, narrow, rows // micro * tokens), F32)
    grads = [shaped(grad.shape, F32) for grad in (qkv, out, unit, down)]
    rest = [shaped((1, down.shape[2]), F32), shaped((1, 6, narrow), F32), shaped((1, 2, narrow), F32)]
    return pl.pallas_call(
        finish_kernel,
        out_shape=[stream, stream, *grads, *rest],
        name="finish",
        compiler_params=pltpu.CompilerParams(vmem_limit_bytes=VMEM_BYTES),
    )(down, out, unit, qkv, small, first, second)


def local(tokens_in, doc_ids, cotangent, qkv_master, out_master, unit_master, down_master, unit_bias, width_bias, norm_gain):
    at = Layout(tokens_in, doc_ids)
    rows, cols, deep = at.rows, at.cols, out_master.shape[2]

    second_in, start, weights, vectors, unit_shift, doc_query, doc_key = first_forward(
        tokens_in, cotangent, qkv_master, out_master, unit_master, down_master, unit_bias, width_bias, norm_gain, doc_ids,
        rows, cols // CORES, at.group,
    )
    (
        dy, query, shared, mixed, log_total, x1_bf, hat_one, scale_one, hat_two, scale_two, act, slope, stream,
    ) = middle(second_in, start, weights, vectors, unit_shift, doc_query, doc_key, at.group)
    weights = weights.reshape(rows, cols, -1, deep)
    ddown, dattn, dpre, pre_sum, top_sums, feed_sums = feed_back(
        dy, hat_two, scale_two, hat_one, scale_one, slope, weights, vectors
    )
    *grads, input_grad = low_back(
        ddown, act, x1_bf, dpre, dattn, query, mixed, log_total, second_in, weights, shared, doc_query, doc_key,
        pre_sum, top_sums, feed_sums,
    )
    return finish(*grads, stream, input_grad, at.micro)


def solution(mesh):
    sections, rows, cols = (mesh.shape[name] for name in ("section", "row", "col"))
    fine = Mesh(
        mesh.devices.reshape(sections, rows, cols // CORES, CORES), ("section", "row", "high", "core")
    )
    col = ("high", "core")
    block = P("section", "row", col)
    stream = P("section", None, "row", col)
    return jax.shard_map(
        local,
        mesh=fine,
        in_specs=(
            P(None, "row", col),
            P(None, col, None),
            P(None, "row", col),
            P("section", None, "row", col),
            block,
            block,
            block,
            P("section", col),
            P("section", None, "row"),
            P("section", None, "row"),
        ),
        out_specs=(
            stream,
            stream,
            stream,
            block,
            block,
            block,
            P("section", col),
            P("section", None, "row"),
            P("section", None, "row"),
        ),
        check_vma=False,
    )
```

```python
import functools

import jax
import jax.numpy as jnp
from jax import lax
from jax.experimental import pallas as pl
from jax.experimental.pallas import tpu as pltpu
from jax.sharding import Mesh
from jax.sharding import PartitionSpec as P

HD = 64
EPSILON = 1e-05
NEG_BIG = -1e30
CORES = 2
PAIR = 128
PLANE = ("row", "high", "core")
MESH = pl.DeviceIdType.MESH

QKV, OUT, UNIT = 0, 3, 4

F32 = jnp.float32
BF16 = jnp.bfloat16
VMEM_BYTES = 56 * 1024 * 1024
LOW_VMEM = 65200 * 1024


def nn(left, right):
    return lax.dot_general(left, right, (((1,), (0,)), ((), ())), preferred_element_type=F32)


def nt(left, right):
    return lax.dot_general(left, right, (((1,), (1,)), ((), ())), preferred_element_type=F32)


def shaped(shape, dtype):
    return jax.ShapeDtypeStruct(shape, dtype)


def row_blocks(rows, narrow):
    take = min(rows, max(1, 256 // narrow))
    while rows % take:
        take += 1
    return take


def side_by_side(blocks):
    take, cols, narrow, deep = blocks.shape
    return jnp.concatenate([blocks[:, k].reshape(take * narrow, deep) for k in range(cols)], axis=1)


def head_lanes(shape, axis):
    return lax.broadcasted_iota(jnp.int32, shape, axis) < HD


def both_heads(array):
    lanes = head_lanes(array.shape, 1)
    return jnp.concatenate([jnp.where(lanes, array, 0), jnp.where(lanes, 0, array)], axis=0)


def own_rows(array):
    tokens = array.shape[1] // 2
    return jnp.where(head_lanes((PAIR, tokens), 0), array[:, :tokens], array[:, tokens:])


def pair_front(query, keys, values, bias_ref):
    tokens = query.shape[0]
    bias = bias_ref[...]
    scores = nt(keys, both_heads(query)) + jnp.concatenate([bias, bias], axis=1)
    top = jnp.max(scores, axis=0, keepdims=True)
    expo = jnp.exp(scores - top)
    total = jnp.sum(expo, axis=0, keepdims=True)
    mixed = own_rows(nn(values.T, expo.astype(BF16)) / total)
    log_row = top + jnp.log(total)
    return mixed.T.astype(BF16), [log_row[:, :tokens], log_row[:, tokens:]]


def pair_back(query, grad, mixed, log_rows, keys, values, bias_ref, tile):
    tokens = query.shape[0]
    keys_t = keys.T
    lanes = head_lanes((tile, PAIR), 1)
    low_t = head_lanes(keys_t.shape, 0)
    products = (grad.astype(F32) * mixed.astype(F32)).T
    grad_query = []
    grad_key = jnp.zeros(keys.shape, F32)
    grad_value = jnp.zeros(keys.shape, F32)
    for at in range(0, tokens, tile):
        some = slice(at, at + tile)
        grad_some = jnp.zeros((PAIR, tile), F32)
        for h in range(2):
            here = lanes if h == 0 else ~lanes
            mine = jnp.where(here, query[some], 0)
            grad_mine = jnp.where(here, grad[some], 0)
            inner = jnp.sum(products[h * HD : (h + 1) * HD, some], axis=0, keepdims=True)
            prob = jnp.exp(nt(keys, mine) + bias_ref[:, some] - log_rows[h][:, some])
            grad_value += nn(prob.astype(BF16), grad_mine)
            grad_scores = (prob * (nt(values, grad_mine) - inner)).astype(BF16)
            grad_key += nn(grad_scores, mine)
            keys_mine = jnp.where(low_t if h == 0 else ~low_t, keys_t, 0)
            grad_some += nn(keys_mine, grad_scores)
        grad_query.append(grad_some)
    grad_query = jnp.concatenate(grad_query, axis=1).T.astype(BF16) * HD**-0.5
    return grad_query, grad_key.astype(BF16), grad_value.astype(BF16)


def normed_of(hidden):
    center = hidden - jnp.mean(hidden, axis=1, keepdims=True)
    scale = lax.rsqrt(jnp.mean(center * center, axis=1, keepdims=True) + EPSILON)
    return center * scale, scale


def norm_back(grad_out, normed, scale, gain):
    scaled = grad_out * gain
    first = jnp.mean(scaled, axis=1, keepdims=True)
    second = jnp.mean(scaled * normed, axis=1, keepdims=True)
    return scale * (scaled - first - normed * second)


SLICE = 128


def by_tokens(tokens, body):
    step = min(SLICE, tokens)
    for at in range(0, tokens, step):
        body(pl.ds(at, step))


def gelu_parts(pre):
    below = 0.5 * (1.0 + lax.erf(pre * 0.5**0.5))
    return pre * below, below + pre * jnp.exp(-0.5 * pre * pre) * (2.0 * jnp.pi) ** -0.5


def column_sum(value):
    return jnp.sum(value, axis=0, keepdims=True)


class Layout:
    def __init__(self, tokens_in, doc_ids):
        self.micro, self.narrow, _ = tokens_in.shape
        self.seq_here, self.seq_len = doc_ids.shape[1:]
        self.rows = lax.axis_size("row")
        self.cols = lax.axis_size("high") * CORES
        self.width = self.narrow * self.rows
        self.places = self.rows * CORES
        self.sequences = self.micro * self.seq_here * CORES
        self.group = self.places // self.sequences
        self.part = self.seq_len // self.group
        self.row = lax.axis_index("row")
        place = self.row * CORES + lax.axis_index("core")
        self.sequence = place // self.group
        self.position = place % self.group
        self.block = (self.sequence // CORES) * self.group + self.position


class Line:
    def __init__(self, axis, size):
        self.axis, self.size, self.here = axis, size, lax.axis_index(axis)

    def sends(self, step):
        last = self.size - 1
        return (
            (True, (self.here < step) & (self.here < last), self.size - step + self.here, self.here > 0),
            (False, (last - self.here < step) & (self.here > 0), step - self.size + self.here, self.here < last),
        )

    def gets(self, step):
        last = self.size - 1
        return (
            (True, (self.here >= 1) & (self.here <= step)),
            (False, (last - self.here >= 1) & (last - self.here <= step)),
        )

    def neighbour(self, right):
        return {self.axis: self.here + (1 if right else -1)}


def greet(lines, pairs, members=(), some=()):
    barrier = pltpu.get_barrier_semaphore()
    count = 0
    for line in lines:
        for right, there in ((True, line.here < line.size - 1), (False, line.here > 0)):

            @pl.when(there)
            def _(line=line, right=right):
                pl.semaphore_signal(barrier, 1, device_id=line.neighbour(right), device_id_type=MESH)

            count = count + there.astype(jnp.int32)
    for axis in pairs:
        pl.semaphore_signal(barrier, 1, device_id={axis: 1 - lax.axis_index(axis)}, device_id_type=MESH)
        count = count + 1
    for member in members:
        pl.semaphore_signal(barrier, 1, device_id=member, device_id_type=MESH)
        count = count + 1
    for member, there in some:

        @pl.when(there)
        def _(member=member):
            pl.semaphore_signal(barrier, 1, device_id=member, device_id_type=MESH)

        count = count + there.astype(jnp.int32)
    pl.semaphore_wait(barrier, count)


def add_into(target, other):
    lead = target.shape[:-2]
    rows = target.shape[-2]
    total = 1
    for size in lead:
        total *= size
    if total == 1:
        target[...] = target[...] + other[...]
        return

    @pl.loop(0, total)
    def _(i):
        index = []
        for size in reversed(lead):
            index.insert(0, lax.rem(i, size))
            i = lax.div(i, size)
        index = tuple(index)
        target[index] = target[index] + other[index]


class Scatter:
    def __init__(self, pieces, refs, highs, rows, give):
        self.pieces, self.give = pieces, give
        (self.landing, self.work, self.got, self.from_high, self.got_high, self.from_row, self.from_wide, *sems) = refs
        self.sem_core, self.sem_load, self.sem_high, self.sem_row = sems
        self.high, self.row = Line("high", highs), Line("row", rows)
        self.core = lax.axis_index("core")
        self.slots = self.work.shape[0]
        self.sent = [[] for _ in pieces]
        self.place, wide, thin = [], 0, 0
        for _, _, row_last in pieces:
            self.place.append(thin if row_last else wide)
            thin, wide = thin + row_last, wide + (not row_last)

    def slot(self, q):
        return q % self.slots

    def cut(self, q, ref):
        return ref.at[..., pl.ds(0, self.pieces[q][1]), :]

    def to_core(self, q, y):
        return pltpu.make_async_remote_copy(
            self.pieces[q][0].at[:, y, 1 - self.core],
            self.cut(q, self.landing.at[q, y]),
            self.sem_core.at[q, y, 0],
            self.sem_core.at[q, y, 1],
            device_id={"core": 1 - self.core},
            device_id_type=MESH,
        )

    def load(self, q, y):
        return pltpu.make_async_copy(
            self.pieces[q][0].at[:, y, self.core],
            self.cut(q, self.work.at[self.slot(q), y]),
            self.sem_load.at[q, y, 0],
        )

    def fetch(self, q, y):
        return pltpu.make_async_copy(
            self.cut(q, self.landing.at[q, y]), self.cut(q, self.got.at[q % 2, y]), self.sem_load.at[q, y, 1]
        )

    def begin(self, q):
        if q >= self.slots:
            self.finish_sends(q - self.slots)
        for y in range(self.high.size):
            self.to_core(q, y).start()
            self.load(q, y).start()

    def arrive(self, q):
        for y in range(self.high.size):
            self.to_core(q, y).wait()
            self.fetch(q, y).start()

    def merge(self, q):
        for y in range(self.high.size):
            self.load(q, y).wait()
            self.fetch(q, y).wait()
            add_into(self.cut(q, self.work.at[self.slot(q), y]), self.cut(q, self.got.at[q % 2, y]))

    def lines(self, q):
        return (self.high, self.row) if self.pieces[q][2] else (self.row, self.high)

    def block(self, q, line, i):
        first = line is self.lines(q)[0]
        if line is self.high:
            ref = self.work.at[self.slot(q), i, slice(None) if first else self.row.here]
        else:
            ref = self.work.at[self.slot(q), slice(None) if first else self.high.here, i]
        return self.cut(q, ref)

    def arrival(self, q, line, step, right):
        way = 0 if line.size == 2 or right else 1
        first = line is self.lines(q)[0]
        if line is self.high:
            index = (slice(None),) if first else (0,)
            return (
                self.cut(q, self.from_high.at[(q, step - 1, way) + index]),
                self.cut(q, self.got_high.at[(way,) + index]),
            )
        ref = (self.from_wide if first else self.from_row).at[self.place[q], step - 1, way]
        return (self.cut(q, ref),) * 2

    def copy(self, q, line, step, right, i):
        sems = (self.sem_high if line is self.high else self.sem_row).at[q, step - 1, 0 if right else 1]
        return pltpu.make_async_remote_copy(
            self.block(q, line, i),
            self.arrival(q, line, step, right)[0],
            sems.at[0],
            sems.at[1],
            device_id=line.neighbour(right),
            device_id_type=MESH,
        )

    def push(self, q, line, step):
        for right, there, i, more in line.sends(step):

            @pl.when(there)
            def _(right=right, i=i, more=more):
                if step > 1:

                    @pl.when(more)
                    def _():
                        add_into(self.block(q, line, i), self.arrival(q, line, step - 1, right)[1])

                self.copy(q, line, step, right, i).start()

            self.sent[q].append((line, step, right, there, i))

    def pull(self, q, line, step):
        for right, there in line.gets(step):

            @pl.when(there)
            def _(right=right):
                self.copy(q, line, step, right, 0).wait_recv()
                if line is self.high:
                    landed, got = self.arrival(q, line, step, right)
                    way = 0 if line.size == 2 or right else 1
                    fetch = pltpu.make_async_copy(landed, got, self.sem_high.at[q, step - 1, way, 2])
                    fetch.start()
                    fetch.wait()

    def close(self, q, line):
        for right, there in line.gets(line.size - 1):

            @pl.when(there)
            def _(right=right):
                add_into(self.block(q, line, line.here), self.arrival(q, line, line.size - 1, right)[1])

    def finish_sends(self, q):
        for line, step, right, there, i in self.sent[q]:

            @pl.when(there)
            def _(line=line, step=step, right=right, i=i):
                self.copy(q, line, step, right, i).wait_send()

        self.sent[q] = []

    def stages(self, q):
        lines = [(line, step) for line in self.lines(q) for step in range(1, line.size)]

        def merge():
            self.merge(q)
            self.push(q, *lines[0])

        stages = [lambda: self.begin(q), lambda: self.arrive(q), merge]
        for n, (line, step) in enumerate(lines):

            def one(n=n, line=line, step=step):
                self.pull(q, line, step)
                if step == line.size - 1:
                    self.close(q, line)
                if n + 1 < len(lines):
                    self.push(q, *lines[n + 1])
                else:
                    self.give(q, self.block(q, line, line.here))

            if line is self.high and step == 1:
                stages.append(lambda: None)
            stages.append(one)
        return stages

    def run(self, between):
        stages = [self.stages(q) for q in range(len(self.pieces))]
        depth, count = len(stages[0]), len(stages)
        for tick in range(count + depth - 1):
            alive = range(max(0, tick - depth + 1), min(tick + 1, count))
            for q in alive:
                stages[q][tick - q]()
            between(tick)
        for q in range(count):
            self.finish_sends(q)


class Spread:
    def __init__(self, axis, size):
        self.axis, self.size, self.here = axis, size, lax.axis_index(axis)

    def sends(self, step):
        last = self.size - 1
        return (
            (True, (self.here < last) & (self.here >= step - 1), self.here - step + 1),
            (False, (self.here > 0) & (self.here + step - 1 <= last), self.here + step - 1),
        )

    def gets(self, step):
        last = self.size - 1
        return ((True, self.here >= step), (False, self.here + step <= last))

    def neighbour(self, right):
        return {self.axis: self.here + (1 if right else -1)}


AHEAD = 2


class Gather:
    def __init__(self, pieces, sems, highs, rows):
        self.pieces = pieces
        self.sem_row, self.sem_high, self.sem_core, self.sem_one = sems
        self.row, self.high = Spread("row", rows), Spread("high", highs)
        self.core = lax.axis_index("core")
        self.sent = []

    def block(self, q, line, i):
        ref, first, count, row_first = self.pieces[q]
        some = pl.ds(first, count)
        if line is self.row:
            return ref.at[i, self.high.here if row_first else slice(None), self.core, some]
        return ref.at[slice(None) if row_first else self.row.here, i, self.core, some]

    def copy(self, q, line, step, right, i):
        sems = (self.sem_row if line is self.row else self.sem_high).at[q, step - 1, 0 if right else 1]
        ref = self.block(q, line, i)
        return pltpu.make_async_remote_copy(
            ref, ref, sems.at[0], sems.at[1], device_id=line.neighbour(right), device_id_type=MESH
        )

    def one(self, q, right, i):
        ref, first, count, _ = self.pieces[q]
        ref = ref.at[i, self.high.here, self.core, pl.ds(first, count)]
        sems = self.sem_one.at[q, i, 0 if right else 1]
        return pltpu.make_async_remote_copy(
            ref, ref, sems.at[0], sems.at[1], device_id=self.high.neighbour(right), device_id_type=MESH
        )

    def start(self, there, copy):
        @pl.when(there)
        def _():
            copy().start()

        self.sent.append((there, copy))

    def over(self, q, i, there=True):
        for right, also, _ in self.high.sends(1):
            self.start(also & there, functools.partial(self.one, q, right, i))

    def push(self, q, line, step):
        if line is self.high and step == 1 and self.pieces[q][3]:
            return
        for right, there, i in line.sends(step):
            self.start(there, functools.partial(self.copy, q, line, step, right, i))

    def pull(self, q, line, step):
        row_first = self.pieces[q][3]
        for right, there in line.gets(step):

            @pl.when(there)
            def _(right=right):
                if line is self.high and step == 1 and row_first:
                    for i in range(self.row.size):
                        self.one(q, right, i).wait_recv()
                else:
                    self.copy(q, line, step, right, line.here).wait_recv()

            if line is self.row and row_first:
                self.over(q, line.here - step if right else line.here + step, there)

    def to_core(self, q):
        ref, first, count, _ = self.pieces[q]
        ref = ref.at[:, :, self.core, pl.ds(first, count)]
        return pltpu.make_async_remote_copy(
            ref, ref, self.sem_core.at[q, 0], self.sem_core.at[q, 1],
            device_id={"core": 1 - self.core}, device_id_type=MESH,
        )

    def stages(self, q):
        first, second = (self.row, self.high) if self.pieces[q][3] else (self.high, self.row)
        def begin():
            self.push(q, first, 1)
            if first is self.row:
                self.over(q, self.row.here)

        steps = [begin] + [lambda: None] * AHEAD
        lines = [(first, i) for i in range(1, first.size)] + [(second, i) for i in range(1, second.size)]
        for n, (line, step) in enumerate(lines):

            def one(n=n, line=line, step=step):
                self.pull(q, line, step)
                if n + 1 < len(lines):
                    self.push(q, *lines[n + 1])
                else:
                    self.to_core(q).start()

            steps.append(lambda: None)
            steps.append(one)
        steps.append(lambda: self.to_core(q).wait())
        return steps

    def run(self, between):
        stages = [self.stages(q) for q in range(len(self.pieces))]
        depth, count = len(stages[0]), len(stages)
        for tick in range(count + depth - 1):
            for q in range(max(0, tick - depth + 1), min(tick + 1, count)):
                stages[q][tick - q]()
            between(tick, tick - depth + 1)

    def finish(self):
        for there, copy in self.sent:

            @pl.when(there)
            def _(copy=copy):
                copy().wait_send()


class Group:
    def __init__(self, size):
        self.size = size
        self.place = lax.axis_index("row") * CORES + lax.axis_index("core")
        self.position = lax.rem(self.place, size)

    def member(self, step):
        other = self.place - self.position + lax.rem(self.position + step, self.size)
        return {"row": lax.div(other, CORES), "core": lax.rem(other, CORES)}

    def members(self):
        return [self.member(step) for step in range(1, self.size)]


class Front:
    def __init__(self, w, vectors, shift, x, q, kv, mixed, mask, x1, x1_bf, acc, log=None):
        self.w, self.vectors, self.shift, self.x, self.q, self.kv = w, vectors, shift, x, q, kv
        self.mixed, self.mask, self.x1, self.x1_bf, self.acc, self.log = mixed, mask, x1, x1_bf, acc, log
        self.tokens, self.width = x.shape
        self.rows, self.highs, _, _, self.deep = w.shape
        self.cols = self.highs * CORES
        self.narrow = self.width // self.rows
        self.group = kv.shape[0]
        self.pairs = self.width // PAIR
        self.blocks = shift.shape[1] // self.cols // self.deep

    def matrix(self, block, k):
        at = pl.ds(block * self.narrow, self.narrow)
        return self.w[:, k // CORES, k % CORES, at].reshape(self.width, self.deep)

    def project(self, j):
        take = row_blocks(self.rows, self.narrow)
        for r in range(0, self.rows, take):
            at = slice(r * self.narrow, (r + take) * self.narrow)
            some = pl.ds((QKV + j) * self.narrow, self.narrow)
            weight = jnp.concatenate(
                [
                    self.w[r : r + take, k // CORES, k % CORES, some].reshape(take * self.narrow, self.deep)
                    for k in range(self.cols)
                ],
                axis=1,
            )
            out = nt(self.x[...], weight)
            if j == 0:
                self.q[:, at] = ((out + self.vectors[0:1, at]) * HD**-0.5).astype(BF16)
            elif j == 1:
                self.kv[0, 0, :, at] = out.astype(BF16)
            else:
                self.kv[0, 1, :, at] = (out + self.vectors[1:2, at]).astype(BF16)

    def attend(self, first, count):
        @pl.loop(first, first + count)
        def _(p):
            at = pl.ds(pl.multiple_of(p * PAIR, PAIR), PAIR)
            keys = jnp.concatenate([self.kv[i, 0, :, at] for i in range(self.group)], axis=0)
            values = jnp.concatenate([self.kv[i, 1, :, at] for i in range(self.group)], axis=0)
            mixed, log_rows = pair_front(self.q[:, at], keys, values, self.mask)
            self.mixed[:, at] = mixed
            if self.log is not None:
                for h in range(2):
                    self.log[p, h : h + 1] = log_rows[h]

    def out(self):
        for k in range(self.cols):
            at = slice(k * self.deep, (k + 1) * self.deep)
            self.acc[:, at] = nn(self.mixed[...], self.matrix(OUT, k))

    def norm_one(self, keep=None):
        def some(at):
            attn = self.acc[at] + self.vectors[2:3]
            normed, scale = normed_of(self.x[at].astype(F32) + attn)
            x1 = normed * self.vectors[6:7] + self.vectors[3:4]
            self.x1[at] = x1
            self.x1_bf[at] = x1.astype(BF16)
            if keep is not None:
                keep(at, normed, scale)

        by_tokens(self.tokens, some)

    def feed(self, block, ks, start, keep=None, at=slice(None)):
        up = jnp.concatenate([self.matrix(UNIT + block, k) for k in ks], axis=1)
        down = jnp.concatenate([self.matrix(UNIT + self.blocks + block, k) for k in ks], axis=1)
        hidden = self.blocks * self.deep
        begins = [k * hidden + block * self.deep for k in ks]
        shift = jnp.concatenate([self.shift[:, b : b + self.deep] for b in begins], axis=1)
        act, slope = gelu_parts(nn(self.x1_bf[at], up) + shift)
        act = act.astype(BF16)
        if keep is not None:
            keep(act, slope.astype(BF16))
        more = nt(act, down)
        if start:
            self.acc[at] = more
        else:
            self.acc[at] += more

    def norm_two(self, at, keep=None):
        normed, scale = normed_of(self.x1[at] + (self.acc[at] + self.vectors[4:5]))
        if keep is not None:
            keep(at, normed, scale)
        return normed * self.vectors[7:8] + self.vectors[5:6]


def share_keys(group, kv, sems):
    def copy(step):
        return pltpu.make_async_remote_copy(
            kv.at[0], kv.at[step], sems.at[step - 1, 0], sems.at[step - 1, 1],
            device_id=group.member(step), device_id_type=MESH,
        )

    return [copy(step) for step in range(1, group.size)]


def first_kernel(*refs, highs, rows, group, micro, seq_here, seq_len):
    (tokens_hbm, cot_hbm, qkv_ref, out_ref, unit_ref, down_ref, unit_bias, width_bias, gain, docs) = refs[:10]
    (next_hbm, start_ref, w_hbm, vectors, shift, doc_q, doc_k) = refs[10:17]
    (w, small, turned, x, q, kv, mixed, mask, x1, x1_bf, acc, y,
     sem_row, sem_high, sem_core, sem_one, sem_x, sem_kv, sem_y, sem_w, sem_next) = refs[17:]
    tokens, width = x.shape
    narrow, deep = width // rows, w.shape[-1]
    cols = highs * CORES
    hidden = unit_ref.shape[2]
    blocks = hidden // deep
    row, high, core = lax.axis_index("row"), lax.axis_index("high"), lax.axis_index("core")
    section = lax.axis_index("section")
    sharing = Group(group)
    sequence = lax.div(sharing.place, group)
    front = Front(w, vectors, shift, x, q, kv, mixed, mask, x1, x1_bf, acc)

    w[row, high, core, 0 : 3 * narrow] = qkv_ref[0].reshape(3 * narrow, deep).astype(BF16)
    w[row, high, core, 3 * narrow : 4 * narrow] = out_ref[0].astype(BF16)
    for i in range(blocks):
        at = slice(i * deep, (i + 1) * deep)
        for j, ref in enumerate((unit_ref, down_ref)):
            first = (UNIT + j * blocks + i) * narrow
            w[row, high, core, first : first + narrow] = ref[0, :, at].astype(BF16)
    small[row, high, core, 0:6, 0:narrow] = width_bias[0]
    small[row, high, core, 6:8, 0:narrow] = gain[0]
    for i in range(blocks):
        small[row, high, core, 8 + i : 9 + i] = unit_bias[:, i * deep : (i + 1) * deep]
    lines = seq_len // deep
    for m in range(micro):
        for i in range(seq_here):
            for j in range(lines):
                at = 8 + blocks + (m * seq_here + i) * lines + j
                small[row, high, core, at : at + 1] = docs[m, i : i + 1, j * deep : (j + 1) * deep].astype(F32)

    def goes(j):
        place = ((j // group) * CORES + core) * group + j % group
        return lax.div(place, CORES), lax.rem(place, CORES)

    source_core = lax.rem(sequence, CORES)
    mine_too = source_core == core

    def block_of(ref, j):
        m, rest = divmod(j // group, seq_here)
        return ref.at[m, :, pl.ds(rest * seq_len + (j % group) * tokens, tokens)]

    def send_block(ref, j):
        there_row, there_core = goes(j)
        return pltpu.make_async_remote_copy(
            block_of(ref, j), turned.at[row], sem_x.at[j, 0], sem_x.at[row, 1],
            device_id={"row": there_row, "core": there_core}, device_id_type=MESH,
        )

    def is_here(j):
        there_row, there_core = goes(j)
        return (there_row == row) & (there_core == core)

    barrier = pltpu.get_barrier_semaphore()
    count = 0
    for line in (Spread("row", rows), Spread("high", highs)):
        for right, there in ((True, line.here < line.size - 1), (False, line.here > 0)):

            @pl.when(there)
            def _(line=line, right=right):
                pl.semaphore_signal(barrier, 1, device_id=line.neighbour(right), device_id_type=MESH)

            count = count + there.astype(jnp.int32)
    others = [{"core": 1 - core}, {"section": 1 - section}] + sharing.members()
    for other in others:
        pl.semaphore_signal(barrier, 1, device_id=other, device_id_type=MESH)
    for r in range(rows):

        @pl.when(jnp.logical_not(mine_too & (row == r)))
        def _(r=r):
            pl.semaphore_signal(barrier, 1, device_id={"row": r, "core": source_core}, device_id_type=MESH)

    pl.semaphore_wait(barrier, count + len(others) + rows - mine_too.astype(jnp.int32))

    row_first = [True] * (4 + 2 * blocks)
    row_first[4 + blocks] = False
    order = [0, 1, 2, 3] + [UNIT + j * blocks + i for i in range(blocks) for j in range(2)]
    pieces = [(small, 0, small.shape[3], True)]
    pieces += [(w, i * narrow, narrow, row_first[n]) for n, i in enumerate(order)]
    gather = Gather(pieces, (sem_row, sem_high, sem_core, sem_one), highs, rows)

    def to_hbm(q):
        at = pl.ds(order[q - 1] * narrow, narrow)
        return pltpu.make_async_copy(w.at[:, :, :, at], w_hbm.at[:, :, :, at], sem_w.at[q])

    keys = share_keys(sharing, kv, sem_kv)

    def begin():
        for j in range(rows):
            for which, ref in ((0, tokens_hbm), (1, cot_hbm)):

                @pl.when((section == which) & is_here(j))
                def _(ref=ref, j=j):
                    pltpu.make_async_copy(block_of(ref, j), turned.at[row], sem_x.at[row, 1]).start()

                @pl.when((section == which) & jnp.logical_not(is_here(j)))
                def _(ref=ref, j=j):
                    send_block(ref, j).start()

    def use_small():
        for r in range(rows):
            vectors[:, r * narrow : (r + 1) * narrow] = small[r, 0, 0, 0:8, 0:narrow]
        for k in range(cols):
            for i in range(blocks):
                at = k * hidden + i * deep
                shift[:, at : at + deep] = small[0, k // CORES, k % CORES, 8 + i : 9 + i]
        lines = tokens // deep
        for slot in range(group):
            part = lax.rem(sharing.position + group - slot, group)
            base = 8 + blocks + (lax.div(sequence, CORES) * group + part) * lines
            doc = jnp.concatenate([small[row, high, source_core, pl.ds(base + i, 1)] for i in range(lines)], axis=1)
            if slot == 0:
                doc_q[...] = doc
            doc_k[slot * tokens : (slot + 1) * tokens] = jnp.broadcast_to(doc, (128, tokens)).T[:, :1]
        mask[...] = jnp.where(doc_k[...] == doc_q[...], 0.0, NEG_BIG)

    def turn():
        for r in range(rows):
            pltpu.make_async_copy(turned.at[r], turned.at[r], sem_x.at[r, 1]).wait()
        for r in range(rows):
            x[:, r * narrow : (r + 1) * narrow] = turned[r].T
        start_ref[...] = x[...]

    half = max(1, cols // 2)
    chunks = min(4, tokens // 8)
    chunk = tokens // chunks

    def send_out(i):
        at = pl.ds(i * chunk, chunk)
        return pltpu.make_async_remote_copy(
            y.at[at], next_hbm.at[at], sem_y.at[i, 0], sem_y.at[i, 1],
            device_id={"section": 1 - section}, device_id_type=MESH,
        )

    stay = pltpu.make_async_copy(x, next_hbm, sem_next.at[0])
    base = 3

    def between(tick, done):
        if tick == 2:
            begin()
        if done >= 1:
            to_hbm(done).start()
        if done == 0:
            use_small()
        if done == 1:
            turn()

            @pl.when(section == 0)
            def _():
                stay.start()

            front.project(0)
        if done == 2:
            front.project(1)
        if done == base:
            front.project(2)
            for copy in keys:
                copy.start()
        if done == base + 1:
            for copy in keys:
                copy.wait()
        if base + 1 <= done < base + 5:
            front.attend((done - base - 1) * (front.pairs // 4), front.pairs // 4)
        if done == base + 5:
            front.out()
            front.norm_one()
        if done >= base + 5:
            first = done == base + 5
            ready = (done - 4) // 2
            from_block = 0 if first else (done - 1 - 4) // 2
            for block in range(from_block, min(ready, blocks)):
                if block < blocks - 1:
                    for k in range(0, cols, half):
                        front.feed(block, range(k, k + half), block == 0 and k == 0)

    gather.run(between)
    for i in range(chunks):
        at = pl.ds(i * chunk, chunk)
        for k in range(0, cols, half):
            front.feed(blocks - 1, range(k, k + half), blocks == 1 and k == 0, at=at)
        y[at] = front.norm_two(at).astype(BF16)

        @pl.when(section == 0)
        def _(i=i):
            send_out(i).start()

    gather.finish()
    for j in range(rows):

        @pl.when(jnp.logical_not(is_here(j)))
        def _(j=j):
            send_block(tokens_hbm, j).wait_send()

    for q in range(1, len(pieces)):
        to_hbm(q).wait()

    @pl.when(section == 0)
    def _():
        stay.wait()
        for i in range(chunks):
            send_out(i).wait_send()

    @pl.when(section == 1)
    def _():
        for i in range(chunks):
            send_out(i).wait_recv()


def first_forward(tokens_in, cotangent, qkv, out, unit, down, unit_bias, width_bias, gain, docs, rows, highs, group):
    micro, narrow, _ = tokens_in.shape
    _, seq_here, seq_len = docs.shape
    deep, hidden = out.shape[2], unit.shape[2]
    width, cols, blocks = narrow * rows, highs * CORES, hidden // deep
    tokens = seq_len // group
    tall = (4 + 2 * blocks) * narrow
    apart = (rows, highs, CORES)
    in_any = pl.BlockSpec(memory_space=pl.ANY)
    in_vmem = pl.BlockSpec(memory_space=pltpu.VMEM)
    count = 1 + 4 + 2 * blocks
    small_rows = 8 + blocks + micro * seq_here * seq_len // deep
    small_rows += -small_rows % 8
    dma = pltpu.SemaphoreType.DMA
    flat, flat_f32 = pltpu.VMEM((tokens, width), BF16), pltpu.VMEM((tokens, width), F32)
    return pl.pallas_call(
        functools.partial(
            first_kernel, highs=highs, rows=rows, group=group, micro=micro, seq_here=seq_here, seq_len=seq_len
        ),
        in_specs=[in_any] * 2 + [in_vmem] * 8,
        out_specs=[in_any, in_vmem, in_any] + [in_vmem] * 4,
        out_shape=[
            shaped((tokens, width), BF16),
            shaped((tokens, width), BF16),
            shaped(apart + (tall, deep), BF16),
            shaped((8, width), F32),
            shaped((1, hidden * cols), F32),
            shaped((1, tokens), F32),
            shaped((group * tokens, 1), F32),
        ],
        scratch_shapes=[
            pltpu.VMEM(apart + (tall, deep), BF16),
            pltpu.VMEM(apart + (small_rows, deep), F32),
            pltpu.VMEM((rows, narrow, tokens), BF16),
            flat,
            flat,
            pltpu.VMEM((group, 2, tokens, width), BF16),
            flat,
            pltpu.VMEM((group * tokens, tokens), F32),
            flat_f32,
            flat,
            flat_f32,
            flat,
            dma((count, rows - 1, 2, 2)),
            dma((count, highs - 1, 2, 2)),
            dma((count, 2)),
            dma((count, rows, 2, 2)),
            dma((rows, 2)),
            dma((max(1, group - 1), 2)),
            dma((4, 2)),
            dma((count,)),
            dma((1,)),
        ],
        name="first_forward",
        compiler_params=pltpu.CompilerParams(collective_id=2, has_side_effects=True, vmem_limit_bytes=LOW_VMEM),
        cost_estimate=pl.CostEstimate(
            flops=24 * tokens * width * width, bytes_accessed=2 * tall * deep * rows * cols, transcendentals=0
        ),
    )(tokens_in, cotangent, qkv, out, unit, down, unit_bias, width_bias, gain, docs)


class Streams:
    def __init__(self, landing, sems, group):
        self.landing, self.sems, self.rows = landing, sems, landing.shape[0]
        self.row, self.core = lax.axis_index("row"), lax.axis_index("core")
        self.place, self.size = group.place, group.size
        sequence = lax.div(group.place, group.size)
        self.to = lax.rem(sequence, CORES)
        self.slot = lax.div(sequence, CORES) * group.size + group.position

    def here(self, r):
        return (self.to == self.core) & (self.row == r)

    def sources(self):
        found = []
        for r in range(self.rows):
            place = ((r // self.size) * CORES + self.core) * self.size + r % self.size
            found.append(({"row": lax.div(place, CORES), "core": lax.rem(place, CORES)}, place != self.place))
        return found

    def copy(self, ref, r):
        return pltpu.make_async_remote_copy(
            ref.at[r], self.landing.at[self.slot], self.sems.at[r, 0], self.sems.at[self.slot, 1],
            device_id={"row": r, "core": self.to}, device_id_type=MESH,
        )

    def start(self, ref):
        for r in range(self.rows):

            @pl.when(self.here(r))
            def _(r=r):
                pltpu.make_async_copy(ref.at[r], self.landing.at[self.slot], self.sems.at[self.slot, 1]).start()

            @pl.when(jnp.logical_not(self.here(r)))
            def _(r=r):
                self.copy(ref, r).start()

    def wait_sent(self, ref):
        for r in range(self.rows):

            @pl.when(jnp.logical_not(self.here(r)))
            def _(r=r):
                self.copy(ref, r).wait_send()

    def wait_here(self):
        for r in range(self.rows):
            pltpu.make_async_copy(self.landing.at[r], self.landing.at[r], self.sems.at[r, 1]).wait()


def share_key_grads(group, dkv, got, sems):
    def copy(step):
        return pltpu.make_async_remote_copy(
            dkv.at[step], got.at[step - 1], sems.at[step - 1, 0], sems.at[step - 1, 1],
            device_id=group.member(group.size - step), device_id_type=MESH,
        )

    return [copy(step) for step in range(1, group.size)]


def join_key_grads(dkv, got):
    group, _, tokens, _ = dkv.shape
    step = min(SLICE, tokens)

    @pl.loop(0, tokens, step=step)
    def _(at):
        some = pl.ds(pl.multiple_of(at, step), step)
        for j in range(2):
            total = dkv[0, j, some].astype(F32)
            for i in range(group - 1):
                total += got[i, j, some].astype(F32)
            dkv[0, j, some] = total.astype(BF16)


def heads_back(q, dmixed, mixed, log, kv, mask, first, count):
    group, _, tokens, _ = kv.shape

    @pl.loop(first, first + count)
    def _(p):
        at = pl.ds(pl.multiple_of(p * PAIR, PAIR), PAIR)
        keys = jnp.concatenate([kv[i, 0, :, at] for i in range(group)], axis=0)
        values = jnp.concatenate([kv[i, 1, :, at] for i in range(group)], axis=0)
        grad_query, grad_key, grad_value = pair_back(
            q[:, at], dmixed[:, at], mixed[:, at], [log[p, h : h + 1] for h in range(2)], keys, values, mask,
            min(256, tokens),
        )
        q[:, at] = grad_query
        for part in range(group):
            kv[part, 0, :, at] = grad_key[part * tokens : (part + 1) * tokens]
            kv[part, 1, :, at] = grad_value[part * tokens : (part + 1) * tokens]


def middle_kernel(*refs, group):
    (in_hbm, start_hbm, w_hbm, vectors, shift, doc_q, doc_k) = refs[:7]
    (next_hbm, q_hbm, kv_hbm, mixed_hbm, log_hbm, x1_hbm, hat1_hbm, scale1_hbm, hat2_hbm, scale2_hbm, act_hbm, slope_hbm,
     landing) = refs[7:20]
    (w, x, q, kv, mixed, log, mask, x1, x1_bf, acc, slope, act, hat1, hat2, scale1, scale2, y_t, got,
     sem_w, sem_in, sem_kv, sem_dkv, sem_keep, sem_act, sem_next, sem_out) = refs[20:]
    tokens, width = x.shape
    rows, highs, _, _, deep = w.shape
    narrow, cols = width // rows, highs * CORES
    section = lax.axis_index("section")
    sharing = Group(group)
    front = Front(w, vectors, shift, x, q, kv, mixed, mask, x1, x1_bf, acc, log)
    blocks = front.blocks
    hidden = blocks * deep
    streams = Streams(landing, sem_out, sharing)

    cuts = [(QKV, 3), (OUT, 1)] + [(UNIT + j * blocks + i, 1) for i in range(blocks) for j in range(2)]

    def load_w(i):
        first, count = cuts[i]
        at = pl.ds(first * narrow, count * narrow)
        return pltpu.make_async_copy(w_hbm.at[:, :, :, at], w.at[:, :, :, at], sem_w.at[i])

    get_x = pltpu.make_async_copy(in_hbm, x, sem_in.at[0])
    get_dy = pltpu.make_async_copy(start_hbm, x, sem_in.at[1])
    get_x.start()
    for i in range(len(cuts)):
        load_w(i).start()
    kept = {}

    def keep(i, ref, there):
        kept[i] = pltpu.make_async_copy(ref, there, sem_keep.at[i])
        kept[i].start()

    greet((), ("section",), sharing.members(), streams.sources())
    mask[...] = jnp.where(doc_k[...] == doc_q[...], 0.0, NEG_BIG)
    get_x.wait()
    load_w(0).wait()
    front.project(1)
    front.project(2)
    keys = share_keys(sharing, kv, sem_kv)
    for copy in keys:
        copy.start()
    front.project(0)
    keep(0, q, q_hbm)
    for copy in keys:
        copy.wait()
    keep(1, kv, kv_hbm)
    front.attend(0, front.pairs)
    keep(2, mixed, mixed_hbm)
    keep(3, log, log_hbm)
    load_w(1).wait()
    front.out()

    def keep_one(at, normed, scale):
        hat1[at] = normed.astype(BF16)
        scale1[at] = jnp.broadcast_to(scale, scale1[at].shape)

    front.norm_one(keep_one)
    get_dy.start()
    keep(4, x1_bf, x1_hbm)
    keep(5, hat1, hat1_hbm)
    keep(6, scale1, scale1_hbm)
    half = cols if tokens * cols * deep <= 1 << 19 else max(1, cols // 2)
    turns = [(block, range(k, k + half)) for block in range(blocks) for k in range(0, cols, half)]

    def keep_act(n):
        block, ks = turns[n]
        return [
            pltpu.make_async_copy(
                act.at[n % 2, :, pl.ds(i * deep, deep)],
                act_hbm.at[:, pl.ds(k * hidden + block * deep, deep)],
                sem_act.at[n % 2, i],
            )
            for i, k in enumerate(ks)
        ]

    for n, (block, ks) in enumerate(turns):
        if n % (cols // half) == 0:
            load_w(2 + 2 * block).wait()
            load_w(3 + 2 * block).wait()

        def keep_both(value, value_slope, n=n, block=block, ks=ks):
            if n >= 2:
                for copy in keep_act(n - 2):
                    copy.wait()
            act[n % 2] = value
            for copy in keep_act(n):
                copy.start()
            for i, k in enumerate(ks):
                begin = k * hidden + block * deep
                slope[:, begin : begin + deep] = value_slope[:, i * deep : (i + 1) * deep]

        front.feed(block, ks, n == 0, keep_both)
    keep(7, slope, slope_hbm)

    def keep_two(at, normed, scale):
        hat2[at] = normed.astype(BF16)
        scale2[at] = jnp.broadcast_to(scale, scale2[at].shape)

    step = min(SLICE, tokens)
    for begin in range(0, tokens, step):
        y = front.norm_two(pl.ds(begin, step), keep_two)
        y_t[:, :, begin : begin + step] = y.T.astype(BF16).reshape(rows, narrow, step)
    streams.start(y_t)
    keep(8, hat2, hat2_hbm)
    keep(9, scale2, scale2_hbm)

    for i in (4, 5):
        kept[i].wait()
    get_dy.wait()
    ddown, dattn, dmixed, dx = x1_bf, x, hat2, hat1

    def top(at):
        ddown[at] = norm_back(x[at].astype(F32), hat2[at].astype(F32), scale2[at][:, :1], vectors[7:8]).astype(BF16)

    by_tokens(tokens, top)
    for n, (block, ks) in enumerate(turns):
        up = jnp.concatenate([front.matrix(UNIT + block, k) for k in ks], axis=1)
        down = jnp.concatenate([front.matrix(UNIT + blocks + block, k) for k in ks], axis=1)
        begins = [k * hidden + block * deep for k in ks]
        slopes = jnp.concatenate([slope[:, b : b + deep] for b in begins], axis=1)
        dpre = (nn(ddown[...], down) * slopes.astype(F32)).astype(BF16)
        more = nt(dpre, up)
        if n == 0:
            acc[...] = more
        else:
            acc[...] += more
    kept[8].wait()

    def bottom(at):
        dx1 = ddown[at].astype(F32) + acc[at]
        dattn[at] = norm_back(dx1, hat1[at].astype(F32), scale1[at][:, :1], vectors[6:7]).astype(BF16)

    by_tokens(tokens, bottom)
    take = row_blocks(rows, narrow)
    for r in range(0, rows, take):
        some = pl.ds(OUT * narrow, narrow)
        weight = jnp.concatenate(
            [w[r : r + take, k // CORES, k % CORES, some].reshape(take * narrow, deep) for k in range(cols)], axis=1
        )
        dmixed[:, r * narrow : (r + take) * narrow] = nt(dattn[...], weight).astype(BF16)
    kept[0].wait()
    kept[1].wait()
    heads_back(q, dmixed, mixed, log, kv, mask, 0, front.pairs)
    grads = share_key_grads(sharing, kv, got, sem_dkv)
    for copy in grads:
        copy.start()
    for copy in grads:
        copy.wait()
    join_key_grads(kv, got)
    chunks = 2
    chunk = tokens // chunks

    def send_on(i):
        at = pl.ds(i * chunk, chunk)
        return pltpu.make_async_remote_copy(
            dx.at[at], next_hbm.at[at], sem_next.at[i, 0], sem_next.at[i, 1],
            device_id={"section": 1 - section}, device_id_type=MESH,
        )

    stay = pltpu.make_async_copy(start_hbm, next_hbm, sem_in.at[0])

    @pl.when(section == 1)
    def _():
        stay.start()

    for i in range(chunks):
        at = pl.ds(i * chunk, chunk)
        for k in range(cols):
            there = slice(k * deep, (k + 1) * deep)
            total = dattn[at, there].astype(F32)
            for j in range(3):
                total += nn(q[at] if j == 0 else kv[0, j - 1, at], front.matrix(QKV + j, k))
            dx[at, there] = total.astype(BF16)

        @pl.when(section == 1)
        def _(i=i):
            send_on(i).start()

    for n in range(len(turns) - 2, len(turns)):
        for copy in keep_act(n):
            copy.wait()
    for i in (2, 3, 6, 7, 9):
        kept[i].wait()
    streams.wait_sent(y_t)
    streams.wait_here()

    @pl.when(section == 1)
    def _():
        stay.wait()
        for i in range(chunks):
            send_on(i).wait_send()

    @pl.when(section == 0)
    def _():
        for i in range(chunks):
            send_on(i).wait_recv()


def middle(second_in, start, weight, vectors, shift, doc_query, doc_key, group):
    tokens, width = second_in.shape
    rows, highs, _, tall, deep = weight.shape
    cols, narrow, units = highs * CORES, width // rows, shift.shape[1]
    pairs, blocks = width // PAIR, units // cols // deep
    in_any = pl.BlockSpec(memory_space=pl.ANY)
    in_vmem = pl.BlockSpec(memory_space=pltpu.VMEM)
    dma = pltpu.SemaphoreType.DMA
    flat = shaped((tokens, width), BF16)
    thin = shaped((tokens, 128), F32)
    kv = shaped((group, 2, tokens, width), BF16)
    log = shaped((pairs, 2, tokens), F32)
    wide = shaped((tokens, units), BF16)
    turned = shaped((rows, narrow, tokens), BF16)
    half = cols if tokens * cols * deep <= 1 << 19 else max(1, cols // 2)

    def vmem(shape):
        return pltpu.VMEM(shape.shape, shape.dtype)

    whole = pltpu.VMEM((tokens, width), F32)
    return pl.pallas_call(
        functools.partial(middle_kernel, group=group),
        in_specs=[in_any] * 3 + [in_vmem] * 4,
        out_specs=[in_any] * 13,
        out_shape=[flat, flat, kv, flat, log, flat, flat, thin, flat, thin, wide, wide, turned],
        scratch_shapes=[
            vmem(weight), vmem(flat), vmem(flat), vmem(kv), vmem(flat), vmem(log),
            pltpu.VMEM((group * tokens, tokens), F32),
            whole, vmem(flat), whole, vmem(wide),
            pltpu.VMEM((2, tokens, half * deep), BF16),
            vmem(flat), vmem(flat), vmem(thin), vmem(thin), vmem(turned),
            pltpu.VMEM((max(1, group - 1), 2, tokens, width), BF16),
            dma((2 + 2 * blocks,)), dma((2,)), dma((max(1, group - 1), 2)), dma((max(1, group - 1), 2)), dma((10,)),
            dma((2, half)), dma((2, 2)), dma((rows, 2)),
        ],
        name="middle",
        compiler_params=pltpu.CompilerParams(collective_id=3, has_side_effects=True, vmem_limit_bytes=LOW_VMEM),
        cost_estimate=pl.CostEstimate(
            flops=72 * tokens * width * width, bytes_accessed=2 * tall * deep * rows * cols, transcendentals=0
        ),
    )(second_in, start, weight, vectors, shift, doc_query, doc_key)


STAGES = 3


def low_kernel(*refs, highs, rows, group):
    (dy_hbm, hat2_hbm, hat1_hbm, slope_hbm, act_hbm, x1_hbm, q_hbm, mixed_hbm, log_hbm, x_hbm, w_hbm, kv_hbm) = refs[:12]
    bias_doc_q, bias_doc_k, scale2, scale1, vectors = refs[12:17]
    down_out, out_out, unit_out, qkv_out, small_out, landed, landing, high_landing, dpre_hbm = refs[17:26]
    (dattn, x, q, mixed, log, w, kv, dmixed, bias, dkv_got, dx, stage, small, left, right,
     work, got, got_high, from_row, from_wide, sem_in, sem_right, sem_core, sem_load, sem_high, sem_row, sem_kv, sem_out,
     acc, top_sums, feed_sums, pre, sem_w, sem_slope, sem_dpre) = refs[26:]
    tokens, width = dattn.shape
    narrow, deep = stage.shape[-2:]
    dq, dkv = q, kv
    cols = highs * CORES

    sharing = Group(group)
    streams = Streams(landed, sem_out, sharing)

    units = act_hbm.shape[1]
    feed_pieces = units // cols // deep
    tail = small.shape[3]
    order = [("down", i) for i in range(feed_pieces)] + [("unit", i) for i in range(feed_pieces)]
    order += [("out", 0), ("qkv", 0), ("qkv", 1), ("small", 0), ("qkv", 2)]
    row_first = (("unit", 0),)
    pieces = [
        (small, tail, True) if name == "small" else (stage.at[n % STAGES], narrow, (name, i) not in row_first)
        for n, (name, i) in enumerate(order)
    ]

    def give(q, ref):
        name, i = order[q]
        value = ref[...]
        if name in ("down", "unit"):
            (down_out if name == "down" else unit_out)[0, :, i * deep : (i + 1) * deep] = value
        elif name == "out":
            out_out[0] = value
        elif name == "qkv":
            qkv_out[0, i] = value
        else:
            small_out[...] = value

    scatter = Scatter(
        pieces, (landing, work, got, high_landing, got_high, from_row, from_wide, sem_core, sem_load, sem_high, sem_row), highs, rows, give,
    )

    def at_block(first, count):
        return pl.ds(first * narrow, count * narrow)

    hat2, hat1, dy, dpres, slopes = kv.at[0, 0], kv.at[0, 1], kv.at[1, 0], (q, mixed), (kv.at[1, 1], dmixed)
    first_inputs = [(dy_hbm, dy), (hat2_hbm, hat2), (x1_hbm, x), (hat1_hbm, hat1)]
    inputs = [
        (w_hbm.at[:, :, :, at_block(OUT, 1)], w.at[:, :, :, at_block(OUT, 1)]),
        (mixed_hbm, mixed),
        (q_hbm, q),
        (log_hbm, log),
        (kv_hbm, kv),
        (w_hbm.at[:, :, :, at_block(QKV, 3)], w.at[:, :, :, at_block(QKV, 3)]),
        (x_hbm, x),
    ]
    first_loads = [pltpu.make_async_copy(a, b, sem_in.at[i]) for i, (a, b) in enumerate(first_inputs)]
    loads = [pltpu.make_async_copy(a, b, sem_in.at[len(first_inputs) + i]) for i, (a, b) in enumerate(inputs)]
    early = 5

    def get_w(block):
        slot = block % 2
        return [
            pltpu.make_async_copy(
                w_hbm.at[:, :, :, at_block(UNIT + j * feed_pieces + block, 1)],
                w.at[:, :, :, at_block(2 * slot + j, 1)],
                sem_w.at[slot, j],
            )
            for j in range(2)
        ]

    def columns_of(ref, buffer, block, sems, out):
        copies = []
        for k in range(cols):
            far = ref.at[:, pl.ds((k * feed_pieces + block) * deep, deep)]
            near = buffer.at[:, pl.ds(k * deep, deep)]
            copies.append(pltpu.make_async_copy(*((near, far) if out else (far, near)), sems.at[k]))
        return copies

    def get_slope(block):
        return columns_of(slope_hbm, slopes[block % 2], block, sem_slope.at[block % 2], False)

    def put_dpre(block):
        return columns_of(dpre_hbm, dpres[block % 2], block, sem_dpre.at[block % 2], True)

    def top():
        top_sums[...] = jnp.zeros_like(top_sums)
        feed_sums[...] = jnp.zeros_like(feed_sums)

        def some(at):
            grad, hat = dy[at].astype(F32), hat2[at].astype(F32)
            ddown = norm_back(grad, hat, scale2[at][:, :1], vectors[7:8]).astype(BF16)
            dattn[at] = ddown
            top_sums[0:1] += column_sum(ddown.astype(F32))
            top_sums[1:2] += column_sum(grad)
            top_sums[2:3] += column_sum(grad * hat)

        by_tokens(tokens, some)

    def turn(block):
        for copy in get_w(block) + get_slope(block):
            copy.wait()
        if block >= 2:
            for copy in put_dpre(block - 2):
                copy.wait()

        for ks in (range(cols // 2), range(cols // 2, cols)):

            def matrix(j):
                some = at_block(2 * (block % 2) + j, 1)
                parts = [w[:, k // CORES, k % CORES, some].reshape(width, deep) for k in ks]
                return jnp.concatenate(parts, axis=1)

            at = slice(ks[0] * deep, (ks[-1] + 1) * deep)
            dpre = (nn(dattn[...], matrix(1)) * slopes[block % 2][:, at].astype(F32)).astype(BF16)
            dpres[block % 2][:, at] = dpre
            total = column_sum(dpre.astype(F32))
            for i, k in enumerate(ks):
                begin = (k * feed_pieces + block) * deep
                pre[:, begin : begin + deep] = total[:, i * deep : (i + 1) * deep]
            more = nt(dpre, matrix(0))
            if block == 0 and ks[0] == 0:
                acc[...] = more
            else:
                acc[...] += more
        for copy in put_dpre(block):
            copy.start()
        if block + 2 < feed_pieces:
            for copy in get_w(block + 2) + get_slope(block + 2):
                copy.start()

    def bottom():
        def some(at):
            dx1, hat = dattn[at].astype(F32) + acc[at], hat1[at].astype(F32)
            grad = norm_back(dx1, hat, scale1[at][:, :1], vectors[6:7]).astype(BF16)
            dattn[at] = grad
            feed_sums[0:1] += column_sum(grad.astype(F32))
            feed_sums[1:2] += column_sum(dx1)
            feed_sums[2:3] += column_sum(dx1 * hat)

        by_tokens(tokens, some)
        for block in range(max(0, feed_pieces - 2), feed_pieces):
            for copy in put_dpre(block):
                copy.wait()
        for load in loads[:-1]:
            load.start()

    key_grads = share_key_grads(sharing, kv, dkv_got, sem_kv)
    take = row_blocks(rows, narrow)

    def w_out(r):
        some = w[pl.ds(r * take, take), :, :, at_block(OUT, 1)]
        return some.reshape(take, cols, narrow, deep)

    def prepare():
        for load in loads[:early]:
            load.wait()
        doc_k = jnp.broadcast_to(bias_doc_k[...], (128, bias_doc_k.shape[1])).T[:, :1]
        bias[...] = jnp.where(doc_k == bias_doc_q[...], 0.0, NEG_BIG).astype(BF16)

        @pl.loop(0, rows // take)
        def _(r):
            at = pl.ds(pl.multiple_of(r * take * narrow, take * narrow), take * narrow)
            dmixed[:, at] = nt(dattn[...], side_by_side(w_out(r))).astype(BF16)

    def fill(slot, block, loaded=None):
        @pl.loop(0, cols)
        def _(k):
            grad = nn(left[...], block(k)).astype(BF16)
            stage[slot, :, lax.div(k, CORES), lax.rem(k, CORES)] = grad.reshape(rows, narrow, deep)

    def column(ref):
        return lambda k: ref[:, pl.ds(pl.multiple_of(k * deep, deep), deep)]

    def fetch(q):
        name, i = order[q]
        source = act_hbm if name == "down" else dpre_hbm
        return [
            pltpu.make_async_copy(
                source.at[:, pl.ds(k * feed_pieces * deep + i * deep, deep)],
                right.at[q % 2, :, pl.ds(k * deep, deep)],
                sem_right.at[q % 2, k],
            )
            for k in range(cols)
        ]

    def is_feed(q):
        return q < len(order) and order[q][0] in ("down", "unit")

    def make(q):
        name, i = order[q]
        slot = q % STAGES
        if q == 0:
            left[...] = dattn[...].T
        if name in ("down", "unit"):
            if (name, i) == ("unit", 0):
                left[...] = x[...].T
                loads[-1].start()
            for copy in fetch(q):
                copy.wait()
            if is_feed(q + 1):
                for copy in fetch(q + 1):
                    copy.start()
            fill(slot, column(right.at[q % 2]))
        elif name == "out":
            left[...] = mixed[...].T
            fill(slot, column(dattn))
        elif name == "qkv":
            if i == 0:
                loads[-1].wait()
            left[...] = grads_of(i).T
            fill(slot, column(x))
        else:
            small_sums()

    pairs = width // PAIR

    def heads(first, count):
        heads_back(q, dmixed, mixed, log, kv, bias, first, count)

    def exchange():
        for copy in key_grads:
            copy.start()

    def join():
        for copy in key_grads:
            copy.wait()
        for load in loads[early:-1]:
            load.wait()
        join_key_grads(kv, dkv_got)

    def grads_of(j):
        return dq[...] if j == 0 else dkv[0, j - 1]

    def input_gradient():
        for k in range(cols):
            at = slice(k * deep, (k + 1) * deep)
            total = dattn[:, at].astype(F32)
            for j in range(3):
                total += nn(grads_of(j), w[:, k // CORES, k % CORES, at_block(QKV + j, 1)].reshape(width, deep))
            for piece in range(0, deep, min(narrow, deep)):
                r, inside = divmod(k * deep + piece, narrow)
                dx[r, inside : inside + min(narrow, deep)] = total[:, piece : piece + min(narrow, deep)].T.astype(BF16)

    def small_sums():
        parts = [column_sum(grads_of(j).astype(F32)) for j in (0, 2)]
        parts += [feed_sums[0:2], top_sums[0:2], feed_sums[2:3], top_sums[2:3]]
        rows_of = jnp.concatenate(parts, axis=0).astype(BF16)
        small[...] = jnp.zeros_like(small)
        lines = pre.shape[1] // cols // deep
        for r in range(rows):
            for k in range(cols):
                small[r, k // CORES, k % CORES, 0:8, 0:narrow] = rows_of[:, r * narrow : (r + 1) * narrow]
                for i in range(lines):
                    at = (k * lines + i) * deep
                    small[r, k // CORES, k % CORES, 8 + i : 9 + i] = pre[:, at : at + deep].astype(BF16)

    share = max(1, pairs // 4)

    def between(tick):
        if tick < feed_pieces:
            turn(tick)
        if tick == feed_pieces:
            bottom()
        if tick == feed_pieces + 1:
            prepare()
        if feed_pieces + 1 <= tick < feed_pieces + 5:
            heads((tick - feed_pieces - 1) * share, share)
        if tick == feed_pieces + 4:
            exchange()
        if tick == feed_pieces + 5:
            join()
        if tick + 1 < len(order):
            make(tick + 1)
        if tick == feed_pieces + 5:
            input_gradient()
            streams.start(dx)

    for load in first_loads:
        load.start()
    for copy in fetch(0) + get_w(0) + get_slope(0) + (get_w(1) + get_slope(1) if feed_pieces > 1 else []):
        copy.start()
    greet((scatter.high, scatter.row), ("core",), sharing.members(), streams.sources())
    for load in first_loads:
        load.wait()
    top()
    make(0)
    scatter.run(between)
    streams.wait_sent(dx)
    streams.wait_here()


def low_back(dy, hat2, scale2, hat1, scale1, slope, act, x1_bf, query, mixed, log_total, x, weight, shared, doc_query, doc_key, vectors):
    tokens, width = dy.shape
    rows, highs, _, _, deep = weight.shape
    cols = highs * CORES
    narrow = width // rows
    units = act.shape[1]
    feed_rows = narrow * units // cols // deep
    group = shared.shape[0]
    keys = group * tokens
    apart = (rows, highs, CORES)
    tail = 16
    lines = 8 + units // cols // deep
    assert lines <= tail and narrow <= deep
    count = 2 * (feed_rows // narrow) + 5
    wide = 1
    steps = 4 + highs - 1 + rows - 1
    slots = min(count, steps)
    in_any = pl.BlockSpec(memory_space=pl.ANY)
    in_vmem = pl.BlockSpec(memory_space=pltpu.VMEM)
    ways = {2: 1}
    block = (rows, narrow, deep)
    dma = pltpu.SemaphoreType.DMA
    args = [dy, hat2, hat1, slope, act, x1_bf, query, mixed, log_total, x, weight, shared]
    *outs, _, _, _ = pl.pallas_call(
        functools.partial(low_kernel, highs=highs, rows=rows, group=group),
        in_specs=[in_any] * len(args) + [in_vmem] * 5,
        out_specs=[in_vmem] * 5 + [in_any] * 4,
        out_shape=[
            shaped((1, narrow, units // cols), BF16),
            shaped((1, narrow, deep), BF16),
            shaped((1, narrow, units // cols), BF16),
            shaped((1, 3, narrow, deep), BF16),
            shaped((tail, deep), BF16),
            shaped((rows, narrow, tokens), BF16),
            shaped((count, highs) + block, BF16),
            shaped((count, highs - 1, ways.get(highs, 2)) + block, BF16),
            shaped((tokens, units), BF16),
        ],
        scratch_shapes=[
            pltpu.VMEM((tokens, width), BF16),
            pltpu.VMEM((tokens, width), BF16),
            pltpu.VMEM((tokens, width), BF16),
            pltpu.VMEM((tokens, width), BF16),
            pltpu.VMEM(log_total.shape, F32),
            pltpu.VMEM(apart + (4 * narrow, deep), BF16),
            pltpu.VMEM((group, 2, tokens, width), BF16),
            pltpu.VMEM((tokens, width), BF16),
            pltpu.VMEM((keys, tokens), BF16),
            pltpu.VMEM((group - 1, 2, tokens, width), BF16),
            pltpu.VMEM((rows, narrow, tokens), BF16),
            pltpu.VMEM((STAGES,) + apart + (narrow, deep), BF16),
            pltpu.VMEM(apart + (tail, deep), BF16),
            pltpu.VMEM((width, tokens), BF16),
            pltpu.VMEM((2, tokens, cols * deep), BF16),
            pltpu.VMEM((slots, highs) + block, BF16),
            pltpu.VMEM((2, highs) + block, BF16),
            pltpu.VMEM((ways.get(highs, 2),) + block, BF16),
            pltpu.VMEM((count - wide, rows - 1, ways.get(rows, 2), narrow, deep), BF16),
            pltpu.VMEM((wide, rows - 1, ways.get(rows, 2), highs, narrow, deep), BF16),
            dma((11,)),
            dma((2, cols)),
            dma((count, highs, 2)),
            dma((count, highs, 2)),
            dma((count, highs - 1, 2, 3)),
            dma((count, rows - 1, 2, 2)),
            dma((max(1, group - 1), 2)),
            dma((rows, 2)),
            pltpu.VMEM((tokens, width), F32),
            pltpu.VMEM((8, width), F32),
            pltpu.VMEM((8, width), F32),
            pltpu.VMEM((1, units), F32),
            dma((2, 2)),
            dma((2, cols)),
            dma((2, cols)),
        ],
        name="low_back",
        compiler_params=pltpu.CompilerParams(collective_id=1, has_side_effects=True, vmem_limit_bytes=LOW_VMEM),
        cost_estimate=pl.CostEstimate(
            flops=64 * tokens * width * width, bytes_accessed=12 * width * units, transcendentals=0
        ),
    )(*args, doc_query, doc_key.reshape(1, keys), scale2, scale1, vectors)
    return outs


def finish_kernel(down, out, unit, qkv, small, first, second, *outs):
    layer_out, input_grad, qkv_out, out_out, unit_out, down_out, bias_out, width_out, gain_out = outs
    for ref, to in ((down, down_out), (out, out_out), (unit, unit_out), (qkv, qkv_out)):
        to[...] = ref[...].astype(F32)
    rows, narrow, tokens = first.shape
    for ref, to in ((first, layer_out), (second, input_grad)):
        per = rows // to.shape[1]
        for r in range(rows):
            to[0, r // per, :, r % per * tokens : (r % per + 1) * tokens] = ref[r].astype(F32)
    values = small[...].astype(F32)
    width_out[0] = values[0:6, :narrow]
    gain_out[0] = values[6:8, :narrow]
    deep = values.shape[1]
    for i in range(bias_out.shape[1] // deep):
        bias_out[:, i * deep : (i + 1) * deep] = values[8 + i : 9 + i]


def finish(down, out, unit, qkv, small, first, second, micro):
    rows, narrow, tokens = first.shape
    stream = shaped((1, micro, narrow, rows // micro * tokens), F32)
    grads = [shaped(grad.shape, F32) for grad in (qkv, out, unit, down)]
    rest = [shaped((1, down.shape[2]), F32), shaped((1, 6, narrow), F32), shaped((1, 2, narrow), F32)]
    return pl.pallas_call(
        finish_kernel,
        out_shape=[stream, stream, *grads, *rest],
        name="finish",
        compiler_params=pltpu.CompilerParams(vmem_limit_bytes=VMEM_BYTES),
    )(down, out, unit, qkv, small, first, second)


def local(tokens_in, doc_ids, cotangent, qkv_master, out_master, unit_master, down_master, unit_bias, width_bias, norm_gain):
    at = Layout(tokens_in, doc_ids)
    rows, cols = at.rows, at.cols

    second_in, start, weights, vectors, unit_shift, doc_query, doc_key = first_forward(
        tokens_in, cotangent, qkv_master, out_master, unit_master, down_master, unit_bias, width_bias, norm_gain, doc_ids,
        rows, cols // CORES, at.group,
    )
    (
        dy, query, shared, mixed, log_total, x1_bf, hat_one, scale_one, hat_two, scale_two, act, slope, stream,
    ) = middle(second_in, start, weights, vectors, unit_shift, doc_query, doc_key, at.group)
    *grads, input_grad = low_back(
        dy, hat_two, scale_two, hat_one, scale_one, slope, act, x1_bf, query, mixed, log_total, second_in, weights, shared,
        doc_query, doc_key, vectors,
    )
    return finish(*grads, stream, input_grad, at.micro)


def solution(mesh):
    sections, rows, cols = (mesh.shape[name] for name in ("section", "row", "col"))
    fine = Mesh(
        mesh.devices.reshape(sections, rows, cols // CORES, CORES), ("section", "row", "high", "core")
    )
    col = ("high", "core")
    block = P("section", "row", col)
    stream = P("section", None, "row", col)
    return jax.shard_map(
        local,
        mesh=fine,
        in_specs=(
            P(None, "row", col),
            P(None, col, None),
            P(None, "row", col),
            P("section", None, "row", col),
            block,
            block,
            block,
            P("section", col),
            P("section", None, "row"),
            P("section", None, "row"),
        ),
        out_specs=(
            stream,
            stream,
            stream,
            block,
            block,
            block,
            P("section", col),
            P("section", None, "row"),
            P("section", None, "row"),
        ),
        check_vma=False,
    )
```

```python
import functools

import jax
import jax.numpy as jnp
from jax import lax
from jax.experimental import pallas as pl
from jax.experimental.pallas import tpu as pltpu
from jax.sharding import Mesh
from jax.sharding import PartitionSpec as P

HD = 64
EPSILON = 1e-05
NEG_BIG = -1e30
CORES = 2
PAIR = 128
PLANE = ("row", "high", "core")
MESH = pl.DeviceIdType.MESH

QKV, OUT, UNIT = 0, 3, 4

F32 = jnp.float32
BF16 = jnp.bfloat16
VMEM_BYTES = 56 * 1024 * 1024
LOW_VMEM = 65200 * 1024


def nn(left, right):
    return lax.dot_general(left, right, (((1,), (0,)), ((), ())), preferred_element_type=F32)


def nt(left, right):
    return lax.dot_general(left, right, (((1,), (1,)), ((), ())), preferred_element_type=F32)


def shaped(shape, dtype):
    return jax.ShapeDtypeStruct(shape, dtype)


def row_blocks(rows, narrow):
    take = min(rows, max(1, 256 // narrow))
    while rows % take:
        take += 1
    return take


def side_by_side(blocks):
    take, cols, narrow, deep = blocks.shape
    return jnp.concatenate([blocks[:, k].reshape(take * narrow, deep) for k in range(cols)], axis=1)


def head_lanes(shape, axis):
    return lax.broadcasted_iota(jnp.int32, shape, axis) < HD


def both_heads(array):
    lanes = head_lanes(array.shape, 1)
    return jnp.concatenate([jnp.where(lanes, array, 0), jnp.where(lanes, 0, array)], axis=0)


def own_rows(array):
    tokens = array.shape[1] // 2
    return jnp.where(head_lanes((PAIR, tokens), 0), array[:, :tokens], array[:, tokens:])


def pair_front(query, keys, values, bias_ref):
    tokens = query.shape[0]
    bias = bias_ref[...]
    scores = nt(keys, both_heads(query)) + jnp.concatenate([bias, bias], axis=1)
    top = jnp.max(scores, axis=0, keepdims=True)
    expo = jnp.exp(scores - top)
    total = jnp.sum(expo, axis=0, keepdims=True)
    mixed = own_rows(nn(values.T, expo.astype(BF16)) / total)
    log_row = top + jnp.log(total)
    return mixed.T.astype(BF16), [log_row[:, :tokens], log_row[:, tokens:]]


def pair_back(query, grad, mixed, log_rows, keys, values, bias_ref, tile):
    tokens = query.shape[0]
    keys_t = keys.T
    lanes = head_lanes((tile, PAIR), 1)
    low_t = head_lanes(keys_t.shape, 0)
    products = (grad.astype(F32) * mixed.astype(F32)).T
    grad_query = []
    grad_key = jnp.zeros(keys.shape, F32)
    grad_value = jnp.zeros(keys.shape, F32)
    for at in range(0, tokens, tile):
        some = slice(at, at + tile)
        grad_some = jnp.zeros((PAIR, tile), F32)
        for h in range(2):
            here = lanes if h == 0 else ~lanes
            mine = jnp.where(here, query[some], 0)
            grad_mine = jnp.where(here, grad[some], 0)
            inner = jnp.sum(products[h * HD : (h + 1) * HD, some], axis=0, keepdims=True)
            prob = jnp.exp(nt(keys, mine) + bias_ref[:, some] - log_rows[h][:, some])
            grad_value += nn(prob.astype(BF16), grad_mine)
            grad_scores = (prob * (nt(values, grad_mine) - inner)).astype(BF16)
            grad_key += nn(grad_scores, mine)
            keys_mine = jnp.where(low_t if h == 0 else ~low_t, keys_t, 0)
            grad_some += nn(keys_mine, grad_scores)
        grad_query.append(grad_some)
    grad_query = jnp.concatenate(grad_query, axis=1).T.astype(BF16) * HD**-0.5
    return grad_query, grad_key.astype(BF16), grad_value.astype(BF16)


def normed_of(hidden):
    center = hidden - jnp.mean(hidden, axis=1, keepdims=True)
    scale = lax.rsqrt(jnp.mean(center * center, axis=1, keepdims=True) + EPSILON)
    return center * scale, scale


def norm_back(grad_out, normed, scale, gain):
    scaled = grad_out * gain
    first = jnp.mean(scaled, axis=1, keepdims=True)
    second = jnp.mean(scaled * normed, axis=1, keepdims=True)
    return scale * (scaled - first - normed * second)


SLICE = 128


def by_tokens(tokens, body):
    step = min(SLICE, tokens)
    for at in range(0, tokens, step):
        body(pl.ds(at, step))


def gelu_parts(pre):
    below = 0.5 * (1.0 + lax.erf(pre * 0.5**0.5))
    return pre * below, below + pre * jnp.exp(-0.5 * pre * pre) * (2.0 * jnp.pi) ** -0.5


def column_sum(value):
    return jnp.sum(value, axis=0, keepdims=True)


class Layout:
    def __init__(self, tokens_in, doc_ids):
        self.micro, self.narrow, _ = tokens_in.shape
        self.seq_here, self.seq_len = doc_ids.shape[1:]
        self.rows = lax.axis_size("row")
        self.cols = lax.axis_size("high") * CORES
        self.width = self.narrow * self.rows
        self.places = self.rows * CORES
        self.sequences = self.micro * self.seq_here * CORES
        self.group = self.places // self.sequences
        self.part = self.seq_len // self.group
        self.row = lax.axis_index("row")
        place = self.row * CORES + lax.axis_index("core")
        self.sequence = place // self.group
        self.position = place % self.group
        self.block = (self.sequence // CORES) * self.group + self.position


class Line:
    def __init__(self, axis, size):
        self.axis, self.size, self.here = axis, size, lax.axis_index(axis)

    def sends(self, step):
        last = self.size - 1
        return (
            (True, (self.here < step) & (self.here < last), self.size - step + self.here, self.here > 0),
            (False, (last - self.here < step) & (self.here > 0), step - self.size + self.here, self.here < last),
        )

    def gets(self, step):
        last = self.size - 1
        return (
            (True, (self.here >= 1) & (self.here <= step)),
            (False, (last - self.here >= 1) & (last - self.here <= step)),
        )

    def neighbour(self, right):
        return {self.axis: self.here + (1 if right else -1)}


def greet(lines, pairs, members=(), some=()):
    barrier = pltpu.get_barrier_semaphore()
    count = 0
    for line in lines:
        for right, there in ((True, line.here < line.size - 1), (False, line.here > 0)):

            @pl.when(there)
            def _(line=line, right=right):
                pl.semaphore_signal(barrier, 1, device_id=line.neighbour(right), device_id_type=MESH)

            count = count + there.astype(jnp.int32)
    for axis in pairs:
        pl.semaphore_signal(barrier, 1, device_id={axis: 1 - lax.axis_index(axis)}, device_id_type=MESH)
        count = count + 1
    for member in members:
        pl.semaphore_signal(barrier, 1, device_id=member, device_id_type=MESH)
        count = count + 1
    for member, there in some:

        @pl.when(there)
        def _(member=member):
            pl.semaphore_signal(barrier, 1, device_id=member, device_id_type=MESH)

        count = count + there.astype(jnp.int32)
    pl.semaphore_wait(barrier, count)


def add_into(target, other):
    lead = target.shape[:-2]
    rows = target.shape[-2]
    total = 1
    for size in lead:
        total *= size
    if total == 1:
        target[...] = target[...] + other[...]
        return

    @pl.loop(0, total)
    def _(i):
        index = []
        for size in reversed(lead):
            index.insert(0, lax.rem(i, size))
            i = lax.div(i, size)
        index = tuple(index)
        target[index] = target[index] + other[index]


class Scatter:
    def __init__(self, pieces, refs, highs, rows, give):
        self.pieces, self.give = pieces, give
        (self.landing, self.work, self.got, self.from_high, self.got_high, self.from_row, self.from_wide, *sems) = refs
        self.sem_core, self.sem_load, self.sem_high, self.sem_row = sems
        self.high, self.row = Line("high", highs), Line("row", rows)
        self.core = lax.axis_index("core")
        self.slots = self.work.shape[0]
        self.sent = [[] for _ in pieces]
        self.place, wide, thin = [], 0, 0
        for _, _, row_last in pieces:
            self.place.append(thin if row_last else wide)
            thin, wide = thin + row_last, wide + (not row_last)

    def slot(self, q):
        return q % self.slots

    def cut(self, q, ref):
        return ref.at[..., pl.ds(0, self.pieces[q][1]), :]

    def to_core(self, q, y):
        return pltpu.make_async_remote_copy(
            self.pieces[q][0].at[:, y, 1 - self.core],
            self.cut(q, self.landing.at[q, y]),
            self.sem_core.at[q, y, 0],
            self.sem_core.at[q, y, 1],
            device_id={"core": 1 - self.core},
            device_id_type=MESH,
        )

    def load(self, q, y):
        return pltpu.make_async_copy(
            self.pieces[q][0].at[:, y, self.core],
            self.cut(q, self.work.at[self.slot(q), y]),
            self.sem_load.at[q, y, 0],
        )

    def fetch(self, q, y):
        return pltpu.make_async_copy(
            self.cut(q, self.landing.at[q, y]), self.cut(q, self.got.at[q % 2, y]), self.sem_load.at[q, y, 1]
        )

    def begin(self, q):
        if q >= self.slots:
            self.finish_sends(q - self.slots)
        for y in range(self.high.size):
            self.to_core(q, y).start()
            self.load(q, y).start()

    def arrive(self, q):
        for y in range(self.high.size):
            self.to_core(q, y).wait()
            self.fetch(q, y).start()

    def merge(self, q):
        for y in range(self.high.size):
            self.load(q, y).wait()
            self.fetch(q, y).wait()
            add_into(self.cut(q, self.work.at[self.slot(q), y]), self.cut(q, self.got.at[q % 2, y]))

    def lines(self, q):
        return (self.high, self.row) if self.pieces[q][2] else (self.row, self.high)

    def block(self, q, line, i):
        first = line is self.lines(q)[0]
        if line is self.high:
            ref = self.work.at[self.slot(q), i, slice(None) if first else self.row.here]
        else:
            ref = self.work.at[self.slot(q), slice(None) if first else self.high.here, i]
        return self.cut(q, ref)

    def arrival(self, q, line, step, right):
        way = 0 if line.size == 2 or right else 1
        first = line is self.lines(q)[0]
        if line is self.high:
            index = (slice(None),) if first else (0,)
            return (
                self.cut(q, self.from_high.at[(q, step - 1, way) + index]),
                self.cut(q, self.got_high.at[(way,) + index]),
            )
        ref = (self.from_wide if first else self.from_row).at[self.place[q], step - 1, way]
        return (self.cut(q, ref),) * 2

    def copy(self, q, line, step, right, i):
        sems = (self.sem_high if line is self.high else self.sem_row).at[q, step - 1, 0 if right else 1]
        return pltpu.make_async_remote_copy(
            self.block(q, line, i),
            self.arrival(q, line, step, right)[0],
            sems.at[0],
            sems.at[1],
            device_id=line.neighbour(right),
            device_id_type=MESH,
        )

    def push(self, q, line, step):
        for right, there, i, more in line.sends(step):

            @pl.when(there)
            def _(right=right, i=i, more=more):
                if step > 1:

                    @pl.when(more)
                    def _():
                        add_into(self.block(q, line, i), self.arrival(q, line, step - 1, right)[1])

                self.copy(q, line, step, right, i).start()

            self.sent[q].append((line, step, right, there, i))

    def pull(self, q, line, step):
        for right, there in line.gets(step):

            @pl.when(there)
            def _(right=right):
                self.copy(q, line, step, right, 0).wait_recv()
                if line is self.high:
                    landed, got = self.arrival(q, line, step, right)
                    way = 0 if line.size == 2 or right else 1
                    fetch = pltpu.make_async_copy(landed, got, self.sem_high.at[q, step - 1, way, 2])
                    fetch.start()
                    fetch.wait()

    def close(self, q, line):
        for right, there in line.gets(line.size - 1):

            @pl.when(there)
            def _(right=right):
                add_into(self.block(q, line, line.here), self.arrival(q, line, line.size - 1, right)[1])

    def finish_sends(self, q):
        for line, step, right, there, i in self.sent[q]:

            @pl.when(there)
            def _(line=line, step=step, right=right, i=i):
                self.copy(q, line, step, right, i).wait_send()

        self.sent[q] = []

    def stages(self, q):
        lines = [(line, step) for line in self.lines(q) for step in range(1, line.size)]

        def merge():
            self.merge(q)
            self.push(q, *lines[0])

        stages = [lambda: self.begin(q), lambda: self.arrive(q), merge]
        for n, (line, step) in enumerate(lines):

            def one(n=n, line=line, step=step):
                self.pull(q, line, step)
                if step == line.size - 1:
                    self.close(q, line)
                if n + 1 < len(lines):
                    self.push(q, *lines[n + 1])
                else:
                    self.give(q, self.block(q, line, line.here))

            if line is self.high and step == 1:
                stages.append(lambda: None)
            stages.append(one)
        return stages

    def run(self, between):
        stages = [self.stages(q) for q in range(len(self.pieces))]
        depth, count = len(stages[0]), len(stages)
        for tick in range(count + depth - 1):
            alive = range(max(0, tick - depth + 1), min(tick + 1, count))
            for q in alive:
                stages[q][tick - q]()
            between(tick)
        for q in range(count):
            self.finish_sends(q)


class Spread:
    def __init__(self, axis, size):
        self.axis, self.size, self.here = axis, size, lax.axis_index(axis)

    def sends(self, step):
        last = self.size - 1
        return (
            (True, (self.here < last) & (self.here >= step - 1), self.here - step + 1),
            (False, (self.here > 0) & (self.here + step - 1 <= last), self.here + step - 1),
        )

    def gets(self, step):
        last = self.size - 1
        return ((True, self.here >= step), (False, self.here + step <= last))

    def neighbour(self, right):
        return {self.axis: self.here + (1 if right else -1)}


AHEAD = 2


class Gather:
    def __init__(self, pieces, sems, highs, rows):
        self.pieces = pieces
        self.sem_row, self.sem_high, self.sem_core, self.sem_one = sems
        self.row, self.high = Spread("row", rows), Spread("high", highs)
        self.core = lax.axis_index("core")
        self.sent = []

    def block(self, q, line, i):
        ref, first, count, row_first = self.pieces[q]
        some = pl.ds(first, count)
        if line is self.row:
            return ref.at[i, self.high.here if row_first else slice(None), self.core, some]
        return ref.at[slice(None) if row_first else self.row.here, i, self.core, some]

    def copy(self, q, line, step, right, i):
        sems = (self.sem_row if line is self.row else self.sem_high).at[q, step - 1, 0 if right else 1]
        ref = self.block(q, line, i)
        return pltpu.make_async_remote_copy(
            ref, ref, sems.at[0], sems.at[1], device_id=line.neighbour(right), device_id_type=MESH
        )

    def one(self, q, right, i):
        ref, first, count, _ = self.pieces[q]
        ref = ref.at[i, self.high.here, self.core, pl.ds(first, count)]
        sems = self.sem_one.at[q, i, 0 if right else 1]
        return pltpu.make_async_remote_copy(
            ref, ref, sems.at[0], sems.at[1], device_id=self.high.neighbour(right), device_id_type=MESH
        )

    def start(self, there, copy):
        @pl.when(there)
        def _():
            copy().start()

        self.sent.append((there, copy))

    def over(self, q, i, there=True):
        for right, also, _ in self.high.sends(1):
            self.start(also & there, functools.partial(self.one, q, right, i))

    def push(self, q, line, step):
        if line is self.high and step == 1 and self.pieces[q][3]:
            return
        for right, there, i in line.sends(step):
            self.start(there, functools.partial(self.copy, q, line, step, right, i))

    def pull(self, q, line, step):
        row_first = self.pieces[q][3]
        for right, there in line.gets(step):

            @pl.when(there)
            def _(right=right):
                if line is self.high and step == 1 and row_first:
                    for i in range(self.row.size):
                        self.one(q, right, i).wait_recv()
                else:
                    self.copy(q, line, step, right, line.here).wait_recv()

            if line is self.row and row_first:
                self.over(q, line.here - step if right else line.here + step, there)

    def to_core(self, q):
        ref, first, count, _ = self.pieces[q]
        ref = ref.at[:, :, self.core, pl.ds(first, count)]
        return pltpu.make_async_remote_copy(
            ref, ref, self.sem_core.at[q, 0], self.sem_core.at[q, 1],
            device_id={"core": 1 - self.core}, device_id_type=MESH,
        )

    def stages(self, q):
        first, second = (self.row, self.high) if self.pieces[q][3] else (self.high, self.row)
        def begin():
            self.push(q, first, 1)
            if first is self.row:
                self.over(q, self.row.here)

        steps = [begin] + [lambda: None] * AHEAD
        lines = [(first, i) for i in range(1, first.size)] + [(second, i) for i in range(1, second.size)]
        for n, (line, step) in enumerate(lines):

            def one(n=n, line=line, step=step):
                self.pull(q, line, step)
                if n + 1 < len(lines):
                    self.push(q, *lines[n + 1])
                else:
                    self.to_core(q).start()

            steps.append(lambda: None)
            steps.append(one)
        steps.append(lambda: self.to_core(q).wait())
        return steps

    def run(self, between):
        stages = [self.stages(q) for q in range(len(self.pieces))]
        depth, count = len(stages[0]), len(stages)
        for tick in range(count + depth - 1):
            for q in range(max(0, tick - depth + 1), min(tick + 1, count)):
                stages[q][tick - q]()
            between(tick, tick - depth + 1)

    def finish(self):
        for there, copy in self.sent:

            @pl.when(there)
            def _(copy=copy):
                copy().wait_send()


class Group:
    def __init__(self, size):
        self.size = size
        self.place = lax.axis_index("row") * CORES + lax.axis_index("core")
        self.position = lax.rem(self.place, size)

    def member(self, step):
        other = self.place - self.position + lax.rem(self.position + step, self.size)
        return {"row": lax.div(other, CORES), "core": lax.rem(other, CORES)}

    def members(self):
        return [self.member(step) for step in range(1, self.size)]


class Front:
    def __init__(self, w, vectors, shift, x, q, kv, mixed, mask, x1, x1_bf, acc, log=None):
        self.w, self.vectors, self.shift, self.x, self.q, self.kv = w, vectors, shift, x, q, kv
        self.mixed, self.mask, self.x1, self.x1_bf, self.acc, self.log = mixed, mask, x1, x1_bf, acc, log
        self.tokens, self.width = x.shape
        self.rows, self.highs, _, _, self.deep = w.shape
        self.cols = self.highs * CORES
        self.narrow = self.width // self.rows
        self.group = kv.shape[0]
        self.pairs = self.width // PAIR
        self.blocks = shift.shape[1] // self.cols // self.deep

    def matrix(self, block, k):
        at = pl.ds(block * self.narrow, self.narrow)
        return self.w[:, k // CORES, k % CORES, at].reshape(self.width, self.deep)

    def project(self, j):
        take = row_blocks(self.rows, self.narrow)
        for r in range(0, self.rows, take):
            at = slice(r * self.narrow, (r + take) * self.narrow)
            some = pl.ds((QKV + j) * self.narrow, self.narrow)
            weight = jnp.concatenate(
                [
                    self.w[r : r + take, k // CORES, k % CORES, some].reshape(take * self.narrow, self.deep)
                    for k in range(self.cols)
                ],
                axis=1,
            )
            out = nt(self.x[...], weight)
            if j == 0:
                self.q[:, at] = ((out + self.vectors[0:1, at]) * HD**-0.5).astype(BF16)
            elif j == 1:
                self.kv[0, 0, :, at] = out.astype(BF16)
            else:
                self.kv[0, 1, :, at] = (out + self.vectors[1:2, at]).astype(BF16)

    def attend(self, first, count):
        @pl.loop(first, first + count)
        def _(p):
            at = pl.ds(pl.multiple_of(p * PAIR, PAIR), PAIR)
            keys = jnp.concatenate([self.kv[i, 0, :, at] for i in range(self.group)], axis=0)
            values = jnp.concatenate([self.kv[i, 1, :, at] for i in range(self.group)], axis=0)
            mixed, log_rows = pair_front(self.q[:, at], keys, values, self.mask)
            self.mixed[:, at] = mixed
            if self.log is not None:
                for h in range(2):
                    self.log[p, h : h + 1] = log_rows[h]

    def out(self):
        for k in range(self.cols):
            at = slice(k * self.deep, (k + 1) * self.deep)
            self.acc[:, at] = nn(self.mixed[...], self.matrix(OUT, k))

    def norm_one(self, keep=None):
        def some(at):
            attn = self.acc[at] + self.vectors[2:3]
            normed, scale = normed_of(self.x[at].astype(F32) + attn)
            x1 = normed * self.vectors[6:7] + self.vectors[3:4]
            self.x1[at] = x1
            self.x1_bf[at] = x1.astype(BF16)
            if keep is not None:
                keep(at, normed, scale)

        by_tokens(self.tokens, some)

    def feed(self, block, ks, start, keep=None, at=slice(None)):
        up = jnp.concatenate([self.matrix(UNIT + block, k) for k in ks], axis=1)
        down = jnp.concatenate([self.matrix(UNIT + self.blocks + block, k) for k in ks], axis=1)
        hidden = self.blocks * self.deep
        begins = [k * hidden + block * self.deep for k in ks]
        shift = jnp.concatenate([self.shift[:, b : b + self.deep] for b in begins], axis=1)
        act, slope = gelu_parts(nn(self.x1_bf[at], up) + shift)
        act = act.astype(BF16)
        if keep is not None:
            keep(act, slope.astype(BF16))
        more = nt(act, down)
        if start:
            self.acc[at] = more
        else:
            self.acc[at] += more

    def norm_two(self, at, keep=None):
        normed, scale = normed_of(self.x1[at] + (self.acc[at] + self.vectors[4:5]))
        if keep is not None:
            keep(at, normed, scale)
        return normed * self.vectors[7:8] + self.vectors[5:6]


def share_keys(group, kv, sems):
    def copy(step):
        return pltpu.make_async_remote_copy(
            kv.at[0], kv.at[step], sems.at[step - 1, 0], sems.at[step - 1, 1],
            device_id=group.member(step), device_id_type=MESH,
        )

    return [copy(step) for step in range(1, group.size)]


def first_kernel(*refs, highs, rows, group, micro, seq_here, seq_len):
    (tokens_hbm, cot_hbm, qkv_ref, out_ref, unit_ref, down_ref, unit_bias, width_bias, gain, docs) = refs[:10]
    (next_hbm, start_ref, w_hbm, vectors, shift, doc_q, doc_k) = refs[10:17]
    (w, small, turned, x, q, kv, mixed, mask, x1, x1_bf, acc, y,
     sem_row, sem_high, sem_core, sem_one, sem_x, sem_kv, sem_y, sem_w, sem_next) = refs[17:]
    tokens, width = x.shape
    narrow, deep = width // rows, w.shape[-1]
    cols = highs * CORES
    hidden = unit_ref.shape[2]
    blocks = hidden // deep
    row, high, core = lax.axis_index("row"), lax.axis_index("high"), lax.axis_index("core")
    section = lax.axis_index("section")
    sharing = Group(group)
    sequence = lax.div(sharing.place, group)
    front = Front(w, vectors, shift, x, q, kv, mixed, mask, x1, x1_bf, acc)

    w[row, high, core, 0 : 3 * narrow] = qkv_ref[0].reshape(3 * narrow, deep).astype(BF16)
    w[row, high, core, 3 * narrow : 4 * narrow] = out_ref[0].astype(BF16)
    for i in range(blocks):
        at = slice(i * deep, (i + 1) * deep)
        for j, ref in enumerate((unit_ref, down_ref)):
            first = (UNIT + j * blocks + i) * narrow
            w[row, high, core, first : first + narrow] = ref[0, :, at].astype(BF16)
    small[row, high, core, 0:6, 0:narrow] = width_bias[0]
    small[row, high, core, 6:8, 0:narrow] = gain[0]
    for i in range(blocks):
        small[row, high, core, 8 + i : 9 + i] = unit_bias[:, i * deep : (i + 1) * deep]
    lines = seq_len // deep
    for m in range(micro):
        for i in range(seq_here):
            for j in range(lines):
                at = 8 + blocks + (m * seq_here + i) * lines + j
                small[row, high, core, at : at + 1] = docs[m, i : i + 1, j * deep : (j + 1) * deep].astype(F32)

    def goes(j):
        place = ((j // group) * CORES + core) * group + j % group
        return lax.div(place, CORES), lax.rem(place, CORES)

    source_core = lax.rem(sequence, CORES)
    mine_too = source_core == core

    def block_of(ref, j):
        m, rest = divmod(j // group, seq_here)
        return ref.at[m, :, pl.ds(rest * seq_len + (j % group) * tokens, tokens)]

    def send_block(ref, j):
        there_row, there_core = goes(j)
        return pltpu.make_async_remote_copy(
            block_of(ref, j), turned.at[row], sem_x.at[j, 0], sem_x.at[row, 1],
            device_id={"row": there_row, "core": there_core}, device_id_type=MESH,
        )

    def is_here(j):
        there_row, there_core = goes(j)
        return (there_row == row) & (there_core == core)

    barrier = pltpu.get_barrier_semaphore()
    count = 0
    for line in (Spread("row", rows), Spread("high", highs)):
        for right, there in ((True, line.here < line.size - 1), (False, line.here > 0)):

            @pl.when(there)
            def _(line=line, right=right):
                pl.semaphore_signal(barrier, 1, device_id=line.neighbour(right), device_id_type=MESH)

            count = count + there.astype(jnp.int32)
    others = [{"core": 1 - core}, {"section": 1 - section}] + sharing.members()
    for other in others:
        pl.semaphore_signal(barrier, 1, device_id=other, device_id_type=MESH)
    for r in range(rows):

        @pl.when(jnp.logical_not(mine_too & (row == r)))
        def _(r=r):
            pl.semaphore_signal(barrier, 1, device_id={"row": r, "core": source_core}, device_id_type=MESH)

    pl.semaphore_wait(barrier, count + len(others) + rows - mine_too.astype(jnp.int32))

    row_first = [True] * (4 + 2 * blocks)
    row_first[4 + blocks] = False
    order = [0, 1, 2, 3] + [UNIT + j * blocks + i for i in range(blocks) for j in range(2)]
    pieces = [(small, 0, small.shape[3], True)]
    pieces += [(w, i * narrow, narrow, row_first[n]) for n, i in enumerate(order)]
    gather = Gather(pieces, (sem_row, sem_high, sem_core, sem_one), highs, rows)

    def to_hbm(q):
        at = pl.ds(order[q - 1] * narrow, narrow)
        return pltpu.make_async_copy(w.at[:, :, :, at], w_hbm.at[:, :, :, at], sem_w.at[q])

    keys = share_keys(sharing, kv, sem_kv)

    def begin():
        for j in range(rows):
            for which, ref in ((0, tokens_hbm), (1, cot_hbm)):

                @pl.when((section == which) & is_here(j))
                def _(ref=ref, j=j):
                    pltpu.make_async_copy(block_of(ref, j), turned.at[row], sem_x.at[row, 1]).start()

                @pl.when((section == which) & jnp.logical_not(is_here(j)))
                def _(ref=ref, j=j):
                    send_block(ref, j).start()

    def use_small():
        for r in range(rows):
            vectors[:, r * narrow : (r + 1) * narrow] = small[r, 0, 0, 0:8, 0:narrow]
        for k in range(cols):
            for i in range(blocks):
                at = k * hidden + i * deep
                shift[:, at : at + deep] = small[0, k // CORES, k % CORES, 8 + i : 9 + i]
        lines = tokens // deep
        for slot in range(group):
            part = lax.rem(sharing.position + group - slot, group)
            base = 8 + blocks + (lax.div(sequence, CORES) * group + part) * lines
            doc = jnp.concatenate([small[row, high, source_core, pl.ds(base + i, 1)] for i in range(lines)], axis=1)
            if slot == 0:
                doc_q[...] = doc
            doc_k[slot * tokens : (slot + 1) * tokens] = jnp.broadcast_to(doc, (128, tokens)).T[:, :1]
        mask[...] = jnp.where(doc_k[...] == doc_q[...], 0.0, NEG_BIG)

    def turn():
        for r in range(rows):
            pltpu.make_async_copy(turned.at[r], turned.at[r], sem_x.at[r, 1]).wait()
        for r in range(rows):
            x[:, r * narrow : (r + 1) * narrow] = turned[r].T
        start_ref[...] = x[...]

    half = max(1, cols // 2)
    chunks = min(4, tokens // 8)
    chunk = tokens // chunks

    def send_out(i):
        at = pl.ds(i * chunk, chunk)
        return pltpu.make_async_remote_copy(
            y.at[at], next_hbm.at[at], sem_y.at[i, 0], sem_y.at[i, 1],
            device_id={"section": 1 - section}, device_id_type=MESH,
        )

    stay = pltpu.make_async_copy(x, next_hbm, sem_next.at[0])
    base = 3

    def between(tick, done):
        if tick == 5:
            begin()
        if done >= 1:
            to_hbm(done).start()
        if done == 0:
            use_small()
        if done == 1:
            turn()

            @pl.when(section == 0)
            def _():
                stay.start()

            front.project(0)
        if done == 2:
            front.project(1)
        if done == base:
            front.project(2)
            for copy in keys:
                copy.start()
        if done == base + 1:
            for copy in keys:
                copy.wait()
        if base + 1 <= done < base + 5:
            front.attend((done - base - 1) * (front.pairs // 4), front.pairs // 4)
        if done == base + 5:
            front.out()
            front.norm_one()
        if done >= base + 5:
            first = done == base + 5
            ready = (done - 4) // 2
            from_block = 0 if first else (done - 1 - 4) // 2
            for block in range(from_block, min(ready, blocks)):
                if block < blocks - 1:
                    for k in range(0, cols, half):
                        front.feed(block, range(k, k + half), block == 0 and k == 0)

    gather.run(between)
    for i in range(chunks):
        at = pl.ds(i * chunk, chunk)
        for k in range(0, cols, half):
            front.feed(blocks - 1, range(k, k + half), blocks == 1 and k == 0, at=at)
        y[at] = front.norm_two(at).astype(BF16)

        @pl.when(section == 0)
        def _(i=i):
            send_out(i).start()

    gather.finish()
    for j in range(rows):

        @pl.when(jnp.logical_not(is_here(j)))
        def _(j=j):
            send_block(tokens_hbm, j).wait_send()

    for q in range(1, len(pieces)):
        to_hbm(q).wait()

    @pl.when(section == 0)
    def _():
        stay.wait()
        for i in range(chunks):
            send_out(i).wait_send()

    @pl.when(section == 1)
    def _():
        for i in range(chunks):
            send_out(i).wait_recv()


def first_forward(tokens_in, cotangent, qkv, out, unit, down, unit_bias, width_bias, gain, docs, rows, highs, group):
    micro, narrow, _ = tokens_in.shape
    _, seq_here, seq_len = docs.shape
    deep, hidden = out.shape[2], unit.shape[2]
    width, cols, blocks = narrow * rows, highs * CORES, hidden // deep
    tokens = seq_len // group
    tall = (4 + 2 * blocks) * narrow
    apart = (rows, highs, CORES)
    in_any = pl.BlockSpec(memory_space=pl.ANY)
    in_vmem = pl.BlockSpec(memory_space=pltpu.VMEM)
    count = 1 + 4 + 2 * blocks
    small_rows = 8 + blocks + micro * seq_here * seq_len // deep
    small_rows += -small_rows % 8
    dma = pltpu.SemaphoreType.DMA
    flat, flat_f32 = pltpu.VMEM((tokens, width), BF16), pltpu.VMEM((tokens, width), F32)
    return pl.pallas_call(
        functools.partial(
            first_kernel, highs=highs, rows=rows, group=group, micro=micro, seq_here=seq_here, seq_len=seq_len
        ),
        in_specs=[in_any] * 2 + [in_vmem] * 8,
        out_specs=[in_any, in_vmem, in_any] + [in_vmem] * 4,
        out_shape=[
            shaped((tokens, width), BF16),
            shaped((tokens, width), BF16),
            shaped(apart + (tall, deep), BF16),
            shaped((8, width), F32),
            shaped((1, hidden * cols), F32),
            shaped((1, tokens), F32),
            shaped((group * tokens, 1), F32),
        ],
        scratch_shapes=[
            pltpu.VMEM(apart + (tall, deep), BF16),
            pltpu.VMEM(apart + (small_rows, deep), F32),
            pltpu.VMEM((rows, narrow, tokens), BF16),
            flat,
            flat,
            pltpu.VMEM((group, 2, tokens, width), BF16),
            flat,
            pltpu.VMEM((group * tokens, tokens), F32),
            flat_f32,
            flat,
            flat_f32,
            flat,
            dma((count, rows - 1, 2, 2)),
            dma((count, highs - 1, 2, 2)),
            dma((count, 2)),
            dma((count, rows, 2, 2)),
            dma((rows, 2)),
            dma((max(1, group - 1), 2)),
            dma((4, 2)),
            dma((count,)),
            dma((1,)),
        ],
        name="first_forward",
        compiler_params=pltpu.CompilerParams(collective_id=2, has_side_effects=True, vmem_limit_bytes=LOW_VMEM),
        cost_estimate=pl.CostEstimate(
            flops=24 * tokens * width * width, bytes_accessed=2 * tall * deep * rows * cols, transcendentals=0
        ),
    )(tokens_in, cotangent, qkv, out, unit, down, unit_bias, width_bias, gain, docs)


class Streams:
    def __init__(self, landing, sems, group):
        self.landing, self.sems, self.rows = landing, sems, landing.shape[0]
        self.row, self.core = lax.axis_index("row"), lax.axis_index("core")
        self.place, self.size = group.place, group.size
        sequence = lax.div(group.place, group.size)
        self.to = lax.rem(sequence, CORES)
        self.slot = lax.div(sequence, CORES) * group.size + group.position

    def here(self, r):
        return (self.to == self.core) & (self.row == r)

    def sources(self):
        found = []
        for r in range(self.rows):
            place = ((r // self.size) * CORES + self.core) * self.size + r % self.size
            found.append(({"row": lax.div(place, CORES), "core": lax.rem(place, CORES)}, place != self.place))
        return found

    def copy(self, ref, r):
        return pltpu.make_async_remote_copy(
            ref.at[r], self.landing.at[self.slot], self.sems.at[r, 0], self.sems.at[self.slot, 1],
            device_id={"row": r, "core": self.to}, device_id_type=MESH,
        )

    def start(self, ref):
        for r in range(self.rows):

            @pl.when(self.here(r))
            def _(r=r):
                pltpu.make_async_copy(ref.at[r], self.landing.at[self.slot], self.sems.at[self.slot, 1]).start()

            @pl.when(jnp.logical_not(self.here(r)))
            def _(r=r):
                self.copy(ref, r).start()

    def wait_sent(self, ref):
        for r in range(self.rows):

            @pl.when(jnp.logical_not(self.here(r)))
            def _(r=r):
                self.copy(ref, r).wait_send()

    def wait_here(self):
        for r in range(self.rows):
            pltpu.make_async_copy(self.landing.at[r], self.landing.at[r], self.sems.at[r, 1]).wait()


def share_key_grads(group, dkv, got, sems):
    def copy(step):
        return pltpu.make_async_remote_copy(
            dkv.at[step], got.at[step - 1], sems.at[step - 1, 0], sems.at[step - 1, 1],
            device_id=group.member(group.size - step), device_id_type=MESH,
        )

    return [copy(step) for step in range(1, group.size)]


def join_key_grads(dkv, got):
    group, _, tokens, _ = dkv.shape
    step = min(SLICE, tokens)

    @pl.loop(0, tokens, step=step)
    def _(at):
        some = pl.ds(pl.multiple_of(at, step), step)
        for j in range(2):
            total = dkv[0, j, some].astype(F32)
            for i in range(group - 1):
                total += got[i, j, some].astype(F32)
            dkv[0, j, some] = total.astype(BF16)


def heads_back(q, dmixed, mixed, log, kv, mask, first, count):
    group, _, tokens, _ = kv.shape

    @pl.loop(first, first + count)
    def _(p):
        at = pl.ds(pl.multiple_of(p * PAIR, PAIR), PAIR)
        keys = jnp.concatenate([kv[i, 0, :, at] for i in range(group)], axis=0)
        values = jnp.concatenate([kv[i, 1, :, at] for i in range(group)], axis=0)
        grad_query, grad_key, grad_value = pair_back(
            q[:, at], dmixed[:, at], mixed[:, at], [log[p, h : h + 1] for h in range(2)], keys, values, mask,
            min(256, tokens),
        )
        q[:, at] = grad_query
        for part in range(group):
            kv[part, 0, :, at] = grad_key[part * tokens : (part + 1) * tokens]
            kv[part, 1, :, at] = grad_value[part * tokens : (part + 1) * tokens]


def middle_kernel(*refs, group):
    (in_hbm, start_hbm, w_hbm, vectors, shift, doc_q, doc_k) = refs[:7]
    (next_hbm, q_hbm, kv_hbm, mixed_hbm, log_hbm, x1_hbm, hat1_hbm, scale1_hbm, hat2_hbm, scale2_hbm, act_hbm, slope_hbm,
     landing) = refs[7:20]
    (w, x, q, kv, mixed, log, mask, x1, x1_bf, acc, slope, act, hat1, hat2, scale1, scale2, y_t, got,
     sem_w, sem_in, sem_kv, sem_dkv, sem_keep, sem_act, sem_next, sem_out) = refs[20:]
    tokens, width = x.shape
    rows, highs, _, _, deep = w.shape
    narrow, cols = width // rows, highs * CORES
    section = lax.axis_index("section")
    sharing = Group(group)
    front = Front(w, vectors, shift, x, q, kv, mixed, mask, x1, x1_bf, acc, log)
    blocks = front.blocks
    hidden = blocks * deep
    streams = Streams(landing, sem_out, sharing)

    cuts = [(QKV, 3), (OUT, 1)] + [(UNIT + j * blocks + i, 1) for i in range(blocks) for j in range(2)]

    def load_w(i):
        first, count = cuts[i]
        at = pl.ds(first * narrow, count * narrow)
        return pltpu.make_async_copy(w_hbm.at[:, :, :, at], w.at[:, :, :, at], sem_w.at[i])

    get_x = pltpu.make_async_copy(in_hbm, x, sem_in.at[0])
    get_dy = pltpu.make_async_copy(start_hbm, x, sem_in.at[1])
    get_x.start()
    for i in range(len(cuts)):
        load_w(i).start()
    kept = {}

    def keep(i, ref, there):
        kept[i] = pltpu.make_async_copy(ref, there, sem_keep.at[i])
        kept[i].start()

    greet((), ("section",), sharing.members(), streams.sources())
    mask[...] = jnp.where(doc_k[...] == doc_q[...], 0.0, NEG_BIG)
    get_x.wait()
    load_w(0).wait()
    front.project(1)
    front.project(2)
    keys = share_keys(sharing, kv, sem_kv)
    for copy in keys:
        copy.start()
    front.project(0)
    keep(0, q, q_hbm)
    for copy in keys:
        copy.wait()
    keep(1, kv, kv_hbm)
    front.attend(0, front.pairs)
    keep(2, mixed, mixed_hbm)
    keep(3, log, log_hbm)
    load_w(1).wait()
    front.out()

    def keep_one(at, normed, scale):
        hat1[at] = normed.astype(BF16)
        scale1[at] = jnp.broadcast_to(scale, scale1[at].shape)

    front.norm_one(keep_one)
    get_dy.start()
    keep(4, x1_bf, x1_hbm)
    keep(5, hat1, hat1_hbm)
    keep(6, scale1, scale1_hbm)
    half = cols if tokens * cols * deep <= 1 << 19 else max(1, cols // 2)
    turns = [(block, range(k, k + half)) for block in range(blocks) for k in range(0, cols, half)]

    def keep_act(n):
        block, ks = turns[n]
        return [
            pltpu.make_async_copy(
                act.at[n % 2, :, pl.ds(i * deep, deep)],
                act_hbm.at[:, pl.ds(k * hidden + block * deep, deep)],
                sem_act.at[n % 2, i],
            )
            for i, k in enumerate(ks)
        ]

    for n, (block, ks) in enumerate(turns):
        if n % (cols // half) == 0:
            load_w(2 + 2 * block).wait()
            load_w(3 + 2 * block).wait()

        def keep_both(value, value_slope, n=n, block=block, ks=ks):
            if n >= 2:
                for copy in keep_act(n - 2):
                    copy.wait()
            act[n % 2] = value
            for copy in keep_act(n):
                copy.start()
            for i, k in enumerate(ks):
                begin = k * hidden + block * deep
                slope[:, begin : begin + deep] = value_slope[:, i * deep : (i + 1) * deep]

        front.feed(block, ks, n == 0, keep_both)
    keep(7, slope, slope_hbm)

    def keep_two(at, normed, scale):
        hat2[at] = normed.astype(BF16)
        scale2[at] = jnp.broadcast_to(scale, scale2[at].shape)

    step = min(SLICE, tokens)
    for begin in range(0, tokens, step):
        y = front.norm_two(pl.ds(begin, step), keep_two)
        y_t[:, :, begin : begin + step] = y.T.astype(BF16).reshape(rows, narrow, step)
    streams.start(y_t)
    keep(8, hat2, hat2_hbm)
    keep(9, scale2, scale2_hbm)

    for i in (4, 5):
        kept[i].wait()
    get_dy.wait()
    ddown, dattn, dmixed, dx = x1_bf, x, hat2, hat1

    def top(at):
        ddown[at] = norm_back(x[at].astype(F32), hat2[at].astype(F32), scale2[at][:, :1], vectors[7:8]).astype(BF16)

    by_tokens(tokens, top)
    for n, (block, ks) in enumerate(turns):
        up = jnp.concatenate([front.matrix(UNIT + block, k) for k in ks], axis=1)
        down = jnp.concatenate([front.matrix(UNIT + blocks + block, k) for k in ks], axis=1)
        begins = [k * hidden + block * deep for k in ks]
        slopes = jnp.concatenate([slope[:, b : b + deep] for b in begins], axis=1)
        dpre = (nn(ddown[...], down) * slopes.astype(F32)).astype(BF16)
        more = nt(dpre, up)
        if n == 0:
            acc[...] = more
        else:
            acc[...] += more
    kept[8].wait()

    def bottom(at):
        dx1 = ddown[at].astype(F32) + acc[at]
        dattn[at] = norm_back(dx1, hat1[at].astype(F32), scale1[at][:, :1], vectors[6:7]).astype(BF16)

    by_tokens(tokens, bottom)
    take = row_blocks(rows, narrow)
    for r in range(0, rows, take):
        some = pl.ds(OUT * narrow, narrow)
        weight = jnp.concatenate(
            [w[r : r + take, k // CORES, k % CORES, some].reshape(take * narrow, deep) for k in range(cols)], axis=1
        )
        dmixed[:, r * narrow : (r + take) * narrow] = nt(dattn[...], weight).astype(BF16)
    kept[0].wait()
    kept[1].wait()
    heads_back(q, dmixed, mixed, log, kv, mask, 0, front.pairs)
    grads = share_key_grads(sharing, kv, got, sem_dkv)
    for copy in grads:
        copy.start()
    for copy in grads:
        copy.wait()
    join_key_grads(kv, got)
    chunks = 2
    chunk = tokens // chunks

    def send_on(i):
        at = pl.ds(i * chunk, chunk)
        return pltpu.make_async_remote_copy(
            dx.at[at], next_hbm.at[at], sem_next.at[i, 0], sem_next.at[i, 1],
            device_id={"section": 1 - section}, device_id_type=MESH,
        )

    stay = pltpu.make_async_copy(start_hbm, next_hbm, sem_in.at[0])

    @pl.when(section == 1)
    def _():
        stay.start()

    for i in range(chunks):
        at = pl.ds(i * chunk, chunk)
        for k in range(cols):
            there = slice(k * deep, (k + 1) * deep)
            total = dattn[at, there].astype(F32)
            for j in range(3):
                total += nn(q[at] if j == 0 else kv[0, j - 1, at], front.matrix(QKV + j, k))
            dx[at, there] = total.astype(BF16)

        @pl.when(section == 1)
        def _(i=i):
            send_on(i).start()

    for n in range(len(turns) - 2, len(turns)):
        for copy in keep_act(n):
            copy.wait()
    for i in (2, 3, 6, 7, 9):
        kept[i].wait()
    streams.wait_sent(y_t)
    streams.wait_here()

    @pl.when(section == 1)
    def _():
        stay.wait()
        for i in range(chunks):
            send_on(i).wait_send()

    @pl.when(section == 0)
    def _():
        for i in range(chunks):
            send_on(i).wait_recv()


def middle(second_in, start, weight, vectors, shift, doc_query, doc_key, group):
    tokens, width = second_in.shape
    rows, highs, _, tall, deep = weight.shape
    cols, narrow, units = highs * CORES, width // rows, shift.shape[1]
    pairs, blocks = width // PAIR, units // cols // deep
    in_any = pl.BlockSpec(memory_space=pl.ANY)
    in_vmem = pl.BlockSpec(memory_space=pltpu.VMEM)
    dma = pltpu.SemaphoreType.DMA
    flat = shaped((tokens, width), BF16)
    thin = shaped((tokens, 128), F32)
    kv = shaped((group, 2, tokens, width), BF16)
    log = shaped((pairs, 2, tokens), F32)
    wide = shaped((tokens, units), BF16)
    turned = shaped((rows, narrow, tokens), BF16)
    half = cols if tokens * cols * deep <= 1 << 19 else max(1, cols // 2)

    def vmem(shape):
        return pltpu.VMEM(shape.shape, shape.dtype)

    whole = pltpu.VMEM((tokens, width), F32)
    return pl.pallas_call(
        functools.partial(middle_kernel, group=group),
        in_specs=[in_any] * 3 + [in_vmem] * 4,
        out_specs=[in_any] * 13,
        out_shape=[flat, flat, kv, flat, log, flat, flat, thin, flat, thin, wide, wide, turned],
        scratch_shapes=[
            vmem(weight), vmem(flat), vmem(flat), vmem(kv), vmem(flat), vmem(log),
            pltpu.VMEM((group * tokens, tokens), F32),
            whole, vmem(flat), whole, vmem(wide),
            pltpu.VMEM((2, tokens, half * deep), BF16),
            vmem(flat), vmem(flat), vmem(thin), vmem(thin), vmem(turned),
            pltpu.VMEM((max(1, group - 1), 2, tokens, width), BF16),
            dma((2 + 2 * blocks,)), dma((2,)), dma((max(1, group - 1), 2)), dma((max(1, group - 1), 2)), dma((10,)),
            dma((2, half)), dma((2, 2)), dma((rows, 2)),
        ],
        name="middle",
        compiler_params=pltpu.CompilerParams(collective_id=3, has_side_effects=True, vmem_limit_bytes=LOW_VMEM),
        cost_estimate=pl.CostEstimate(
            flops=72 * tokens * width * width, bytes_accessed=2 * tall * deep * rows * cols, transcendentals=0
        ),
    )(second_in, start, weight, vectors, shift, doc_query, doc_key)


STAGES = 3


def low_kernel(*refs, highs, rows, group):
    (dy_hbm, hat2_hbm, hat1_hbm, slope_hbm, act_hbm, x1_hbm, q_hbm, mixed_hbm, log_hbm, x_hbm, w_hbm, kv_hbm) = refs[:12]
    bias_doc_q, bias_doc_k, scale2, scale1, vectors = refs[12:17]
    down_out, out_out, unit_out, qkv_out, small_out, landed, landing, high_landing, dpre_hbm = refs[17:26]
    (dattn, x, q, mixed, log, w, kv, dmixed, bias, dkv_got, dx, stage, small, left, right,
     work, got, got_high, from_row, from_wide, sem_in, sem_right, sem_core, sem_load, sem_high, sem_row, sem_kv, sem_out,
     acc, top_sums, feed_sums, pre, sem_w, sem_slope, sem_dpre) = refs[26:]
    tokens, width = dattn.shape
    narrow, deep = stage.shape[-2:]
    dq, dkv = q, kv
    cols = highs * CORES

    sharing = Group(group)
    streams = Streams(landed, sem_out, sharing)

    units = act_hbm.shape[1]
    feed_pieces = units // cols // deep
    tail = small.shape[3]
    order = [("down", i) for i in range(feed_pieces)] + [("unit", i) for i in range(feed_pieces)]
    order += [("out", 0), ("qkv", 0), ("qkv", 1), ("small", 0), ("qkv", 2)]
    row_first = ()
    pieces = [
        (small, tail, True) if name == "small" else (stage.at[n % STAGES], narrow, (name, i) not in row_first)
        for n, (name, i) in enumerate(order)
    ]

    def give(q, ref):
        name, i = order[q]
        value = ref[...]
        if name in ("down", "unit"):
            (down_out if name == "down" else unit_out)[0, :, i * deep : (i + 1) * deep] = value
        elif name == "out":
            out_out[0] = value
        elif name == "qkv":
            qkv_out[0, i] = value
        else:
            small_out[...] = value

    scatter = Scatter(
        pieces, (landing, work, got, high_landing, got_high, from_row, from_wide, sem_core, sem_load, sem_high, sem_row), highs, rows, give,
    )

    def at_block(first, count):
        return pl.ds(first * narrow, count * narrow)

    hat2, hat1, dy, dpres, slopes = kv.at[0, 0], kv.at[0, 1], kv.at[1, 0], (q, mixed), (kv.at[1, 1], dmixed)
    first_inputs = [(dy_hbm, dy), (hat2_hbm, hat2), (x1_hbm, x), (hat1_hbm, hat1)]
    inputs = [
        (w_hbm.at[:, :, :, at_block(OUT, 1)], w.at[:, :, :, at_block(OUT, 1)]),
        (mixed_hbm, mixed),
        (q_hbm, q),
        (log_hbm, log),
        (kv_hbm, kv),
        (w_hbm.at[:, :, :, at_block(QKV, 3)], w.at[:, :, :, at_block(QKV, 3)]),
        (x_hbm, x),
    ]
    first_loads = [pltpu.make_async_copy(a, b, sem_in.at[i]) for i, (a, b) in enumerate(first_inputs)]
    loads = [pltpu.make_async_copy(a, b, sem_in.at[len(first_inputs) + i]) for i, (a, b) in enumerate(inputs)]
    early = 5

    def get_w(block):
        slot = block % 2
        return [
            pltpu.make_async_copy(
                w_hbm.at[:, :, :, at_block(UNIT + j * feed_pieces + block, 1)],
                w.at[:, :, :, at_block(2 * slot + j, 1)],
                sem_w.at[slot, j],
            )
            for j in range(2)
        ]

    def columns_of(ref, buffer, block, sems, out):
        copies = []
        for k in range(cols):
            far = ref.at[:, pl.ds((k * feed_pieces + block) * deep, deep)]
            near = buffer.at[:, pl.ds(k * deep, deep)]
            copies.append(pltpu.make_async_copy(*((near, far) if out else (far, near)), sems.at[k]))
        return copies

    def get_slope(block):
        return columns_of(slope_hbm, slopes[block % 2], block, sem_slope.at[block % 2], False)

    def put_dpre(block):
        return columns_of(dpre_hbm, dpres[block % 2], block, sem_dpre.at[block % 2], True)

    def top():
        top_sums[...] = jnp.zeros_like(top_sums)
        feed_sums[...] = jnp.zeros_like(feed_sums)

        def some(at):
            grad, hat = dy[at].astype(F32), hat2[at].astype(F32)
            ddown = norm_back(grad, hat, scale2[at][:, :1], vectors[7:8]).astype(BF16)
            dattn[at] = ddown
            top_sums[0:1] += column_sum(ddown.astype(F32))
            top_sums[1:2] += column_sum(grad)
            top_sums[2:3] += column_sum(grad * hat)

        by_tokens(tokens, some)

    def turn(block):
        for copy in get_w(block) + get_slope(block):
            copy.wait()
        if block >= 2:
            for copy in put_dpre(block - 2):
                copy.wait()

        for ks in (range(cols // 2), range(cols // 2, cols)):

            def matrix(j):
                some = at_block(2 * (block % 2) + j, 1)
                parts = [w[:, k // CORES, k % CORES, some].reshape(width, deep) for k in ks]
                return jnp.concatenate(parts, axis=1)

            at = slice(ks[0] * deep, (ks[-1] + 1) * deep)
            dpre = (nn(dattn[...], matrix(1)) * slopes[block % 2][:, at].astype(F32)).astype(BF16)
            dpres[block % 2][:, at] = dpre
            total = column_sum(dpre.astype(F32))
            for i, k in enumerate(ks):
                begin = (k * feed_pieces + block) * deep
                pre[:, begin : begin + deep] = total[:, i * deep : (i + 1) * deep]
            more = nt(dpre, matrix(0))
            if block == 0 and ks[0] == 0:
                acc[...] = more
            else:
                acc[...] += more
        for copy in put_dpre(block):
            copy.start()
        if block + 2 < feed_pieces:
            for copy in get_w(block + 2) + get_slope(block + 2):
                copy.start()

    def bottom():
        def some(at):
            dx1, hat = dattn[at].astype(F32) + acc[at], hat1[at].astype(F32)
            grad = norm_back(dx1, hat, scale1[at][:, :1], vectors[6:7]).astype(BF16)
            dattn[at] = grad
            feed_sums[0:1] += column_sum(grad.astype(F32))
            feed_sums[1:2] += column_sum(dx1)
            feed_sums[2:3] += column_sum(dx1 * hat)

        by_tokens(tokens, some)
        for block in range(max(0, feed_pieces - 2), feed_pieces):
            for copy in put_dpre(block):
                copy.wait()
        for load in loads[:-1]:
            load.start()

    key_grads = share_key_grads(sharing, kv, dkv_got, sem_kv)
    take = row_blocks(rows, narrow)

    def w_out(r):
        some = w[pl.ds(r * take, take), :, :, at_block(OUT, 1)]
        return some.reshape(take, cols, narrow, deep)

    def prepare():
        for load in loads[:early]:
            load.wait()
        doc_k = jnp.broadcast_to(bias_doc_k[...], (128, bias_doc_k.shape[1])).T[:, :1]
        bias[...] = jnp.where(doc_k == bias_doc_q[...], 0.0, NEG_BIG).astype(BF16)

        @pl.loop(0, rows // take)
        def _(r):
            at = pl.ds(pl.multiple_of(r * take * narrow, take * narrow), take * narrow)
            dmixed[:, at] = nt(dattn[...], side_by_side(w_out(r))).astype(BF16)

    def fill(slot, block, loaded=None):
        @pl.loop(0, cols)
        def _(k):
            grad = nn(left[...], block(k)).astype(BF16)
            stage[slot, :, lax.div(k, CORES), lax.rem(k, CORES)] = grad.reshape(rows, narrow, deep)

    def column(ref):
        return lambda k: ref[:, pl.ds(pl.multiple_of(k * deep, deep), deep)]

    def fetch(q):
        name, i = order[q]
        source = act_hbm if name == "down" else dpre_hbm
        return [
            pltpu.make_async_copy(
                source.at[:, pl.ds(k * feed_pieces * deep + i * deep, deep)],
                right.at[q % 2, :, pl.ds(k * deep, deep)],
                sem_right.at[q % 2, k],
            )
            for k in range(cols)
        ]

    def is_feed(q):
        return q < len(order) and order[q][0] in ("down", "unit")

    def make(q):
        name, i = order[q]
        slot = q % STAGES
        if q == 0:
            left[...] = dattn[...].T
        if name in ("down", "unit"):
            if (name, i) == ("unit", 0):
                left[...] = x[...].T
                loads[-1].start()
            for copy in fetch(q):
                copy.wait()
            if is_feed(q + 1):
                for copy in fetch(q + 1):
                    copy.start()
            fill(slot, column(right.at[q % 2]))
        elif name == "out":
            left[...] = mixed[...].T
            fill(slot, column(dattn))
        elif name == "qkv":
            if i == 0:
                loads[-1].wait()
            left[...] = grads_of(i).T
            fill(slot, column(x))
        else:
            small_sums()

    pairs = width // PAIR

    def heads(first, count):
        heads_back(q, dmixed, mixed, log, kv, bias, first, count)

    def exchange():
        for copy in key_grads:
            copy.start()

    def join():
        for copy in key_grads:
            copy.wait()
        for load in loads[early:-1]:
            load.wait()
        join_key_grads(kv, dkv_got)

    def grads_of(j):
        return dq[...] if j == 0 else dkv[0, j - 1]

    def input_gradient():
        for k in range(cols):
            at = slice(k * deep, (k + 1) * deep)
            total = dattn[:, at].astype(F32)
            for j in range(3):
                total += nn(grads_of(j), w[:, k // CORES, k % CORES, at_block(QKV + j, 1)].reshape(width, deep))
            for piece in range(0, deep, min(narrow, deep)):
                r, inside = divmod(k * deep + piece, narrow)
                dx[r, inside : inside + min(narrow, deep)] = total[:, piece : piece + min(narrow, deep)].T.astype(BF16)

    def small_sums():
        parts = [column_sum(grads_of(j).astype(F32)) for j in (0, 2)]
        parts += [feed_sums[0:2], top_sums[0:2], feed_sums[2:3], top_sums[2:3]]
        rows_of = jnp.concatenate(parts, axis=0).astype(BF16)
        small[...] = jnp.zeros_like(small)
        lines = pre.shape[1] // cols // deep
        for r in range(rows):
            for k in range(cols):
                small[r, k // CORES, k % CORES, 0:8, 0:narrow] = rows_of[:, r * narrow : (r + 1) * narrow]
                for i in range(lines):
                    at = (k * lines + i) * deep
                    small[r, k // CORES, k % CORES, 8 + i : 9 + i] = pre[:, at : at + deep].astype(BF16)

    share = max(1, pairs // 4)

    def between(tick):
        if tick < feed_pieces:
            turn(tick)
        if tick == feed_pieces:
            bottom()
        if tick == feed_pieces + 1:
            prepare()
        if feed_pieces + 1 <= tick < feed_pieces + 5:
            heads((tick - feed_pieces - 1) * share, share)
        if tick == feed_pieces + 4:
            exchange()
        if tick == feed_pieces + 5:
            join()
        if tick + 1 < len(order):
            make(tick + 1)
        if tick == feed_pieces + 5:
            input_gradient()
            streams.start(dx)

    for load in first_loads:
        load.start()
    for copy in fetch(0) + get_w(0) + get_slope(0) + (get_w(1) + get_slope(1) if feed_pieces > 1 else []):
        copy.start()
    greet((scatter.high, scatter.row), ("core",), sharing.members(), streams.sources())
    for load in first_loads:
        load.wait()
    top()
    make(0)
    scatter.run(between)
    streams.wait_sent(dx)
    streams.wait_here()


def low_back(dy, hat2, scale2, hat1, scale1, slope, act, x1_bf, query, mixed, log_total, x, weight, shared, doc_query, doc_key, vectors):
    tokens, width = dy.shape
    rows, highs, _, _, deep = weight.shape
    cols = highs * CORES
    narrow = width // rows
    units = act.shape[1]
    feed_rows = narrow * units // cols // deep
    group = shared.shape[0]
    keys = group * tokens
    apart = (rows, highs, CORES)
    tail = 16
    lines = 8 + units // cols // deep
    assert lines <= tail and narrow <= deep
    count = 2 * (feed_rows // narrow) + 5
    wide = 0
    steps = 4 + highs - 1 + rows - 1
    slots = min(count, steps)
    in_any = pl.BlockSpec(memory_space=pl.ANY)
    in_vmem = pl.BlockSpec(memory_space=pltpu.VMEM)
    ways = {2: 1}
    block = (rows, narrow, deep)
    dma = pltpu.SemaphoreType.DMA
    args = [dy, hat2, hat1, slope, act, x1_bf, query, mixed, log_total, x, weight, shared]
    *outs, _, _, _ = pl.pallas_call(
        functools.partial(low_kernel, highs=highs, rows=rows, group=group),
        in_specs=[in_any] * len(args) + [in_vmem] * 5,
        out_specs=[in_vmem] * 5 + [in_any] * 4,
        out_shape=[
            shaped((1, narrow, units // cols), BF16),
            shaped((1, narrow, deep), BF16),
            shaped((1, narrow, units // cols), BF16),
            shaped((1, 3, narrow, deep), BF16),
            shaped((tail, deep), BF16),
            shaped((rows, narrow, tokens), BF16),
            shaped((count, highs) + block, BF16),
            shaped((count, highs - 1, ways.get(highs, 2)) + block, BF16),
            shaped((tokens, units), BF16),
        ],
        scratch_shapes=[
            pltpu.VMEM((tokens, width), BF16),
            pltpu.VMEM((tokens, width), BF16),
            pltpu.VMEM((tokens, width), BF16),
            pltpu.VMEM((tokens, width), BF16),
            pltpu.VMEM(log_total.shape, F32),
            pltpu.VMEM(apart + (4 * narrow, deep), BF16),
            pltpu.VMEM((group, 2, tokens, width), BF16),
            pltpu.VMEM((tokens, width), BF16),
            pltpu.VMEM((keys, tokens), BF16),
            pltpu.VMEM((group - 1, 2, tokens, width), BF16),
            pltpu.VMEM((rows, narrow, tokens), BF16),
            pltpu.VMEM((STAGES,) + apart + (narrow, deep), BF16),
            pltpu.VMEM(apart + (tail, deep), BF16),
            pltpu.VMEM((width, tokens), BF16),
            pltpu.VMEM((2, tokens, cols * deep), BF16),
            pltpu.VMEM((slots, highs) + block, BF16),
            pltpu.VMEM((2, highs) + block, BF16),
            pltpu.VMEM((ways.get(highs, 2),) + block, BF16),
            pltpu.VMEM((count - wide, rows - 1, ways.get(rows, 2), narrow, deep), BF16),
            pltpu.VMEM((max(1, wide), rows - 1, ways.get(rows, 2), highs, narrow, deep), BF16),
            dma((11,)),
            dma((2, cols)),
            dma((count, highs, 2)),
            dma((count, highs, 2)),
            dma((count, highs - 1, 2, 3)),
            dma((count, rows - 1, 2, 2)),
            dma((max(1, group - 1), 2)),
            dma((rows, 2)),
            pltpu.VMEM((tokens, width), F32),
            pltpu.VMEM((8, width), F32),
            pltpu.VMEM((8, width), F32),
            pltpu.VMEM((1, units), F32),
            dma((2, 2)),
            dma((2, cols)),
            dma((2, cols)),
        ],
        name="low_back",
        compiler_params=pltpu.CompilerParams(collective_id=1, has_side_effects=True, vmem_limit_bytes=LOW_VMEM),
        cost_estimate=pl.CostEstimate(
            flops=64 * tokens * width * width, bytes_accessed=12 * width * units, transcendentals=0
        ),
    )(*args, doc_query, doc_key.reshape(1, keys), scale2, scale1, vectors)
    return outs


def finish_kernel(down, out, unit, qkv, small, first, second, *outs):
    layer_out, input_grad, qkv_out, out_out, unit_out, down_out, bias_out, width_out, gain_out = outs
    for ref, to in ((down, down_out), (out, out_out), (unit, unit_out), (qkv, qkv_out)):
        to[...] = ref[...].astype(F32)
    rows, narrow, tokens = first.shape
    for ref, to in ((first, layer_out), (second, input_grad)):
        per = rows // to.shape[1]
        for r in range(rows):
            to[0, r // per, :, r % per * tokens : (r % per + 1) * tokens] = ref[r].astype(F32)
    values = small[...].astype(F32)
    width_out[0] = values[0:6, :narrow]
    gain_out[0] = values[6:8, :narrow]
    deep = values.shape[1]
    for i in range(bias_out.shape[1] // deep):
        bias_out[:, i * deep : (i + 1) * deep] = values[8 + i : 9 + i]


def finish(down, out, unit, qkv, small, first, second, micro):
    rows, narrow, tokens = first.shape
    stream = shaped((1, micro, narrow, rows // micro * tokens), F32)
    grads = [shaped(grad.shape, F32) for grad in (qkv, out, unit, down)]
    rest = [shaped((1, down.shape[2]), F32), shaped((1, 6, narrow), F32), shaped((1, 2, narrow), F32)]
    return pl.pallas_call(
        finish_kernel,
        out_shape=[stream, stream, *grads, *rest],
        name="finish",
        compiler_params=pltpu.CompilerParams(vmem_limit_bytes=VMEM_BYTES),
    )(down, out, unit, qkv, small, first, second)


def local(tokens_in, doc_ids, cotangent, qkv_master, out_master, unit_master, down_master, unit_bias, width_bias, norm_gain):
    at = Layout(tokens_in, doc_ids)
    rows, cols = at.rows, at.cols

    second_in, start, weights, vectors, unit_shift, doc_query, doc_key = first_forward(
        tokens_in, cotangent, qkv_master, out_master, unit_master, down_master, unit_bias, width_bias, norm_gain, doc_ids,
        rows, cols // CORES, at.group,
    )
    (
        dy, query, shared, mixed, log_total, x1_bf, hat_one, scale_one, hat_two, scale_two, act, slope, stream,
    ) = middle(second_in, start, weights, vectors, unit_shift, doc_query, doc_key, at.group)
    *grads, input_grad = low_back(
        dy, hat_two, scale_two, hat_one, scale_one, slope, act, x1_bf, query, mixed, log_total, second_in, weights, shared,
        doc_query, doc_key, vectors,
    )
    return finish(*grads, stream, input_grad, at.micro)


def solution(mesh):
    sections, rows, cols = (mesh.shape[name] for name in ("section", "row", "col"))
    fine = Mesh(
        mesh.devices.reshape(sections, rows, cols // CORES, CORES), ("section", "row", "high", "core")
    )
    col = ("high", "core")
    block = P("section", "row", col)
    stream = P("section", None, "row", col)
    return jax.shard_map(
        local,
        mesh=fine,
        in_specs=(
            P(None, "row", col),
            P(None, col, None),
            P(None, "row", col),
            P("section", None, "row", col),
            block,
            block,
            block,
            P("section", col),
            P("section", None, "row"),
            P("section", None, "row"),
        ),
        out_specs=(
            stream,
            stream,
            stream,
            block,
            block,
            block,
            P("section", col),
            P("section", None, "row"),
            P("section", None, "row"),
        ),
        check_vma=False,
    )
```
